32 devices in a mesh: face: 4 (over z), tile: 8 (over y, x, core).
Axes of the slice: x: 2, y: 2, z: 4, core: 2. Of those that a mesh axis runs over, the one named last changes fastest.
Arguments:
- state: bfloat16 [4, 8, 2, 4, 512, 128], P('face', 'tile'), may hold values from -6 to 6
- obs_values: bfloat16 [32768, 256], P(('face', 'tile')), may hold values from -6 to 6
- obs_dest: int32 [32768, 1], P(('face', 'tile')), may hold values from 0 to 31; in each aligned block of 1024 rows (0 to 1023, 1024 to 2047, ...) at most 64 rows name the same one
- obs_pixel: int32 [32768], P(('face', 'tile')), may hold values from 0 to 4095
- matching: int32 [4, 2, 3], replicated, may hold values from 0 to 3, as said below
- kernel_one: bfloat16 [9, 128, 256], replicated, may hold values from -0.1875 to 0.1875
- bias_one: float32 [256], replicated, may hold values from -3 to 3
- kernel_two: bfloat16 [9, 256, 128], replicated, may hold values from -0.125 to 0.125
- bias_two: float32 [128], replicated, may hold values from -3 to 3
- cotangent: bfloat16 [4, 8, 2, 4, 512, 128], P('face', 'tile'), may hold values from -6 to 6
Outputs:
- analysis: bfloat16 [4, 8, 2, 4, 512, 128], P('face', 'tile')
- grad_state: float32 [4, 8, 2, 4, 512, 128], P('face', 'tile')
The draws below stay inside these ranges and needn't reach their ends.
Inputs may be any that keep to these rules, and one draw needn't show every extreme that they name: `obs_dest`: of the rows of one device, at most 64 name the same pixel tile, and in every draw some device names some tile exactly 64 times. The matching pairs sides: if side s of face block f is matched with side s2 of block g and flag r, then side s2 of g is matched with side s of f and the same flag. A block may be matched with itself on its other side.
All inputs are finite; a program needn't handle non-finite values.
Results may differ from the reference program's by a relative error of at most 0.0034.
Values may be sent and summed in bfloat16 or wider, within the bound.
No kernel may reach another device: no remote copies, remote signals or barrier semaphores. Data moves between devices by JAX's collectives and lax.ppermute only.
A program may use at most 192 MiB of HBM per device.

```python
import math
import jax
import jax.numpy as jnp
import numpy as np
from jax import lax

CHANNELS = 128
LIFTED = 256
BAND = 4
COLUMNS = 512
OBS_DEV = 1024
FACES = 4
TILES = 8
ROWS = 64
PIX = 4096
CAP = 64
OBS_TOTAL = 32768
DEVICES = 32


def draw_matching(key, part):
    perm_key, flag_key = jax.random.split(key)
    side_count = 2 * FACES
    side_order = jax.random.permutation(perm_key, side_count).astype(jnp.int32)
    pair_flags = jax.random.randint(flag_key, (FACES,), 0, 2, dtype=jnp.int32)
    first_sides = side_order[0::2]
    second_sides = side_order[1::2]
    partner_side = jnp.zeros((side_count,), jnp.int32).at[first_sides].set(second_sides).at[second_sides].set(first_sides)
    side_flag = jnp.zeros((side_count,), jnp.int32).at[first_sides].set(pair_flags).at[second_sides].set(pair_flags)
    table = jnp.stack([partner_side // 2, partner_side % 2, side_flag], axis=1)
    return table.reshape(FACES, 2, 3)


def plant(result, rng, smallest, top_value):
    place = [jax.random.randint(jax.random.fold_in(rng, axis), (), 0, length) for axis, length in enumerate(result.shape)]
    longest = result.shape.index(max(result.shape))
    next_to = place[:longest] + [(place[longest] + 1) % result.shape[longest]] + place[longest + 1:]
    return result.at[tuple(place)].set(smallest).at[tuple(next_to)].set(top_value)


def shard_levels(own_key, shape, cuts, smallest, largest):
    def one(dim, shards_of):
        draws = jax.random.uniform(jax.random.fold_in(jax.random.fold_in(own_key, 6), dim), (shards_of,), jnp.float32, smallest / len(cuts), largest / len(cuts))
        return jnp.repeat(jnp.exp(draws), shape[dim] // shards_of).reshape((-1,) + (1,) * (len(shape) - dim - 1))

    factor_of = one(*cuts[0])
    for cut in cuts[1:]:
        factor_of = factor_of * one(*cut)
    return factor_of


def shared_out(stream_key, own, number, rows, amount, top, most, lean):
    sequence = jax.random.permutation(stream_key, amount)
    packed, ordinary = portions_of(amount, rows * top, most, lean, True), portions_of(amount, rows * top, most, lean, False)
    places = jnp.arange(amount)

    def named(tallies, turn):
        used = int((tallies > 0).sum())
        fixed = max(1, used // 4)
        shifted = fixed + (places - fixed + turn * (used - fixed)) % max(1, amount - fixed)
        return jnp.zeros((amount,), jnp.int32).at[sequence[jnp.where(places < fixed, places, shifted)]].set(jnp.asarray(tallies, jnp.int32))

    tallies = jnp.where(number % 4 == 0, named(packed, number // 4), named(ordinary, number - number // 4 - 1))
    mixed = jax.random.permutation(jax.random.fold_in(own, 3), amount)
    giver, taker = mixed[0:amount // 2 * 2:2], mixed[1:amount // 2 * 2:2]
    slack = jnp.minimum(tallies[giver] - 1, most - tallies[taker]) // 2
    slack = jnp.where((giver == sequence[0]) | (taker == sequence[0]) | (tallies[taker] == 0), 0, jnp.maximum(slack, 0))
    shifted = jax.random.randint(jax.random.fold_in(own, 4), (amount // 2,), 0, 1 << 20) % (slack + 1)
    tallies = tallies.at[giver].add(-shifted).at[taker].add(shifted)
    labels = jnp.searchsorted(jnp.cumsum(tallies), jnp.arange(rows * top), side="right").astype(jnp.int32)
    listing = labels.reshape(top, rows).T
    listing = listing[jax.random.permutation(jax.random.fold_in(own, 1), rows)]
    turn = jax.random.randint(jax.random.fold_in(own, 2), (rows, 1), 0, top)
    return jnp.take_along_axis(listing, (jnp.arange(top)[None, :] + turn) % top, axis=1)


def portions_of(amount, total, reach, skew, full):
    weights = [(1 << 20) // math.isqrt(standing ** skew) + 1 for standing in range(1, amount + 1)]
    largest = reach if full else min(reach, max(-(-total // amount), total * weights[0] // sum(weights)))
    least = 1 if total - largest >= amount - 1 else 0
    given, rest = [largest] + [least] * (amount - 1), total - largest - least * (amount - 1)
    while rest > 0:
        free = [i for i in range(1, amount) if given[i] < largest] or [i for i in range(1, amount) if given[i] < reach]
        mass, remaining = sum([weights[i] for i in free]), rest
        for i in free:
            more = min(reach - given[i], max(1, remaining * weights[i] // mass), rest)
            given[i] = given[i] + more
            rest = rest - more
    return np.array(given)


def noise(key, dims, deviation, most, shards=(), kind=jnp.bfloat16):
    array = deviation * jax.random.normal(key, dims, jnp.float32)
    if shards:
        array = array * shard_levels(key, dims, shards, -0.22, 0.18)
    return jnp.clip(array, -most, most).astype(kind)


def setup_inputs(seed: int = 0) -> dict:
    arg_keys = jax.random.split(jax.random.key(seed), 11)
    state = noise(arg_keys[0], (FACES, TILES, 2, BAND, COLUMNS, CHANNELS), 1.0, 6.0, ((0, 4), (1, 8)))
    obs_values = noise(arg_keys[1], (OBS_TOTAL, LIFTED), 1.0, 6.0, ((0, 32),))
    obs_dest_keys = jax.random.split(jax.random.fold_in(arg_keys[2], 1), OBS_TOTAL // OBS_DEV)
    obs_dest_turns = jax.random.permutation(jax.random.fold_in(arg_keys[2], 3), OBS_TOTAL // OBS_DEV)
    obs_dest = jax.vmap(lambda own, number: shared_out(jax.random.fold_in(arg_keys[2], 2), own, number, OBS_DEV, DEVICES, 1, CAP, 2))(obs_dest_keys, obs_dest_turns).reshape((OBS_TOTAL, 1))
    obs_pixel = plant(jax.random.randint(arg_keys[3], (OBS_TOTAL,), 0, PIX), jax.random.fold_in(arg_keys[3], 1), 0, PIX - 1).astype(jnp.int32)
    matching = draw_matching(jax.random.fold_in(arg_keys[10], 71), 0)
    kernel_one = noise(arg_keys[5], (9, CHANNELS, LIFTED), (9 * CHANNELS) ** -0.5, 0.1875)
    bias_one = noise(arg_keys[6], (LIFTED,), 0.5, 3.0, (), jnp.float32)
    kernel_two = noise(arg_keys[7], (9, LIFTED, CHANNELS), (9 * LIFTED) ** -0.5, 0.125)
    bias_two = noise(arg_keys[8], (CHANNELS,), 0.5, 3.0, (), jnp.float32)
    cotangent = noise(arg_keys[9], (FACES, TILES, 2, BAND, COLUMNS, CHANNELS), 1.0, 6.0, ((0, 4), (1, 8)))
    return dict(state=state, obs_values=obs_values, obs_dest=obs_dest, obs_pixel=obs_pixel, matching=matching, kernel_one=kernel_one, bias_one=bias_one, kernel_two=kernel_two, bias_two=bias_two, cotangent=cotangent)


def activation(values):
    return jax.nn.gelu(values, approximate=True)

def unfold(blocks):
    lower = blocks[:, :, 0].reshape(FACES, TILES * BAND, COLUMNS, blocks.shape[-1])
    upper = blocks[:, :, 1].reshape(FACES, TILES * BAND, COLUMNS, blocks.shape[-1])[:, ::-1]
    return jnp.concatenate([lower, upper], axis=1)

def fold(grid):
    half = TILES * BAND
    lower = grid[:, :half].reshape(FACES, TILES, BAND, COLUMNS, grid.shape[-1])
    upper = grid[:, half:][:, ::-1].reshape(FACES, TILES, BAND, COLUMNS, grid.shape[-1])
    return jnp.stack([lower, upper], axis=2)

def pad_sides(grid, matching):
    row_padded = jnp.pad(grid, ((0, 0), (1, 1), (0, 0), (0, 0)))
    edges = jnp.stack([row_padded[:, :, 0], row_padded[:, :, -1]], axis=1)
    partner = matching[:, :, 0]
    their_side = matching[:, :, 1]
    flipped = matching[:, :, 2]
    picked = edges[partner, their_side]
    picked = jnp.where(flipped[:, :, None, None] == 1, picked[:, :, ::-1], picked)
    return jnp.concatenate([picked[:, 0][:, :, None], row_padded, picked[:, 1][:, :, None]], axis=2)

def convolve(padded, kernel):
    total = None
    for row_tap in range(3):
        for col_tap in range(3):
            window = padded[:, row_tap:row_tap + ROWS, col_tap:col_tap + COLUMNS]
            term = jnp.einsum('frwc,co->frwo', window, kernel[3 * row_tap + col_tap], precision=lax.Precision.HIGHEST)
            total = term if total is None else total + term
    return total

def reference(state, obs_values, obs_dest, obs_pixel, matching, kernel_one, bias_one, kernel_two, bias_two, cotangent):
    base_field = unfold(state).astype(jnp.float32)
    target = obs_dest[:, 0].astype(jnp.int32) * PIX + obs_pixel.astype(jnp.int32)
    gridded = jax.ops.segment_sum(obs_values.astype(jnp.float32), target, num_segments=DEVICES * PIX)
    gridded = unfold(gridded.reshape(FACES, TILES, 2, BAND, COLUMNS, LIFTED))
    first_kernel = kernel_one.astype(jnp.float32)
    second_kernel = kernel_two.astype(jnp.float32)

    def layer_one(values):
        return convolve(pad_sides(values, matching), first_kernel)

    def layer_two(values):
        return convolve(pad_sides(values, matching), second_kernel)
    first_out, first_pull = jax.vjp(layer_one, base_field)
    pre_act = first_out + bias_one + gridded
    inner = activation(pre_act).astype(jnp.bfloat16)
    second_out, second_pull = jax.vjp(layer_two, inner.astype(jnp.float32))
    analysis = (base_field + second_out + bias_two).astype(jnp.bfloat16)
    cot_field = unfold(cotangent).astype(jnp.float32)
    grad_inner = second_pull(cot_field)[0]
    grad_pre = jax.vjp(activation, pre_act)[1](grad_inner)[0].astype(jnp.bfloat16)
    grad_state = cot_field + first_pull(grad_pre.astype(jnp.float32))[0]
    return (fold(analysis), fold(grad_state))
```

```python
import functools
import math

import jax
import jax.numpy as jnp
from jax import lax
from jax.experimental import pallas as pl
from jax.experimental.pallas import tpu as pltpu
from jax.sharding import PartitionSpec as P

F32 = jnp.float32
BF16 = jnp.bfloat16
GROUP = 8
HIGH = 64
PIXEL_ROWS = 8
VMEM_LIMIT = 48 * 1024 * 1024
ROOT = math.sqrt(2.0 / math.pi)
CUBIC = 0.044715


def params():
    return pltpu.CompilerParams(vmem_limit_bytes=VMEM_LIMIT)


def cost(flops, nbytes):
    return pl.CostEstimate(flops=int(flops), bytes_accessed=int(nbytes), transcendentals=0)


def whole(shape):
    return pl.BlockSpec(shape, lambda *_: (0,) * len(shape))


def dot(a, b):
    return jnp.dot(a, b, preferred_element_type=F32)


def matched(matching_ref, side, faces):
    face = lax.axis_index("face")
    partner = matching_ref[face, side, 0]
    return lax.rem(partner - face + faces, faces), matching_ref[face, side, 1], matching_ref[face, side, 2]


def partner_rows(part_refs, array, hop, their_side, flipped):
    rows = None
    for k, ref in enumerate(part_refs):
        mine = jnp.where(their_side == 1, ref[array, 1], ref[array, 0])
        rows = mine if rows is None else jnp.where(hop == k, mine, rows)
    swapped = jnp.concatenate([rows[GROUP:], rows[:GROUP]], axis=0)
    return jnp.where(flipped == 1, swapped, rows)


def rolled_rows(rows, step):
    first, second = rows[:GROUP], rows[GROUP:]
    if step:
        first = pltpu.roll(first, (-step) % GROUP, 0)
        second = pltpu.roll(second, step % GROUP, 0)
    return jnp.concatenate([first, second], axis=0).astype(BF16)


def side_forward(rows, side, taps_ref):
    total = None
    for dy in (-1, 0, 1):
        term = dot(rolled_rows(rows, dy), taps_ref[3 * (dy + 1) + 2 * side])
        total = term if total is None else total + term
    return total


def side_adjoint(rows, their_side, flipped, taps_ref):
    total = None
    for dy in (-1, 0, 1):
        row_tap = jnp.where(flipped == 1, 1 - dy, 1 + dy)
        term = dot(rolled_rows(rows, -dy), taps_ref[3 * row_tap + 2 * their_side])
        total = term if total is None else total + term
    return total


def shift_columns(values, step):
    count = values.shape[0]
    at = lax.broadcasted_iota(jnp.int32, values.shape, 0)
    moved = pltpu.roll(values, (-step) % count, 0)
    edge = count - 1 if step == 1 else 0
    return jnp.where(at == edge, 0.0, moved)


def pack_body(capacity, dest_ref, pixel_ref, values_ref, out_ref):
    count = values_ref.shape[0]
    devices = out_ref.shape[0]
    block = 128
    dest_row = dest_ref[...].astype(F32)
    pixel_row = pixel_ref[...]
    eye = lax.broadcasted_iota(jnp.int32, (block, block), 0) == lax.broadcasted_iota(
        jnp.int32, (block, block), 1
    )

    def column(row, start):
        piece = row[:, start : start + block]
        return jnp.sum(jnp.where(eye, piece, 0.0), axis=1, keepdims=True)

    high_row = lax.shift_right_logical(pixel_row, 6).astype(F32) + 1.0
    low_row = (pixel_row & (HIGH - 1)).astype(F32)
    own = lax.broadcasted_iota(jnp.int32, (block, count), 0)
    other = lax.broadcasted_iota(jnp.int32, (block, count), 1)
    lane = lax.broadcasted_iota(jnp.int32, (block, 128), 1)
    lane_rank = (lane & (HIGH - 1)).astype(F32)
    rank_row = jnp.zeros((1, count), F32)
    coded = []
    for start in range(0, count, block):
        same = column(dest_row, start) == dest_row
        later = (own + start) < other
        earlier = (own + start) > other
        rank_row = rank_row + jnp.sum(
            jnp.where(same & later, 1.0, 0.0), axis=0, keepdims=True
        )
        rank = jnp.sum(jnp.where(same & earlier, 1.0, 0.0), axis=1, keepdims=True)
        code = jnp.where(lane < HIGH, column(high_row, start), column(low_row, start))
        coded.append(jnp.where(rank == lane_rank, code, 0.0).astype(BF16))
    to_device = (
        lax.broadcasted_iota(jnp.int32, (devices, count), 0).astype(F32) == dest_row
    )
    pixels = dot(
        jnp.where(to_device, 1.0, 0.0).astype(BF16), jnp.concatenate(coded, axis=0)
    )
    out_ref[:, 2 * capacity :, :] = jnp.broadcast_to(
        pixels[:, None, :], (devices, PIXEL_ROWS, 128)
    ).astype(BF16)
    slot_row = dest_row * capacity + rank_row
    slots = 256
    per_block = slots // capacity
    values = values_ref[...]
    slot_at = lax.broadcasted_iota(jnp.int32, (slots, count), 0).astype(F32)
    for start in range(0, devices * capacity, slots):
        onehot = jnp.where(slot_at == slot_row - start, 1.0, 0.0).astype(BF16)
        rows = dot(onehot, values).astype(BF16)
        first = start // capacity
        for half in range(2):
            out_ref[first : first + per_block, half * capacity : (half + 1) * capacity, :] = (
                rows[:, half * 128 : (half + 1) * 128].reshape(per_block, capacity, 128)
            )


def edge_body(rows, x_lo, x_hi, c_lo, c_hi, p_lo, p_hi, n_lo, n_hi, out_ref):
    tiles = lax.axis_size("tile")
    last = lax.axis_index("tile") == tiles - 1
    out_ref[...] = jnp.zeros_like(out_ref)
    for side in range(2):
        at = 0 if side == 0 else -1
        prev = (p_lo, p_hi)[side][...].astype(F32)
        after = (n_lo, n_hi)[side][...].astype(F32)
        at = 0 if side == 0 else prev.shape[1] - 1
        for array in range(2):
            own = ((x_lo, x_hi), (c_lo, c_hi))[array][side][...].astype(F32)
            for band in range(2):
                base = band * GROUP
                out_ref[array, side, base, :] = prev[2 * array + band, at]
                for r in range(rows):
                    out_ref[array, side, base + 1 + r, :] = own[band * rows + r, at]
                fold = own[(1 - band) * rows + rows - 1, at]
                out_ref[array, side, base + 1 + rows, :] = jnp.where(
                    last, fold, after[2 * array + band, at]
                )


def lift_body(
    rows, faces, matching_ref, x_ref, c_ref, prev_ref, next_ref, k1_ref, b1_ref, k2t_ref, *rest
):
    parts = rest[:faces]
    pre_ref, grad_ref, x_cat, c_cat, x_side, c_side = rest[faces:]
    step = pl.program_id(0)
    ext = rows + 2
    channels = x_ref.shape[2]
    last = lax.axis_index("tile") == lax.axis_size("tile") - 1

    @pl.when(step == 0)
    def _():
        for array, (own, cat) in enumerate(((x_ref, x_cat), (c_ref, c_cat))):
            order = (-1, 0, 1) if array == 0 else (1, 0, -1)
            for band in range(2):
                for e in range(ext):
                    if e == 0:
                        row = prev_ref[2 * array + band].astype(F32)
                    elif e <= rows:
                        row = own[band * rows + e - 1].astype(F32)
                    else:
                        fold = own[(1 - band) * rows + rows - 1].astype(F32)
                        row = jnp.where(last, fold, next_ref[2 * array + band].astype(F32))
                    for place, shift in enumerate(order):
                        moved = row if shift == 0 else shift_columns(row, shift)
                        cat[band * ext + e, :, place * channels : (place + 1) * channels] = (
                            moved.astype(BF16)
                        )
        for side in range(2):
            hop, their_side, flipped = matched(matching_ref, side, faces)
            x_side[side] = side_forward(
                partner_rows(parts, 0, hop, their_side, flipped), side, k1_ref
            )
            c_side[side] = side_adjoint(
                partner_rows(parts, 1, hop, their_side, flipped), their_side, flipped, k2t_ref
            )

    band = step // rows
    r = lax.rem(step, rows)
    centre = band * ext + r + 1
    sign = 1 - 2 * band
    taps = k1_ref.shape[0] * channels
    for cat, side_ref, weights, out_ref, way in (
        (x_cat, x_side, k1_ref, pre_ref, sign),
        (c_cat, c_side, k2t_ref, grad_ref, -sign),
    ):
        lhs = jnp.concatenate([cat[centre - way], cat[centre], cat[centre + way]], axis=1)
        total = dot(lhs, weights[...].reshape(taps, weights.shape[2]))
        if out_ref is pre_ref:
            total = total + b1_ref[...]
        out_ref[0] = total
        width = out_ref.shape[1]
        at = band * GROUP + r + 1
        out_ref[0, 0:1, :] += side_ref[0, pl.ds(at, 1), :]
        out_ref[0, width - 1 : width, :] += side_ref[1, pl.ds(at, 1), :]


def row_taps(taps_ref, row):
    return jnp.concatenate([taps_ref[3 * row + dx] for dx in range(3)], axis=1)


def merge_shifts(wide, forward):
    channels = wide.shape[1] // 3
    left, mid, right = (wide[:, k * channels : (k + 1) * channels] for k in range(3))
    step = -1 if forward else 1
    return mid + shift_columns(left, step) + shift_columns(right, -step)


def gelu_body(
    rows, capacity, recv_ref, pre_ref, grad_ref, k2_ref, k1t_ref, inner_ref, gp_ref, up_ref, down_ref,
    edge_ref, values, keys,
):
    step = pl.program_id(0)
    devices = recv_ref.shape[0]
    width = pre_ref.shape[1]
    slots = devices * capacity
    per_lane = 128 // capacity

    @pl.when(step == 0)
    def _():
        edge_ref[...] = jnp.zeros_like(edge_ref)
        for half in range(2):
            values[:, half * 128 : (half + 1) * 128] = recv_ref[
                :, half * capacity : (half + 1) * capacity, :
            ].reshape(slots, 128)
        owner = lax.broadcasted_iota(jnp.int32, (GROUP, 128), 1) // capacity
        for start in range(0, devices, per_lane):
            key = jnp.zeros((GROUP, 128), F32)
            for k in range(per_lane):
                code = recv_ref[start + k, 2 * capacity :, :].astype(F32)
                mine = (code - 1.0) * HIGH + pltpu.roll(code, HIGH, 1)
                if k:
                    mine = pltpu.roll(mine, k * capacity, 1)
                key = jnp.where(owner == k, mine, key)
            keys[:, start * capacity : start * capacity + 128] = key

    band = step // rows
    r = lax.rem(step, rows)
    local = keys[0:1, :] - (step * width).astype(F32)
    column = lax.broadcasted_iota(jnp.int32, (width, slots), 0).astype(F32)
    onehot = jnp.where(column == local, 1.0, 0.0).astype(BF16)
    v = pre_ref[0] + dot(onehot, values[...])
    square = v * v
    t = jnp.tanh(v * (ROOT + (ROOT * CUBIC) * square))
    half = 0.5 + 0.5 * t
    inner = (v * half).astype(BF16)
    slope = half + (0.5 * v) * (1.0 - t * t) * (ROOT + (3.0 * ROOT * CUBIC) * square)
    gp = (grad_ref[0] * slope).astype(BF16)
    inner_ref[0] = inner
    gp_ref[0] = gp
    at = band * GROUP + r + 1
    for array, (ref, _) in enumerate(((inner_ref, inner), (gp_ref, gp))):
        edge_ref[array, 0, pl.ds(at, 1), :] = ref[0, 0:16, :].astype(F32)[0:1]
        edge_ref[array, 1, pl.ds(at, 1), :] = ref[0, width - 16 :, :].astype(F32)[15:16]

    for edge_row, out_ref in ((0, down_ref), (rows - 1, up_ref)):

        @pl.when(r == edge_row)
        def _():
            sign = 1 - 2 * band
            outward = -1 if edge_row == 0 else 1
            tap = 1 - outward * sign
            up = merge_shifts(dot(inner_ref[0], row_taps(k2_ref, tap)), True)
            out_ref[band] = up.astype(BF16)
            tap = 1 + outward * sign
            back = merge_shifts(dot(gp_ref[0], row_taps(k1t_ref, tap)), False)
            out_ref[2 + band] = back.astype(BF16)


def inside_body(rows, inner_ref, gp_ref, k2_ref, k1t_ref, ana_ref, grad_ref, w2, w1):
    step = pl.program_id(0)
    band = step // rows
    r = lax.rem(step, rows)
    sign = 1 - 2 * band
    lifted, channels = k2_ref.shape[1], k2_ref.shape[2]

    @pl.when(step == 0)
    def _():
        for taps, w in ((k2_ref, w2), (k1t_ref, w1)):
            for dy in range(3):
                for dx in range(3):
                    w[dy * lifted : (dy + 1) * lifted, dx * channels : (dx + 1) * channels] = taps[
                        3 * dy + dx
                    ]

    for source, w, out_ref, forward in ((inner_ref, w2, ana_ref, True), (gp_ref, w1, grad_ref, False)):
        way = sign if forward else -sign
        pieces = []
        for dy in (-1, 0, 1):
            at = r + way * dy
            if dy == 0:
                pieces.append(source[step])
            else:
                inside = (at >= 0) & (at < rows)
                piece = source[band * rows + jnp.clip(at, 0, rows - 1)]
                pieces.append(jnp.where(inside, piece, jnp.zeros_like(piece)))
        out_ref[0] = merge_shifts(dot(jnp.concatenate(pieces, axis=1), w[...]), forward)


def side_body(faces, matching_ref, k2_ref, k1t_ref, *rest):
    parts = rest[:faces]
    out_ref = rest[faces]
    for side in range(2):
        hop, their_side, flipped = matched(matching_ref, side, faces)
        out_ref[0, side] = side_forward(
            partner_rows(parts, 0, hop, their_side, flipped), side, k2_ref
        )
        out_ref[1, side] = side_adjoint(
            partner_rows(parts, 1, hop, their_side, flipped), their_side, flipped, k1t_ref
        )


def final_body(
    rows, x_ref, c_ref, ana_ref, grad_ref, b2_ref, up_ref, prev_ref, next_ref, own_ref, below_ref,
    above_ref, out_ana, out_grad, held,
):
    step = pl.program_id(0)
    band = step // rows
    r = lax.rem(step, rows)
    last = lax.axis_index("tile") == lax.axis_size("tile") - 1
    width = x_ref.shape[1]
    for array, (own, acc, out) in enumerate(
        ((x_ref, ana_ref, out_ana), (c_ref, grad_ref, out_grad))
    ):
        total = own[0].astype(F32) + acc[0]
        if array == 0:
            total = total + b2_ref[...]
        held[...] = total

        @pl.when(r == 0)
        def _():
            held[...] += prev_ref[2 * array + band].astype(F32)

        @pl.when(r == rows - 1)
        def _():
            fold = up_ref[2 * array + 1 - band].astype(F32)
            held[...] += jnp.where(last, fold, next_ref[2 * array + band].astype(F32))

        for side in range(2):
            column = 0 if side == 0 else width - 1
            base = band * GROUP
            extra = own_ref[array, side, pl.ds(base + r + 1, 1), :]
            before = below_ref[array, side, pl.ds(base + rows + 1, 1), :]
            fold = own_ref[array, side, pl.ds((1 - band) * GROUP + rows + 1, 1), :]
            after = jnp.where(last, fold, above_ref[array, side, pl.ds(base, 1), :])
            extra = extra + jnp.where(r == 0, before, 0.0) + jnp.where(r == rows - 1, after, 0.0)
            held[column : column + 1, :] += extra
        out[0] = held[...].astype(out.dtype)


def per_device(
    state,
    obs_values,
    obs_dest,
    obs_pixel,
    matching,
    kernel_one,
    bias_one,
    kernel_two,
    bias_two,
    cotangent,
):
    rows, width, channels = state.shape[3], state.shape[4], state.shape[5]
    lifted = kernel_one.shape[2]
    tiles, faces = lax.axis_size("tile"), lax.axis_size("face")
    devices = tiles * faces
    count = obs_values.shape[0]
    capacity = 2 * count // devices
    all_rows = 2 * rows
    chunk = 2 * capacity + PIXEL_ROWS
    x = state.reshape(all_rows, width, channels)
    c = cotangent.reshape(all_rows, width, channels)
    forward = [(i, i + 1) for i in range(tiles - 1)]
    backward = [(i + 1, i) for i in range(tiles - 1)]
    up_rows = jnp.concatenate([x[rows - 1 :: rows], c[rows - 1 :: rows]], axis=0)
    down_rows = jnp.concatenate([x[0::rows], c[0::rows]], axis=0)
    prev_rows = lax.ppermute(up_rows, "tile", forward)
    next_rows = lax.ppermute(down_rows, "tile", backward)

    packed = pl.pallas_call(
        functools.partial(pack_body, capacity),
        out_shape=jax.ShapeDtypeStruct((devices, chunk, 128), BF16),
        compiler_params=params(),
        cost_estimate=cost(2 * devices * capacity * count * lifted, 2 << 20),
        name="pack",
    )(obs_dest.reshape(1, count), obs_pixel.reshape(1, count), obs_values)
    received = lax.all_to_all(packed, ("face", "tile"), 0, 0, tiled=True)

    def exchange(own):
        parts = [own]
        for k in range(1, faces):
            parts.append(
                lax.ppermute(own, "face", [((i + k) % faces, i) for i in range(faces)])
            )
        return parts

    strip = 16
    low = lambda n: pl.BlockSpec((n, strip, channels), lambda *_: (0, 0, 0))
    high = lambda n: pl.BlockSpec((n, strip, channels), lambda *_: (0, width // strip - 1, 0))
    edges = pl.pallas_call(
        functools.partial(edge_body, rows),
        grid=(1,),
        in_specs=[low(all_rows), high(all_rows)] * 2 + [low(4), high(4)] * 2,
        out_specs=whole((2, 2, 2 * GROUP, channels)),
        out_shape=jax.ShapeDtypeStruct((2, 2, 2 * GROUP, channels), F32),
        compiler_params=params(),
        cost_estimate=cost(0, 1 << 18),
        name="edges",
    )(x, x, c, c, prev_rows, prev_rows, next_rows, next_rows)
    parts = exchange(edges)

    k1t = jnp.transpose(kernel_one, (0, 2, 1))
    k2t = jnp.transpose(kernel_two, (0, 2, 1))
    b1 = bias_one.reshape(1, lifted)
    b2 = bias_two.reshape(1, channels)
    smem = pl.BlockSpec(memory_space=pltpu.SMEM)
    row_block = lambda n: pl.BlockSpec((1, width, n), lambda i: (i, 0, 0))
    part_shape = (2, 2, 2 * GROUP, channels)
    conv_flops = 2 * 9 * all_rows * width * channels * lifted
    pre, grad_inner = pl.pallas_call(
        functools.partial(lift_body, rows, faces),
        grid=(all_rows,),
        in_specs=[
            smem,
            whole(x.shape),
            whole(c.shape),
            whole(prev_rows.shape),
            whole(next_rows.shape),
            whole(kernel_one.shape),
            whole(b1.shape),
            whole(k2t.shape),
        ]
        + [whole(part_shape)] * faces,
        out_specs=[row_block(lifted)] * 2,
        out_shape=[jax.ShapeDtypeStruct((all_rows, width, lifted), F32)] * 2,
        scratch_shapes=[
            pltpu.VMEM((2 * (rows + 2), width, 3 * channels), BF16),
            pltpu.VMEM((2 * (rows + 2), width, 3 * channels), BF16),
            pltpu.VMEM((2, 2 * GROUP, lifted), F32),
            pltpu.VMEM((2, 2 * GROUP, lifted), F32),
        ],
        compiler_params=params(),
        cost_estimate=cost(2 * conv_flops, 12 << 20),
        name="lift",
    )(matching, x, c, prev_rows, next_rows, kernel_one, b1, k2t, *parts)

    grown = (2, 2, 2 * GROUP, lifted)
    inner, grad_pre, up, down, edges_two = pl.pallas_call(
        functools.partial(gelu_body, rows, capacity),
        grid=(all_rows,),
        in_specs=[
            whole(received.shape),
            row_block(lifted),
            row_block(lifted),
            whole(kernel_two.shape),
            whole(k1t.shape),
        ],
        out_specs=[
            row_block(lifted),
            row_block(lifted),
            whole((4, width, channels)),
            whole((4, width, channels)),
            whole(grown),
        ],
        out_shape=[
            jax.ShapeDtypeStruct((all_rows, width, lifted), BF16),
            jax.ShapeDtypeStruct((all_rows, width, lifted), BF16),
            jax.ShapeDtypeStruct((4, width, channels), BF16),
            jax.ShapeDtypeStruct((4, width, channels), BF16),
            jax.ShapeDtypeStruct(grown, F32),
        ],
        scratch_shapes=[
            pltpu.VMEM((devices * capacity, 2 * 128), BF16),
            pltpu.VMEM((GROUP, devices * capacity), F32),
        ],
        compiler_params=params(),
        cost_estimate=cost(2 * all_rows * width * devices * capacity * lifted, 14 << 20),
        name="activate",
    )(received, pre, grad_inner, kernel_two, k1t)
    from_prev = lax.ppermute(up, "tile", forward)
    from_next = lax.ppermute(down, "tile", backward)
    parts_two = exchange(edges_two)

    ana, grad = pl.pallas_call(
        functools.partial(inside_body, rows),
        grid=(all_rows,),
        in_specs=[
            whole(inner.shape),
            whole(inner.shape),
            whole(kernel_two.shape),
            whole(k1t.shape),
        ],
        out_specs=[row_block(channels)] * 2,
        out_shape=[jax.ShapeDtypeStruct((all_rows, width, channels), F32)] * 2,
        scratch_shapes=[
            pltpu.VMEM((3 * lifted, 3 * channels), BF16),
            pltpu.VMEM((3 * lifted, 3 * channels), BF16),
        ],
        compiler_params=params(),
        cost_estimate=cost(2 * conv_flops, 10 << 20),
        name="inside",
    )(inner, grad_pre, kernel_two, k1t)

    side_shape = (2, 2, 2 * GROUP, channels)
    sides = pl.pallas_call(
        functools.partial(side_body, faces),
        in_specs=[smem] + [pl.BlockSpec(memory_space=pltpu.VMEM)] * (2 + faces),
        out_shape=jax.ShapeDtypeStruct(side_shape, F32),
        compiler_params=params(),
        cost_estimate=cost(0, 2 << 20),
        name="sides",
    )(matching, kernel_two, k1t, *parts_two)
    below = lax.ppermute(sides, "tile", forward)
    above = lax.ppermute(sides, "tile", backward)

    analysis, grad_state = pl.pallas_call(
        functools.partial(final_body, rows),
        grid=(all_rows,),
        in_specs=[
            row_block(channels),
            row_block(channels),
            row_block(channels),
            row_block(channels),
            whole(b2.shape),
            whole(up.shape),
            whole(up.shape),
            whole(up.shape),
            whole(side_shape),
            whole(side_shape),
            whole(side_shape),
        ],
        out_specs=[row_block(channels)] * 2,
        out_shape=[
            jax.ShapeDtypeStruct((all_rows, width, channels), BF16),
            jax.ShapeDtypeStruct((all_rows, width, channels), F32),
        ],
        scratch_shapes=[pltpu.VMEM((width, channels), F32)],
        compiler_params=params(),
        cost_estimate=cost(0, 12 << 20),
        name="final",
    )(x, c, ana, grad, b2, up, from_prev, from_next, sides, below, above)
    return analysis.reshape(state.shape), grad_state.reshape(cotangent.shape)


def solution(mesh):
    return jax.shard_map(
        per_device,
        mesh=mesh,
        in_specs=(
            P("face", "tile", None, None, None, None),
            P(("face", "tile"), None),
            P(("face", "tile"), None),
            P(("face", "tile")),
            P(),
            P(),
            P(),
            P(),
            P(),
            P("face", "tile", None, None, None, None),
        ),
        out_specs=(
            P("face", "tile", None, None, None, None),
            P("face", "tile", None, None, None, None),
        ),
        check_vma=False,
    )
```

```python
import functools
import math

import jax
import jax.numpy as jnp
from jax import lax
from jax.experimental import pallas as pl
from jax.experimental.pallas import tpu as pltpu
from jax.sharding import PartitionSpec as P

F32 = jnp.float32
BF16 = jnp.bfloat16
GROUP = 8
HIGH = 64
PIXEL_ROWS = 8
ROOT = math.sqrt(2.0 / math.pi)
CUBIC = 0.044715


def params(mib=24):
    return pltpu.CompilerParams(vmem_limit_bytes=mib << 20)


def cost(flops, nbytes):
    return pl.CostEstimate(flops=int(flops), bytes_accessed=int(nbytes), transcendentals=0)


def hold(shape, kind):
    return pltpu.VMEM(shape, kind)


def held(array):
    return pltpu.with_memory_space_constraint(array, pltpu.VMEM)


def far(array):
    return pltpu.with_memory_space_constraint(array, pltpu.HBM)


def fixed(shape):
    return pl.BlockSpec(shape, lambda *_: (0,) * len(shape))


def dot(a, b):
    return jnp.dot(a, b, preferred_element_type=F32)


def matched(matching_ref, side, faces):
    face = lax.axis_index("face")
    partner = matching_ref[face, side, 0]
    return lax.rem(partner - face + faces, faces), matching_ref[face, side, 1], matching_ref[face, side, 2]


def partner_rows(part_refs, array, hop, their_side, flipped):
    rows = None
    for k, ref in enumerate(part_refs):
        mine = jnp.where(their_side == 1, ref[array, 1], ref[array, 0])
        rows = mine if rows is None else jnp.where(hop == k, mine, rows)
    swapped = jnp.concatenate([rows[GROUP:], rows[:GROUP]], axis=0)
    return jnp.where(flipped == 1, swapped, rows)


def rolled_rows(rows, step):
    first, second = rows[:GROUP], rows[GROUP:]
    if step:
        first = pltpu.roll(first, (-step) % GROUP, 0)
        second = pltpu.roll(second, step % GROUP, 0)
    return jnp.concatenate([first, second], axis=0).astype(BF16)


def side_forward(rows, side, taps_ref):
    lhs = jnp.concatenate([rolled_rows(rows, dy) for dy in (-1, 0, 1)], axis=1)
    taps = jnp.concatenate([taps_ref[3 * row + 2 * side] for row in range(3)], axis=0)
    return dot(lhs, taps)


def side_adjoint(rows, their_side, flipped, taps_ref):
    lhs = jnp.concatenate([rolled_rows(rows, -dy) for dy in (-1, 0, 1)], axis=1)
    order = [jnp.where(flipped == 1, 2 - row, row) for row in range(3)]
    taps = jnp.concatenate([taps_ref[3 * row + 2 * their_side] for row in order], axis=0)
    return dot(lhs, taps)


def shift_columns(values, step):
    count = values.shape[0]
    at = lax.broadcasted_iota(jnp.int32, values.shape, 0)
    moved = pltpu.roll(values, (-step) % count, 0)
    edge = count - 1 if step == 1 else 0
    return jnp.where(at == edge, 0.0, moved)


def spread_columns(row, order):
    wide = row.astype(F32)
    return jnp.concatenate(
        [row if s == 0 else shift_columns(wide, s).astype(BF16) for s in order], axis=1
    )


def add_edges(values, left, right):
    count = values.shape[0]
    at = lax.broadcasted_iota(jnp.int32, (GROUP, values.shape[1]), 0)
    first = values[:GROUP] + jnp.where(at == 0, left, 0.0)
    tail = values[count - GROUP :] + jnp.where(at == GROUP - 1, right, 0.0)
    return jnp.concatenate([first, values[GROUP : count - GROUP], tail], axis=0)


def pack_body(
    capacity, dest_in, pixel_in, values_in, out_hbm, dest_ref, pixel_ref, values_ref, out_ref, in_sem,
    out_sem,
):
    count = values_ref.shape[0]
    devices = out_ref.shape[0]
    block = 128
    loads = [
        pltpu.make_async_copy(source, target, in_sem.at[k])
        for k, (source, target) in enumerate(
            ((dest_in, dest_ref), (pixel_in, pixel_ref), (values_in, values_ref))
        )
    ]
    for load in loads:
        load.start()
    loads[0].wait()
    loads[1].wait()
    dest_row = dest_ref[...].astype(F32)
    pixel_row = pixel_ref[...]
    eye = lax.broadcasted_iota(jnp.int32, (block, block), 0) == lax.broadcasted_iota(
        jnp.int32, (block, block), 1
    )

    def column(row, start):
        piece = row[:, start : start + block]
        return jnp.sum(jnp.where(eye, piece, 0.0), axis=1, keepdims=True)

    high_row = lax.shift_right_logical(pixel_row, 6).astype(F32) + 1.0
    low_row = (pixel_row & (HIGH - 1)).astype(F32)
    own = lax.broadcasted_iota(jnp.int32, (block, count), 0)
    other = lax.broadcasted_iota(jnp.int32, (block, count), 1)
    lane = lax.broadcasted_iota(jnp.int32, (block, 128), 1)
    lane_rank = (lane & (HIGH - 1)).astype(F32)
    rank_row = jnp.zeros((1, count), F32)
    coded = []
    for start in range(0, count, block):
        same = column(dest_row, start) == dest_row
        later = (own + start) < other
        earlier = (own + start) > other
        rank_row = rank_row + jnp.sum(
            jnp.where(same & later, 1.0, 0.0), axis=0, keepdims=True
        )
        rank = jnp.sum(jnp.where(same & earlier, 1.0, 0.0), axis=1, keepdims=True)
        code = jnp.where(lane < HIGH, column(high_row, start), column(low_row, start))
        coded.append(jnp.where(rank == lane_rank, code, 0.0).astype(BF16))
    to_device = (
        lax.broadcasted_iota(jnp.int32, (devices, count), 0).astype(F32) == dest_row
    )
    pixels = dot(
        jnp.where(to_device, 1.0, 0.0).astype(BF16), jnp.concatenate(coded, axis=0)
    )
    out_ref[:, 2 * capacity :, :] = jnp.broadcast_to(
        pixels[:, None, :], (devices, PIXEL_ROWS, 128)
    ).astype(BF16)
    slot_row = dest_row * capacity + rank_row
    slots = 256
    per_block = slots // capacity
    loads[2].wait()
    values = values_ref[...]
    stores = []
    slot_at = lax.broadcasted_iota(jnp.int32, (slots, count), 0).astype(F32)
    for start in range(0, devices * capacity, slots):
        onehot = jnp.where(slot_at == slot_row - start, 1.0, 0.0).astype(BF16)
        rows = dot(onehot, values).astype(BF16)
        first = start // capacity
        for half in range(2):
            out_ref[first : first + per_block, half * capacity : (half + 1) * capacity, :] = (
                rows[:, half * 128 : (half + 1) * 128].reshape(per_block, capacity, 128)
            )
        store = pltpu.make_async_copy(
            out_ref.at[first : first + per_block],
            out_hbm.at[first : first + per_block],
            out_sem.at[len(stores)],
        )
        store.start()
        stores.append(store)
    for store in stores:
        store.wait()


def edge_body(rows, _, x_lo, x_hi, c_lo, c_hi, p_lo, p_hi, n_lo, n_hi, out_ref):
    tiles = lax.axis_size("tile")
    last = lax.axis_index("tile") == tiles - 1
    out_ref[...] = jnp.zeros_like(out_ref)
    for side in range(2):
        prev = (p_lo, p_hi)[side][...].astype(F32)
        after = (n_lo, n_hi)[side][...].astype(F32)
        at = 0 if side == 0 else prev.shape[1] - 1
        for array in range(2):
            own = ((x_lo, x_hi), (c_lo, c_hi))[array][side][...].astype(F32)
            for band in range(2):
                base = band * GROUP
                out_ref[array, side, base, :] = prev[2 * array + band, at]
                for r in range(rows):
                    out_ref[array, side, base + 1 + r, :] = own[band * rows + r, at]
                fold = own[(1 - band) * rows + rows - 1, at]
                out_ref[array, side, base + 1 + rows, :] = jnp.where(
                    last, fold, after[2 * array + band, at]
                )


def border_row(j, rows):
    return (j // 2) * rows + lax.rem(j, 2) * (rows - 1)


def lift_body(
    rows, x_ref, c_ref, k1_ref, b1_ref, k2_ref, pre_ref, grad_ref, k1t_ref, k2t_ref, k2t
):
    step = pl.program_id(0)
    band = step // rows
    r = lax.rem(step, rows)
    taps = k1_ref.shape[0] * x_ref.shape[2]
    lifted = k1_ref.shape[2]

    @pl.when(step == 0)
    def _():
        for t in range(k1_ref.shape[0]):
            k2t[t] = k2_ref[t].astype(F32).T.astype(BF16)
            k1t_ref[t] = k1_ref[t].astype(F32).T.astype(BF16)
        k2t_ref[...] = k2t[...]

    for source, weights, order, way, out_ref in (
        (x_ref, k1_ref, (-1, 0, 1), 1 - 2 * band, pre_ref),
        (c_ref, k2t, (1, 0, -1), 2 * band - 1, grad_ref),
    ):
        pieces = []
        for dy in (-1, 0, 1):
            at = r + way * dy
            row = source[band * rows + jnp.clip(at, 0, rows - 1)]
            if dy:
                row = jnp.where((at >= 0) & (at < rows), row, jnp.zeros_like(row))
            pieces.append(spread_columns(row, order))
        total = dot(jnp.concatenate(pieces, axis=1), weights[...].reshape(taps, lifted))
        if out_ref is pre_ref:
            total = total + b1_ref[...]
        out_ref[0] = total


def side_in_body(faces, matching_ref, k1_ref, k2t_ref, *rest):
    parts = rest[:faces]
    x_side, c_side = rest[faces:]
    for side in range(2):
        hop, their_side, flipped = matched(matching_ref, side, faces)
        near = partner_rows(parts, 0, hop, their_side, flipped)
        x_side[side] = side_forward(near, side, k1_ref)
        near = partner_rows(parts, 1, hop, their_side, flipped)
        c_side[side] = side_adjoint(near, their_side, flipped, k2t_ref)


def gelu_pair(v, grad):
    square = v * v
    t = jnp.tanh(v * (ROOT + (ROOT * CUBIC) * square))
    half = 0.5 + 0.5 * t
    slope = half + (0.5 * v) * (1.0 - t * t) * (ROOT + (3.0 * ROOT * CUBIC) * square)
    return (v * half).astype(BF16), (grad * slope).astype(BF16)


def unpack_received(capacity, recv_ref, values, keys):
    devices = recv_ref.shape[0]
    slots = devices * capacity
    per_lane = 128 // capacity
    for half in range(2):
        values[:, half * 128 : (half + 1) * 128] = recv_ref[
            :, half * capacity : (half + 1) * capacity, :
        ].reshape(slots, 128)
    owner = lax.broadcasted_iota(jnp.int32, (PIXEL_ROWS, 128), 1) // capacity
    for start in range(0, devices, per_lane):
        key = jnp.zeros((PIXEL_ROWS, 128), F32)
        for k in range(per_lane):
            code = recv_ref[start + k, 2 * capacity :, :].astype(F32)
            mine = (code - 1.0) * HIGH + pltpu.roll(code, HIGH, 1)
            if k:
                mine = pltpu.roll(mine, k * capacity, 1)
            key = jnp.where(owner == k, mine, key)
        keys[:, start * capacity : start * capacity + 128] = key


def row_taps(taps_ref, row):
    return jnp.concatenate([taps_ref[3 * row + dx] for dx in range(3)], axis=1)


def merge_shifts(wide, forward):
    channels = wide.shape[1] // 3
    left, mid, right = (wide[:, k * channels : (k + 1) * channels] for k in range(3))
    step = -1 if forward else 1
    return mid + shift_columns(left, step) + shift_columns(right, -step)


def border_body(
    rows, capacity, recv_in, pre_in, grad_in, prev_in, next_in, x_in, c_in, k1_in, k2t_in, x_side,
    c_side, inner_ref, gp_ref, edge_ref, values, keys, recv_ref, base, outside, strips, k1_ref, k2t_ref,
    edge_sums, sem,
):
    width = base.shape[2]
    channels = outside.shape[3]
    last = lax.axis_index("tile") == lax.axis_size("tile") - 1
    at_row = [0, rows - 1, rows, 2 * rows - 1]
    loads = []

    def load(source, target):
        copy = pltpu.make_async_copy(source, target, sem.at[len(loads)])
        loads.append(copy)
        copy.start()

    load(recv_in, recv_ref)
    for array, own in enumerate((x_in, c_in)):
        for band in range(2):
            plane = 2 * array + band
            load(prev_in.at[plane], outside.at[array, 2 * band])
            target = outside.at[array, 2 * band + 1]
            after = pltpu.make_async_copy(next_in.at[plane], target, sem.at[len(loads)])
            fold = pltpu.make_async_copy(
                own.at[(1 - band) * rows + rows - 1], target, sem.at[len(loads)]
            )

            @pl.when(last)
            def _():
                fold.start()

            @pl.when(jnp.logical_not(last))
            def _():
                after.start()

            loads.append(after)
    load(k1_in, k1_ref)
    load(k2t_in, k2t_ref)
    for array, source in enumerate((pre_in, grad_in)):
        for j in range(4):
            load(source.at[at_row[j]], base.at[array, j])
    for array, source in enumerate((pre_in, grad_in)):
        for side in range(2):
            start = 0 if side == 0 else width - GROUP
            load(source.at[:, start : start + GROUP], strips.at[array, side])
    loads[0].wait()
    unpack_received(capacity, recv_ref, values, keys)
    for copy in loads[1:]:
        copy.wait()

    lifted = base.shape[3]
    column = lax.broadcasted_iota(jnp.int32, (width, keys.shape[1]), 0).astype(F32)
    kept = []
    for pair, dy in (((0, 3), -1), ((1, 2), 1)):
        totals = []
        for array, (weights, order, way) in enumerate(
            ((k1_ref, (-1, 0, 1), 1), (k2t_ref, (1, 0, -1), -1))
        ):
            lhs = jnp.concatenate([spread_columns(outside[array, j], order) for j in pair], axis=0)
            row = 3 * (way * dy + 1)
            tap = weights[row : row + 3].reshape(3 * channels, lifted)
            own = jnp.concatenate([base[array, j] for j in pair], axis=0)
            totals.append(own + dot(lhs, tap))
        onehot = jnp.concatenate(
            [
                jnp.where(column == keys[0:1, :] - float(at_row[j] * width), 1.0, 0.0).astype(BF16)
                for j in pair
            ],
            axis=0,
        )
        v = totals[0] + dot(onehot, values[...])
        for k, j in enumerate(pair):
            at = GROUP * (j // 2) + 1 + (rows - 1) * (j % 2)
            piece = slice(k * width, (k + 1) * width)
            inner, gp = gelu_pair(
                add_edges(v[piece], x_side[0, at : at + 1, :], x_side[1, at : at + 1, :]),
                add_edges(totals[1][piece], c_side[0, at : at + 1, :], c_side[1, at : at + 1, :]),
            )
            inner_ref[j] = inner
            gp_ref[j] = gp
            kept.append(at)

    count = 4 * GROUP
    for array, side_ref in enumerate((x_side, c_side)):
        edge_sums[array] = side_ref[...].reshape(count, lifted)
        for b in range(2):
            for r in range(1, rows - 1):
                for side in range(2):
                    at = 2 * GROUP * side + GROUP * b + r + 1
                    spot = 0 if side == 0 else GROUP - 1
                    edge_sums[array, at : at + 1, :] += strips[
                        array, side, b * rows + r, spot : spot + 1, :
                    ]
    at = lax.broadcasted_iota(jnp.int32, (count, 1), 0)
    e = at & (GROUP - 1)
    b = (at // GROUP) & 1
    side = at // (2 * GROUP)
    inside = (e >= 2) & (e < rows)
    pixel = (b * rows + e - 1) * width + side * (width - 1)
    wanted = jnp.where(inside, pixel, -1).astype(F32)
    onehot = jnp.where(keys[0:1, :] == wanted, 1.0, 0.0).astype(BF16)
    v = edge_sums[0] + dot(onehot, values[...])
    inner, gp = gelu_pair(v, edge_sums[1])
    shape = (2, 2 * GROUP, lifted)
    edge_ref[0] = jnp.where(inside, inner.astype(F32), 0.0).reshape(shape)
    edge_ref[1] = jnp.where(inside, gp.astype(F32), 0.0).reshape(shape)
    for array, ref in enumerate((inner_ref, gp_ref)):
        for j in range(4):
            at = GROUP * (j // 2) + 1 + (rows - 1) * (j % 2)
            edge_ref[array, 0, at : at + 1, :] = ref[j, :16].astype(F32)[0:1]
            edge_ref[array, 1, at : at + 1, :] = ref[j, width - 16 :].astype(F32)[15:16]


def send_body(rows, faces, matching_ref, inner_ref, gp_ref, k2_ref, k1t_ref, *rest):
    parts = rest[:faces]
    up_ref, down_ref, side_ref = rest[faces:]
    width = inner_ref.shape[1]
    for side in range(2):
        hop, their_side, flipped = matched(matching_ref, side, faces)
        near = partner_rows(parts, 0, hop, their_side, flipped)
        side_ref[0, side] = side_forward(near, side, k2_ref)
        near = partner_rows(parts, 1, hop, their_side, flipped)
        side_ref[1, side] = side_adjoint(near, their_side, flipped, k1t_ref)
    for array, (source, taps, first) in enumerate(((inner_ref, k2_ref, 2), (gp_ref, k1t_ref, 0))):
        for pair, tap in (((0, 3), first), ((1, 2), 2 - first)):
            lhs = jnp.concatenate([source[j] for j in pair], axis=0)
            wide = dot(lhs, row_taps(taps, tap))
            for k, j in enumerate(pair):
                part = merge_shifts(wide[k * width : (k + 1) * width], array == 0)
                corner = GROUP * (j // 2) + (rows + 1) * (j % 2)
                part = add_edges(
                    part,
                    side_ref[array, 0, corner : corner + 1, :],
                    side_ref[array, 1, corner : corner + 1, :],
                )
                target = up_ref if j % 2 else down_ref
                target[2 * array + j // 2] = part.astype(BF16)


def middle_body(rows, _, values, keys, *rest):
    middle = rows - 2
    pre_refs, grad_refs = rest[:middle], rest[middle : 2 * middle]
    x_side, c_side, inner_ref, gp_ref = rest[2 * middle :]
    band = pl.program_id(0)
    width, lifted = pre_refs[0].shape[1], pre_refs[0].shape[2]
    column = lax.broadcasted_iota(jnp.int32, (width, keys.shape[1]), 0).astype(F32)
    onehots = []
    for k in range(middle):
        local = keys[0:1, :] - ((band * rows + k + 1) * width).astype(F32)
        onehots.append(jnp.where(column == local, 1.0, 0.0).astype(BF16))
    found = dot(jnp.concatenate(onehots, axis=0), values[...])
    for k in range(middle):
        at = band * GROUP + k + 2
        inner, gp = gelu_pair(
            add_edges(
                pre_refs[k][0] + found[k * width : (k + 1) * width],
                x_side[0, pl.ds(at, 1), :],
                x_side[1, pl.ds(at, 1), :],
            ),
            add_edges(grad_refs[k][0], c_side[0, pl.ds(at, 1), :], c_side[1, pl.ds(at, 1), :]),
        )
        inner_ref[k] = inner
        gp_ref[k] = gp


def inside_body(
    rows, inner_b, gp_b, inner_m, gp_m, side_ref, k2_ref, k1t_ref, x_ref, c_ref, b2_ref, ana_ref,
    ana_b, out_grad, grad_b, w2, w1,
):
    step = pl.program_id(0)
    band = step // rows
    r = lax.rem(step, rows)
    middle = rows - 2
    lifted, channels = k2_ref.shape[1], k2_ref.shape[2]

    @pl.when(step == 0)
    def _():
        for taps, w, way in ((k2_ref, w2, 1), (k1t_ref, w1, -1)):
            for b in range(2):
                for offset in (-1, 0, 1):
                    dy = offset * way * (1 - 2 * b)
                    for dx in range(3):
                        w[
                            b,
                            (offset + 1) * lifted : (offset + 2) * lifted,
                            dx * channels : (dx + 1) * channels,
                        ] = taps[3 * (dy + 1) + dx]

    def finish(row):
        low = max(row - 1, 0)
        high = min(row + 1, rows - 1)
        at = band * GROUP + row + 1
        for array, (border, inner, w, own) in enumerate(
            ((inner_b, inner_m, w2, x_ref), (gp_b, gp_m, w1, c_ref))
        ):
            pieces = []
            for k in range(low, high + 1):
                if k == 0 or k == rows - 1:
                    pieces.append(border[2 * band + k // (rows - 1)])
                else:
                    pieces.append(inner[middle * band + k - 1])
            taps = w[band, (low - row + 1) * lifted : (high - row + 2) * lifted, :]
            total = merge_shifts(dot(jnp.concatenate(pieces, axis=1), taps), array == 0)
            total = add_edges(
                total + own[0].astype(F32),
                side_ref[array, 0, pl.ds(at, 1), :],
                side_ref[array, 1, pl.ds(at, 1), :],
            )
            if array == 0:
                total = total + b2_ref[...]
            if row == 0 or row == rows - 1:
                (ana_b, grad_b)[array][0] = total
            elif array == 0:
                ana_ref[0] = total.astype(BF16)
            else:
                out_grad[0] = total

    for row in range(rows):

        @pl.when(r == row)
        def _():
            finish(row)


def final_body(
    rows, ana_b, grad_b, _, __, up_ref, prev_ref, next_ref, out_ana, out_grad
):
    j = pl.program_id(0)
    band = j // 2
    bottom = lax.rem(j, 2)
    last = lax.axis_index("tile") == lax.axis_size("tile") - 1
    for array, (acc, out) in enumerate(((ana_b, out_ana), (grad_b, out_grad))):
        after = jnp.where(last, up_ref[2 * array + 1 - band], next_ref[2 * array + band])
        add = jnp.where(bottom == 1, after, prev_ref[2 * array + band])
        out[0] = (acc[0] + add.astype(F32)).astype(out.dtype)


def per_device(
    state,
    obs_values,
    obs_dest,
    obs_pixel,
    matching,
    kernel_one,
    bias_one,
    kernel_two,
    bias_two,
    cotangent,
):
    rows, width, channels = state.shape[3], state.shape[4], state.shape[5]
    lifted = kernel_one.shape[2]
    tiles, faces = lax.axis_size("tile"), lax.axis_size("face")
    devices = tiles * faces
    count = obs_values.shape[0]
    capacity = 2 * count // devices
    all_rows = 2 * rows
    middle = rows - 2
    chunk = 2 * capacity + PIXEL_ROWS
    x = state.reshape(all_rows, width, channels)
    c = cotangent.reshape(all_rows, width, channels)
    forward = [(i, i + 1) for i in range(tiles - 1)]
    backward = [(i + 1, i) for i in range(tiles - 1)]
    up_rows = jnp.concatenate([x[rows - 1 :: rows], c[rows - 1 :: rows]], axis=0)
    down_rows = jnp.concatenate([x[0::rows], c[0::rows]], axis=0)
    prev_rows = lax.ppermute(up_rows, "tile", forward)
    next_rows = lax.ppermute(down_rows, "tile", backward)
    strip = 16

    def ends(planes):
        return jnp.concatenate([planes[:, :strip], planes[:, width - strip :]], axis=1)

    prev_ends = lax.ppermute(ends(up_rows), "tile", forward)
    next_ends = lax.ppermute(ends(down_rows), "tile", backward)
    smem = pl.BlockSpec(memory_space=pltpu.SMEM)
    vmem = pl.BlockSpec(memory_space=pltpu.VMEM)
    hbm = pl.BlockSpec(memory_space=pl.ANY)

    def exchange(own):
        parts = [own]
        for k in range(1, faces):
            parts.append(
                lax.ppermute(own, "face", [((i + k) % faces, i) for i in range(faces)])
            )
        return parts

    packed = pl.pallas_call(
        functools.partial(pack_body, capacity),
        in_specs=[hbm] * 3,
        out_specs=hbm,
        out_shape=pltpu.HBM((devices, chunk, 128), BF16),
        scratch_shapes=[
            pltpu.VMEM((1, count), jnp.int32),
            pltpu.VMEM((1, count), jnp.int32),
            pltpu.VMEM((count, lifted), BF16),
            pltpu.VMEM((devices, chunk, 128), BF16),
            pltpu.SemaphoreType.DMA((3,)),
            pltpu.SemaphoreType.DMA((devices * capacity // 256,)),
        ],
        compiler_params=params(16),
        cost_estimate=cost(2 * devices * capacity * count * lifted, 2 << 20),
        name="pack",
    )(far(obs_dest.reshape(1, count)), far(obs_pixel.reshape(1, count)), far(obs_values))
    received = lax.all_to_all(packed, ("face", "tile"), 0, 0, tiled=True)

    b1 = bias_one.reshape(1, lifted)
    b2 = bias_two.reshape(1, channels)
    row_block = lambda n: pl.BlockSpec((1, width, n), lambda i: (i, 0, 0))
    edge_block = lambda n: pl.BlockSpec((1, width, n), lambda i: (border_row(i, rows), 0, 0))
    conv_flops = 2 * 9 * all_rows * width * channels * lifted
    pre, grad_inner, k1t, k2t = pl.pallas_call(
        functools.partial(lift_body, rows),
        grid=(all_rows,),
        in_specs=[
            fixed(x.shape), fixed(c.shape), fixed(kernel_one.shape), fixed(b1.shape),
            fixed(kernel_two.shape),
        ],
        out_specs=[row_block(lifted)] * 2
        + [fixed(kernel_two.shape), fixed(kernel_one.shape)],
        out_shape=[pltpu.HBM((all_rows, width, lifted), F32)] * 2
        + [pltpu.HBM(kernel_two.shape, BF16), pltpu.HBM(kernel_one.shape, BF16)],
        scratch_shapes=[pltpu.VMEM(kernel_one.shape, BF16)],
        compiler_params=params(),
        cost_estimate=cost(2 * conv_flops, 12 << 20),
        name="lift",
    )(x, c, kernel_one, b1, kernel_two)
    pre, grad_inner = far(pre), far(grad_inner)

    low = lambda n: pl.BlockSpec((n, strip, channels), lambda *_: (0, 0, 0))
    high = lambda n, at: pl.BlockSpec((n, strip, channels), lambda *_: (0, at, 0))
    tail = width // strip - 1
    edge_shape = (2, 2, 2 * GROUP, channels)
    edges = pl.pallas_call(
        functools.partial(edge_body, rows),
        grid=(1,),
        in_specs=[hbm] + [low(all_rows), high(all_rows, tail)] * 2 + [low(4), high(4, 1)] * 2,
        out_specs=fixed(edge_shape),
        out_shape=jax.ShapeDtypeStruct(edge_shape, F32),
        compiler_params=params(8),
        cost_estimate=cost(0, 1 << 18),
        name="edges",
    )(k1t, x, x, c, c, prev_ends, prev_ends, next_ends, next_ends)
    parts = exchange(edges)

    side_in = (2, 2 * GROUP, lifted)
    x_side, c_side = pl.pallas_call(
        functools.partial(side_in_body, faces),
        in_specs=[smem] + [vmem] * (2 + faces),
        out_specs=[vmem] * 2,
        out_shape=[jax.ShapeDtypeStruct(side_in, F32)] * 2,
        compiler_params=params(8),
        cost_estimate=cost(0, 2 << 20),
        name="sides_in",
    )(matching, kernel_one, k2t, *parts)
    plane = (4, width, channels)
    side_two = (2, 2, 2 * GROUP, lifted)
    slots = devices * capacity
    onehot_flops = 2 * width * slots * lifted
    other_block = pl.BlockSpec(
        (1, width, channels), lambda j: ((1 - j // 2) * rows + rows - 1, 0, 0)
    )
    border_shape = hold((4, width, lifted), BF16)
    border_shape = hold((4, width, lifted), BF16)
    inner_b, gp_b, edges_two, values, keys = pl.pallas_call(
        functools.partial(border_body, rows, capacity),
        in_specs=[hbm] * 9 + [vmem] * 2,
        out_specs=[vmem] * 5,
        out_shape=[
            border_shape,
            border_shape,
            jax.ShapeDtypeStruct(side_two, F32),
            hold((slots, lifted), BF16),
            hold((PIXEL_ROWS, slots), F32),
        ],
        scratch_shapes=[
            pltpu.VMEM(received.shape, BF16),
            pltpu.VMEM((2, 4, width, lifted), F32),
            pltpu.VMEM((2, 4, width, channels), BF16),
            pltpu.VMEM((2, 2, all_rows, GROUP, lifted), F32),
            pltpu.VMEM(kernel_one.shape, BF16),
            pltpu.VMEM(k2t.shape, BF16),
            pltpu.VMEM((2, 4 * GROUP, lifted), F32),
            pltpu.SemaphoreType.DMA((23,)),
        ],
        compiler_params=params(32),
        cost_estimate=cost(4 * onehot_flops + conv_flops // 6, 10 << 20),
        name="border",
    )(
        far(received), pre, grad_inner, far(prev_rows), far(next_rows), far(x), far(c),
        far(kernel_one), far(k2t), x_side, c_side,
    )
    inner_b, gp_b, values, keys = held(inner_b), held(gp_b), held(values), held(keys)
    parts_two = exchange(edges_two)

    side_out = (2, 2, 2 * GROUP, channels)
    up, down, sides = pl.pallas_call(
        functools.partial(send_body, rows, faces),
        in_specs=[smem] + [vmem] * (4 + faces),
        out_specs=[vmem] * 3,
        out_shape=[
            jax.ShapeDtypeStruct(plane, BF16),
            jax.ShapeDtypeStruct(plane, BF16),
            jax.ShapeDtypeStruct(side_out, F32),
        ],
        compiler_params=params(16),
        cost_estimate=cost(conv_flops // 6, 4 << 20),
        name="send",
    )(matching, inner_b, gp_b, kernel_two, k1t, *parts_two)
    from_prev = lax.ppermute(up, "tile", forward)
    from_next = lax.ppermute(down, "tile", backward)

    middle_block = lambda k: pl.BlockSpec((1, width, lifted), lambda i: (i * rows + k + 1, 0, 0))
    inner_m, gp_m = pl.pallas_call(
        functools.partial(middle_body, rows),
        grid=(2,),
        in_specs=[hbm, fixed(values.shape), fixed(keys.shape)]
        + [middle_block(k) for k in range(middle)] * 2
        + [fixed(side_in)] * 2,
        out_specs=[pl.BlockSpec((middle, width, lifted), lambda i: (i, 0, 0))] * 2,
        out_shape=[hold((2 * middle, width, lifted), BF16)] * 2,
        compiler_params=params(),
        cost_estimate=cost(2 * middle * onehot_flops, 10 << 20),
        name="middle",
    )(down, values, keys, *[pre] * middle, *[grad_inner] * middle, x_side, c_side)
    inner_m, gp_m = held(inner_m), held(gp_m)

    inner_block = lambda n: pl.BlockSpec(
        (1, width, n),
        lambda i: ((i // rows) * rows + jnp.clip(lax.rem(i, rows), 1, rows - 2), 0, 0),
    )
    held_block = pl.BlockSpec(
        (1, width, channels), lambda i: (2 * (i // rows) + lax.rem(i, rows) // (rows - 1), 0, 0)
    )
    analysis, ana_b, grad_state, grad_b = pl.pallas_call(
        functools.partial(inside_body, rows),
        grid=(all_rows,),
        in_specs=[
            fixed(inner_b.shape),
            fixed(gp_b.shape),
            fixed(inner_m.shape),
            fixed(gp_m.shape),
            fixed(side_out),
            fixed(kernel_two.shape),
            fixed(k1t.shape),
            row_block(channels),
            row_block(channels),
            fixed(b2.shape),
        ],
        out_specs=[inner_block(channels), held_block, inner_block(channels), held_block],
        out_shape=[
            pltpu.HBM((all_rows, width, channels), BF16),
            hold(plane, F32),
            pltpu.HBM((all_rows, width, channels), F32),
            hold(plane, F32),
        ],
        scratch_shapes=[pltpu.VMEM((2, 3 * lifted, 3 * channels), BF16)] * 2,
        compiler_params=params(),
        cost_estimate=cost(2 * conv_flops, 14 << 20),
        name="inside",
    )(inner_b, gp_b, inner_m, gp_m, sides, kernel_two, k1t, x, c, b2)
    ana_b, grad_b = held(ana_b), held(grad_b)

    analysis, grad_state = pl.pallas_call(
        functools.partial(final_body, rows),
        grid=(4,),
        in_specs=[row_block(channels)] * 2
        + [hbm] * 2
        + [fixed(plane)] * 3,
        out_specs=[edge_block(channels)] * 2,
        out_shape=[
            pltpu.HBM((all_rows, width, channels), BF16),
            pltpu.HBM((all_rows, width, channels), F32),
        ],
        input_output_aliases={2: 0, 3: 1},
        compiler_params=params(16),
        cost_estimate=cost(0, 6 << 20),
        name="final",
    )(ana_b, grad_b, far(analysis), far(grad_state), up, from_prev, from_next)
    return analysis.reshape(state.shape), grad_state.reshape(cotangent.shape)


def solution(mesh):
    return jax.shard_map(
        per_device,
        mesh=mesh,
        in_specs=(
            P("face", "tile", None, None, None, None),
            P(("face", "tile"), None),
            P(("face", "tile"), None),
            P(("face", "tile")),
            P(),
            P(),
            P(),
            P(),
            P(),
            P("face", "tile", None, None, None, None),
        ),
        out_specs=(
            P("face", "tile", None, None, None, None),
            P("face", "tile", None, None, None, None),
        ),
        check_vma=False,
    )
```

```python
import functools
import math

import jax
import jax.numpy as jnp
from jax import lax
from jax.experimental import pallas as pl
from jax.experimental.pallas import tpu as pltpu
from jax.sharding import PartitionSpec as P

F32 = jnp.float32
BF16 = jnp.bfloat16
GROUP = 8
HIGH = 64
PIXEL_ROWS = 8
ROOT = math.sqrt(2.0 / math.pi)
CUBIC = 0.044715


def params(mib=24):
    return pltpu.CompilerParams(vmem_limit_bytes=mib << 20)


def cost(flops, nbytes):
    return pl.CostEstimate(flops=int(flops), bytes_accessed=int(nbytes), transcendentals=0)


def hold(shape, kind):
    return pltpu.VMEM(shape, kind)


def held(array):
    return pltpu.with_memory_space_constraint(array, pltpu.VMEM)


def far(array):
    return pltpu.with_memory_space_constraint(array, pltpu.HBM)


def fixed(shape):
    return pl.BlockSpec(shape, lambda *_: (0,) * len(shape))


def dot(a, b):
    return jnp.dot(a, b, preferred_element_type=F32)


def matched(matching_ref, side, faces):
    face = lax.axis_index("face")
    partner = matching_ref[face, side, 0]
    return lax.rem(partner - face + faces, faces), matching_ref[face, side, 1], matching_ref[face, side, 2]


def is_even():
    return lax.rem(lax.axis_index("tile"), 2) == 0


def is_last():
    return lax.axis_index("tile") == lax.axis_size("tile") - 1


def partner_rows(part_refs, array, hop, their_side, flipped):
    rows = None
    for k, ref in enumerate(part_refs):
        mine = jnp.where(their_side == 1, ref[array, 1], ref[array, 0])
        rows = mine if rows is None else jnp.where(hop == k, mine, rows)
    swapped = jnp.concatenate([rows[GROUP:], rows[:GROUP]], axis=0)
    return jnp.where(flipped == 1, swapped, rows)


def rolled_rows(rows, step):
    first, second = rows[:GROUP], rows[GROUP:]
    if step:
        first = pltpu.roll(first, (-step) % GROUP, 0)
        second = pltpu.roll(second, step % GROUP, 0)
    return jnp.concatenate([first, second], axis=0).astype(BF16)


def side_forward(rows, side, taps_ref):
    lhs = jnp.concatenate([rolled_rows(rows, dy) for dy in (-1, 0, 1)], axis=1)
    taps = jnp.concatenate([taps_ref[3 * row + 2 * side] for row in range(3)], axis=0)
    return dot(lhs, taps)


def side_adjoint(rows, their_side, flipped, taps_ref):
    lhs = jnp.concatenate([rolled_rows(rows, -dy) for dy in (-1, 0, 1)], axis=1)
    order = [jnp.where(flipped == 1, 2 - row, row) for row in range(3)]
    taps = jnp.concatenate([taps_ref[3 * row + 2 * their_side] for row in order], axis=0)
    return dot(lhs, taps)


def shift_columns(values, step):
    count = values.shape[0]
    at = lax.broadcasted_iota(jnp.int32, values.shape, 0)
    moved = pltpu.roll(values, (-step) % count, 0)
    edge = count - 1 if step == 1 else 0
    return jnp.where(at == edge, 0.0, moved)


def spread_columns(row, order):
    wide = row.astype(F32)
    return jnp.concatenate(
        [row if s == 0 else shift_columns(wide, s).astype(BF16) for s in order], axis=1
    )


def add_edges(values, left, right):
    count = values.shape[0]
    at = lax.broadcasted_iota(jnp.int32, (GROUP, values.shape[1]), 0)
    first = values[:GROUP] + jnp.where(at == 0, left, 0.0)
    tail = values[count - GROUP :] + jnp.where(at == GROUP - 1, right, 0.0)
    return jnp.concatenate([first, values[GROUP : count - GROUP], tail], axis=0)


def pack_body(
    capacity, dest_in, pixel_in, values_in, out_hbm, dest_ref, pixel_ref, values_ref, out_ref, in_sem,
    out_sem,
):
    count = values_ref.shape[0]
    devices = out_ref.shape[0]
    block = 128
    loads = [
        pltpu.make_async_copy(source, target, in_sem.at[k])
        for k, (source, target) in enumerate(
            ((dest_in, dest_ref), (pixel_in, pixel_ref), (values_in, values_ref))
        )
    ]
    for load in loads:
        load.start()
    loads[0].wait()
    loads[1].wait()
    dest_row = dest_ref[...].astype(F32)
    pixel_row = pixel_ref[...]
    eye = lax.broadcasted_iota(jnp.int32, (block, block), 0) == lax.broadcasted_iota(
        jnp.int32, (block, block), 1
    )

    def column(row, start):
        piece = row[:, start : start + block]
        return jnp.sum(jnp.where(eye, piece, 0.0), axis=1, keepdims=True)

    high_row = lax.shift_right_logical(pixel_row, 6).astype(F32) + 1.0
    low_row = (pixel_row & (HIGH - 1)).astype(F32)
    own = lax.broadcasted_iota(jnp.int32, (block, count), 0)
    other = lax.broadcasted_iota(jnp.int32, (block, count), 1)
    lane = lax.broadcasted_iota(jnp.int32, (block, 128), 1)
    lane_rank = (lane & (HIGH - 1)).astype(F32)
    rank_row = jnp.zeros((1, count), F32)
    coded = []
    for start in range(0, count, block):
        same = column(dest_row, start) == dest_row
        later = (own + start) < other
        earlier = (own + start) > other
        rank_row = rank_row + jnp.sum(
            jnp.where(same & later, 1.0, 0.0), axis=0, keepdims=True
        )
        rank = jnp.sum(jnp.where(same & earlier, 1.0, 0.0), axis=1, keepdims=True)
        code = jnp.where(lane < HIGH, column(high_row, start), column(low_row, start))
        coded.append(jnp.where(rank == lane_rank, code, 0.0).astype(BF16))
    to_device = (
        lax.broadcasted_iota(jnp.int32, (devices, count), 0).astype(F32) == dest_row
    )
    pixels = dot(
        jnp.where(to_device, 1.0, 0.0).astype(BF16), jnp.concatenate(coded, axis=0)
    )
    out_ref[:, 2 * capacity :, :] = jnp.broadcast_to(
        pixels[:, None, :], (devices, PIXEL_ROWS, 128)
    ).astype(BF16)
    slot_row = dest_row * capacity + rank_row
    slots = 512
    per_block = slots // capacity
    loads[2].wait()
    values = values_ref[...]
    stores = []
    slot_at = lax.broadcasted_iota(jnp.int32, (slots, count), 0).astype(F32)
    for start in range(0, devices * capacity, slots):
        onehot = jnp.where(slot_at == slot_row - start, 1.0, 0.0).astype(BF16)
        rows = dot(onehot, values).astype(BF16)
        first = start // capacity
        for half in range(2):
            out_ref[first : first + per_block, half * capacity : (half + 1) * capacity, :] = (
                rows[:, half * 128 : (half + 1) * 128].reshape(per_block, capacity, 128)
            )
        store = pltpu.make_async_copy(
            out_ref.at[first : first + per_block],
            out_hbm.at[first : first + per_block],
            out_sem.at[len(stores)],
        )
        store.start()
        stores.append(store)
    for store in stores:
        store.wait()


def end_rows(rows, x_ends, c_ends, pair_ends, cross_ends):
    prev, after = [], []
    even = is_even()
    for side in range(2):
        pair, cross = pair_ends[side], cross_ends[side]
        prev.append(jnp.where(even, cross, pair))
        after.append(jnp.where(even, pair, cross))
    outside = {}
    for array, own in enumerate((x_ends, c_ends)):
        for side in range(2):
            for band in range(2):
                plane = 2 * array + band
                fold = own[side][(1 - band) * rows + rows - 1]
                outside[array, side, 2 * band] = prev[side][plane]
                outside[array, side, 2 * band + 1] = jnp.where(is_last(), fold, after[side][plane])
    return outside


def edge_body(rows, x_lo, x_hi, c_lo, c_hi, a_lo, a_hi, b_lo, b_hi, out_ref):
    out_ref[...] = jnp.zeros_like(out_ref)
    wide = lambda refs: [ref[...].astype(F32) for ref in refs]
    x_ends, c_ends = wide((x_lo, x_hi)), wide((c_lo, c_hi))
    outside = end_rows(rows, x_ends, c_ends, wide((a_lo, a_hi)), wide((b_lo, b_hi)))
    for array, own in enumerate((x_ends, c_ends)):
        for side in range(2):
            at = 0 if side == 0 else own[side].shape[1] - 1
            for band in range(2):
                base = band * GROUP
                out_ref[array, side, base, :] = outside[array, side, 2 * band][at]
                for r in range(rows):
                    out_ref[array, side, base + 1 + r, :] = own[side][band * rows + r, at]
                out_ref[array, side, base + 1 + rows, :] = outside[array, side, 2 * band + 1][at]


def row_groups(rows, way):
    first, last = ((0, 0), (1, rows - 1)), ((0, rows - 1), (1, 0))
    if way < 0:
        first, last = last, first
    inner = tuple((b, r) for b in range(2) for r in range(1, rows - 1))
    return ((inner, (-1, 0, 1)), (first, (0, 1)), (last, (-1, 0)))


def border_index(j, rows):
    return (j // 2) * rows + (j % 2) * (rows - 1)


def border_row(j, rows):
    return (j // 2) * rows + lax.rem(j, 2) * (rows - 1)


def lift_body(
    rows, x_in, c_in, k1_in, k2_in, b1_ref, pre_out, grad_out, k1t_ref, k2t_ref, x_ref, c_ref, k1_ref,
    k2_ref, cat, held_rows, sem,
):
    width, channels = x_ref.shape[1], x_ref.shape[2]
    lifted = k1_ref.shape[2]
    used = [0]

    def slot():
        used[0] += 1
        return sem.at[used[0] - 1]

    loads = [
        pltpu.make_async_copy(source, target, slot())
        for source, target in ((x_in, x_ref), (k1_in, k1_ref), (k2_in, k2_ref), (c_in, c_ref))
    ]
    for load in loads:
        load.start()
    stores = []
    for array, (source, weights, order, out) in enumerate(
        ((x_ref, k1_ref, (-1, 0, 1), pre_out), (c_ref, k2t_ref, (1, 0, -1), grad_out))
    ):
        way = 1 - 2 * array
        loads[2 * array].wait()
        loads[2 * array + 1].wait()
        if array == 1:
            for t in range(k2_ref.shape[0]):
                k2t_ref[t] = k2_ref[t].astype(F32).T.astype(BF16)
        for i in range(2 * rows):
            cat[array, i] = spread_columns(source[i], order)
        members, steps = row_groups(rows, way)[0]
        lhs = jnp.concatenate(
            [
                jnp.concatenate(
                    [cat[array, b * rows + r + way * (1 - 2 * b) * dy] for dy in steps], axis=1
                )
                for b, r in members
            ],
            axis=0,
        )
        taps = weights[...].reshape(3 * len(steps) * channels, lifted)
        half = len(members) // 2
        for first in (0, half):
            total = dot(lhs[first * width : (first + half) * width], taps)
            if array == 0:
                total = total + b1_ref[...]
            for k in range(half):
                held_rows[array, first + k] = total[k * width : (k + 1) * width]
                store = pltpu.make_async_copy(
                    held_rows.at[array, first + k], out.at[first + k], slot()
                )
                store.start()
                stores.append(store)
    for t in range(k1_ref.shape[0]):
        k1t_ref[t] = k1_ref[t].astype(F32).T.astype(BF16)
    for store in stores:
        store.wait()


def border_pieces(array, pair, outside, own, inside):
    first = (pair[0] == 0) == (array == 0)
    return [outside, own, inside] if first else [inside, own, outside]


def rim_in_body(
    rows, matching_ref, k1_in, b1_ref, k2t_in, pre_lo, pre_hi, grad_lo, grad_hi, x_lo, x_hi, c_lo, c_hi,
    a_lo, a_hi, b_lo, b_hi, base_ref, taps_ref, k1_ref, k2t_ref, sem,
):
    loads = [
        pltpu.make_async_copy(k1_in, k1_ref, sem.at[0]),
        pltpu.make_async_copy(k2t_in, k2t_ref, sem.at[1]),
    ]
    for load in loads:
        load.start()
    for load in loads:
        load.wait()
    face = lax.axis_index("face")
    for side in range(2):
        their_side, flipped = matching_ref[face, side, 1], matching_ref[face, side, 2]
        for row in range(3):
            taps_ref[0, side, row] = k1_ref[3 * row + 2 * side]
            turned = jnp.where(flipped == 1, 2 - row, row)
            taps_ref[1, side, row] = k2t_ref[3 * turned + 2 * their_side]
    whole = lambda refs: [ref[...] for ref in refs]
    x_ends, c_ends = whole((x_lo, x_hi)), whole((c_lo, c_hi))
    outside = end_rows(rows, x_ends, c_ends, whole((a_lo, a_hi)), whole((b_lo, b_hi)))
    channels, lifted = k1_ref.shape[1], k1_ref.shape[2]
    base_ref[...] = jnp.zeros_like(base_ref)
    for array, (strips, own, weights, order) in enumerate(
        (
            ((pre_lo, pre_hi), x_ends, k1_ref, (-1, 0, 1)),
            ((grad_lo, grad_hi), c_ends, k2t_ref, (1, 0, -1)),
        )
    ):
        for side in range(2):
            spot = 0 if side == 0 else GROUP - 1
            for b in range(2):
                for r in range(1, rows - 1):
                    at = 2 * GROUP * side + GROUP * b + r + 1
                    base_ref[array, at : at + 1, :] = strips[side][
                        b * (rows - 2) + r - 1, spot : spot + 1, :
                    ]
        for pair in ((0, 3), (1, 2)):
            spots = [(side, j) for side in range(2) for j in pair]
            lhs = []
            for side, j in spots:
                i = border_index(j, rows)
                planes = border_pieces(
                    array, pair, outside[array, side, j], own[side][i], own[side][i + 1 - 2 * (j % 2)]
                )
                lhs.append(
                    jnp.concatenate([spread_columns(plane, order) for plane in planes], axis=1)
                )
            found = dot(
                jnp.concatenate(lhs, axis=0),
                weights[...].reshape(weights.shape[0] * channels, lifted),
            )
            if array == 0:
                found = found + b1_ref[...]
            strip = found.shape[0] // len(spots)
            for k, (side, j) in enumerate(spots):
                at = 2 * GROUP * side + GROUP * (j // 2) + 1 + (rows - 1) * (j % 2)
                spot = k * strip + (0 if side == 0 else strip - 1)
                base_ref[array, at : at + 1, :] = found[spot : spot + 1]


def side_in_body(faces, matching_ref, taps_ref, base_ref, *rest):
    parts = rest[:faces]
    x_side, c_side, sums_ref = rest[faces:]
    taps = taps_ref[...].reshape(2, 2, 3 * taps_ref.shape[3], taps_ref.shape[4])
    for side in range(2):
        hop, their_side, flipped = matched(matching_ref, side, faces)
        for array, out in enumerate((x_side, c_side)):
            near = partner_rows(parts, array, hop, their_side, flipped)
            way = 1 - 2 * array
            lhs = jnp.concatenate([rolled_rows(near, way * dy) for dy in (-1, 0, 1)], axis=1)
            out[side] = dot(lhs, taps[array, side])
    for array, out in enumerate((x_side, c_side)):
        sums_ref[array] = base_ref[array] + out[...].reshape(sums_ref.shape[1:])


def gelu_pair(v, grad):
    square = v * v
    t = jnp.tanh(v * (ROOT + (ROOT * CUBIC) * square))
    half = 0.5 + 0.5 * t
    slope = half + (0.5 * v) * (1.0 - t * t) * (ROOT + (3.0 * ROOT * CUBIC) * square)
    return (v * half).astype(BF16), (grad * slope).astype(BF16)


def unpack_received(capacity, recv_ref, values, keys):
    devices = recv_ref.shape[0]
    slots = devices * capacity
    per_lane = 128 // capacity
    for half in range(2):
        values[:, half * 128 : (half + 1) * 128] = recv_ref[
            :, half * capacity : (half + 1) * capacity, :
        ].reshape(slots, 128)
    owner = lax.broadcasted_iota(jnp.int32, (PIXEL_ROWS, 128), 1) // capacity
    for start in range(0, devices, per_lane):
        key = jnp.zeros((PIXEL_ROWS, 128), F32)
        for k in range(per_lane):
            code = recv_ref[start + k, 2 * capacity :, :].astype(F32)
            mine = (code - 1.0) * HIGH + pltpu.roll(code, HIGH, 1)
            if k:
                mine = pltpu.roll(mine, k * capacity, 1)
            key = jnp.where(owner == k, mine, key)
        keys[:, start * capacity : start * capacity + 128] = key


def row_taps(taps_ref, row):
    return jnp.concatenate([taps_ref[3 * row + dx] for dx in range(3)], axis=1)


def merge_shifts(wide, forward):
    channels = wide.shape[1] // 3
    left, mid, right = (wide[:, k * channels : (k + 1) * channels] for k in range(3))
    step = -1 if forward else 1
    return mid + shift_columns(left, step) + shift_columns(right, -step)


def rim_body(rows, width, capacity, recv_ref, base_ref, edge_ref, values, keys):
    unpack_received(capacity, recv_ref, values, keys)
    at = lax.broadcasted_iota(jnp.int32, (4 * GROUP, 1), 0)
    e = at & (GROUP - 1)
    b = (at // GROUP) & 1
    side = at // (2 * GROUP)
    inside = (e >= 1) & (e <= rows)
    pixel = (b * rows + e - 1) * width + side * (width - 1)
    wanted = jnp.where(inside, pixel, -1).astype(F32)
    onehot = jnp.where(keys[0:1, :] == wanted, 1.0, 0.0).astype(BF16)
    v = base_ref[0] + dot(onehot, values[...])
    inner, gp = gelu_pair(v, base_ref[1])
    shape = (2, 2 * GROUP, v.shape[1])
    edge_ref[0] = jnp.where(inside, inner.astype(F32), 0.0).reshape(shape)
    edge_ref[1] = jnp.where(inside, gp.astype(F32), 0.0).reshape(shape)


def border_body(
    rows, values, keys, x_side, c_side, b1_ref, a_in, b_in, x_in, c_in, k1_in, k2t_in, inner_ref, gp_ref,
    x_ref, c_ref, outside, k1_ref, k2t_ref, sem,
):
    width, lifted = inner_ref.shape[1], inner_ref.shape[2]
    channels = outside.shape[3]
    even, last = is_even(), is_last()
    waits = []

    def load(target, *sources):
        slot = sem.at[len(waits)]
        for condition, source in sources:
            copy = pltpu.make_async_copy(source, target, slot)
            if condition is None:
                copy.start()
            else:
                pl.when(condition)(copy.start)
        waits.append(copy)

    for array, (source, target, weights, held_weights) in enumerate(
        ((x_in, x_ref, k1_in, k1_ref), (c_in, c_ref, k2t_in, k2t_ref))
    ):
        load(target, (None, source))
        load(held_weights, (None, weights))
        for j in range(4):
            band = j // 2
            plane = 2 * array + band
            if j % 2 == 0:
                choices = ((even, b_in.at[plane]), (jnp.logical_not(even), a_in.at[plane]))
            else:
                fold = source.at[(1 - band) * rows + rows - 1]
                middle = jnp.logical_not(even) & jnp.logical_not(last)
                choices = ((last, fold), (even, a_in.at[plane]), (middle, b_in.at[plane]))
            load(outside.at[array, j], *choices)

    column = lax.broadcasted_iota(jnp.int32, (width, keys.shape[1]), 0).astype(F32)
    for pair in ((0, 3), (1, 2)):
        onehot = jnp.concatenate(
            [
                jnp.where(
                    column == keys[0:1, :] - float(border_index(j, rows) * width), 1.0, 0.0
                ).astype(BF16)
                for j in pair
            ],
            axis=0,
        )
        found = dot(onehot, values[...]) + b1_ref[...]
        totals = []
        for array, (own, weights, order) in enumerate(
            ((x_ref, k1_ref, (-1, 0, 1)), (c_ref, k2t_ref, (1, 0, -1)))
        ):
            if pair[0] == 0:
                for copy in waits[6 * array : 6 * array + 6]:
                    copy.wait()
            lhs = []
            for j in pair:
                i = border_index(j, rows)
                planes = border_pieces(
                    array, pair, outside[array, j], own[i], own[i + 1 - 2 * (j % 2)]
                )
                lhs.append(
                    jnp.concatenate([spread_columns(plane, order) for plane in planes], axis=1)
                )
            totals.append(
                dot(
                    jnp.concatenate(lhs, axis=0),
                    weights[...].reshape(weights.shape[0] * channels, lifted),
                )
            )
        v = found + totals[0]
        for k, j in enumerate(pair):
            at = GROUP * (j // 2) + 1 + (rows - 1) * (j % 2)
            piece = slice(k * width, (k + 1) * width)
            inner, gp = gelu_pair(
                add_edges(v[piece], x_side[0, at : at + 1, :], x_side[1, at : at + 1, :]),
                add_edges(totals[1][piece], c_side[0, at : at + 1, :], c_side[1, at : at + 1, :]),
            )
            inner_ref[j] = inner
            gp_ref[j] = gp


def send_body(rows, faces, matching_ref, inner_ref, gp_ref, k2_ref, k1t_ref, *rest):
    parts = rest[:faces]
    pair_ref, cross_ref, side_ref = rest[faces:]
    even = is_even()
    width = inner_ref.shape[1]
    for side in range(2):
        hop, their_side, flipped = matched(matching_ref, side, faces)
        near = partner_rows(parts, 0, hop, their_side, flipped)
        side_ref[0, side] = side_forward(near, side, k2_ref)
        near = partner_rows(parts, 1, hop, their_side, flipped)
        side_ref[1, side] = side_adjoint(near, their_side, flipped, k1t_ref)
    up = jnp.where(even, 1, 0)
    for array, (source, taps) in enumerate(((inner_ref, k2_ref), (gp_ref, k1t_ref))):
        for group in range(2):
            members = ((pair_ref, group, up), (cross_ref, 1 - group, 1 - up))
            tap = jnp.where((group == up) == (array == 0), 2, 0)
            lhs = jnp.concatenate([source[2 * band + bottom] for _, band, bottom in members], axis=0)
            wide = dot(lhs, row_taps(taps, tap))
            for k, (target, band, bottom) in enumerate(members):
                part = merge_shifts(wide[k * width : (k + 1) * width], array == 0)
                corner = GROUP * band + (rows + 1) * bottom
                part = add_edges(
                    part,
                    side_ref[array, 0, pl.ds(corner, 1), :],
                    side_ref[array, 1, pl.ds(corner, 1), :],
                )
                target[2 * array + band] = part.astype(BF16)


def middle_body(rows, _, values, keys, *rest):
    middle = rows - 2
    pre_refs, grad_refs = rest[:middle], rest[middle : 2 * middle]
    x_side, c_side, inner_ref, gp_ref = rest[2 * middle :]
    band = pl.program_id(0)
    width, lifted = pre_refs[0].shape[1], pre_refs[0].shape[2]
    column = lax.broadcasted_iota(jnp.int32, (width, keys.shape[1]), 0).astype(F32)
    onehots = []
    for k in range(middle):
        local = keys[0:1, :] - ((band * rows + k + 1) * width).astype(F32)
        onehots.append(jnp.where(column == local, 1.0, 0.0).astype(BF16))
    found = dot(jnp.concatenate(onehots, axis=0), values[...])
    for k in range(middle):
        at = band * GROUP + k + 2
        inner, gp = gelu_pair(
            add_edges(
                pre_refs[k][0] + found[k * width : (k + 1) * width],
                x_side[0, pl.ds(at, 1), :],
                x_side[1, pl.ds(at, 1), :],
            ),
            add_edges(grad_refs[k][0], c_side[0, pl.ds(at, 1), :], c_side[1, pl.ds(at, 1), :]),
        )
        inner_ref[k] = inner
        gp_ref[k] = gp


def inside_body(
    rows, inner_b, gp_b, inner_m, gp_m, side_ref, k2_ref, k1t_ref, b2_ref, x_in, c_in, ana_out, ana_b,
    grad_out, grad_b, own_rows, ana_rows, grad_rows, sem,
):
    width, channels = own_rows.shape[2], own_rows.shape[3]
    middle = rows - 2
    loads = [
        pltpu.make_async_copy(x_in, own_rows.at[0], sem.at[0]),
        pltpu.make_async_copy(c_in, own_rows.at[1], sem.at[1]),
    ]
    for load in loads:
        load.start()
    stores = []
    for array, (border, inner, taps) in enumerate(
        ((inner_b, inner_m, k2_ref), (gp_b, gp_m, k1t_ref))
    ):
        way = 1 - 2 * array

        def plane(b, r):
            if r == 0 or r == rows - 1:
                return border[2 * b + r // (rows - 1)]
            return inner[middle * b + r - 1]

        for members, steps in row_groups(rows, way):
            lhs = jnp.concatenate(
                [
                    jnp.concatenate(
                        [plane(b, r + way * (1 - 2 * b) * dy) for dy in steps], axis=1
                    )
                    for b, r in members
                ],
                axis=0,
            )
            wide = dot(lhs, jnp.concatenate([row_taps(taps, dy + 1) for dy in steps], axis=0))
            if len(steps) == 3:
                loads[array].wait()
            for k, (b, r) in enumerate(members):
                i = b * rows + r
                at = b * GROUP + r + 1
                total = merge_shifts(wide[k * width : (k + 1) * width], array == 0)
                total = add_edges(
                    total + own_rows[array, i].astype(F32),
                    side_ref[array, 0, at : at + 1, :],
                    side_ref[array, 1, at : at + 1, :],
                )
                if array == 0:
                    total = total + b2_ref[...]
                if len(steps) == 2:
                    (ana_b, grad_b)[array][2 * b + r // (rows - 1)] = total
                    continue
                held_rows, out = ((ana_rows, ana_out), (grad_rows, grad_out))[array]
                held_rows[k] = total.astype(held_rows.dtype)
                store = pltpu.make_async_copy(held_rows.at[k], out.at[i], sem.at[2 + len(stores)])
                store.start()
                stores.append(store)
    for store in stores:
        store.wait()


def final_body(
    rows, ana_b, grad_b, own_ref, pair_ref, cross_ref, _, __, ana_out, grad_out, ana_rows, grad_rows, sem
):
    even, last = is_even(), is_last()
    stores = []
    for array, (acc, held_rows, out) in enumerate(
        ((ana_b, ana_rows, ana_out), (grad_b, grad_rows, grad_out))
    ):
        for j in range(4):
            band = j // 2
            plane = 2 * array + band
            if j % 2:
                add = jnp.where(even, pair_ref[plane], cross_ref[plane])
                add = jnp.where(last, own_ref[2 * array + 1 - band], add)
            else:
                add = jnp.where(even, cross_ref[plane], pair_ref[plane])
            held_rows[j] = (acc[j] + add.astype(F32)).astype(held_rows.dtype)
            store = pltpu.make_async_copy(
                held_rows.at[j], out.at[border_index(j, rows)], sem.at[len(stores)]
            )
            store.start()
            stores.append(store)
    for store in stores:
        store.wait()


def per_device(
    state,
    obs_values,
    obs_dest,
    obs_pixel,
    matching,
    kernel_one,
    bias_one,
    kernel_two,
    bias_two,
    cotangent,
):
    rows, width, channels = state.shape[3], state.shape[4], state.shape[5]
    lifted = kernel_one.shape[2]
    tiles, faces = lax.axis_size("tile"), lax.axis_size("face")
    devices = tiles * faces
    count = obs_values.shape[0]
    capacity = 2 * count // devices
    all_rows = 2 * rows
    middle = rows - 2
    chunk = 2 * capacity + PIXEL_ROWS
    x = state.reshape(all_rows, width, channels)
    c = cotangent.reshape(all_rows, width, channels)
    even = is_even()
    pairs = [(i, i ^ 1) for i in range(tiles)]
    crosses = [(i, i + 1 if i % 2 else i - 1) for i in range(1, tiles - 1)]
    strip = 16

    def ends(at):
        fields = [field.reshape(2, rows, width, channels) for field in (x, c)]
        picked = [
            jnp.concatenate(
                [
                    lax.dynamic_slice(field, (0, at, start, 0), (2, 1, strip, channels))[:, 0]
                    for start in (0, width - strip)
                ],
                axis=1,
            )
            for field in fields
        ]
        return jnp.concatenate(picked, axis=0)

    pair_ends = lax.ppermute(ends(jnp.where(even, rows - 1, 0)), "tile", pairs)
    cross_ends = lax.ppermute(ends(jnp.where(even, 0, rows - 1)), "tile", crosses)
    low_row = lambda field, at: lax.dynamic_index_in_dim(
        field.reshape(2, rows, width, channels), at, 1, keepdims=False
    )
    border_rows = lambda at: jnp.concatenate([low_row(x, at), low_row(c, at)], axis=0)
    pair_out = border_rows(jnp.where(even, rows - 1, 0))
    cross_out = border_rows(jnp.where(even, 0, rows - 1))
    cross_out, pair_ends, cross_ends = lax.optimization_barrier(
        (cross_out, pair_ends, cross_ends)
    )
    pair_rows = lax.ppermute(pair_out, "tile", pairs)
    cross_rows = lax.ppermute(cross_out, "tile", crosses)
    smem = pl.BlockSpec(memory_space=pltpu.SMEM)
    vmem = pl.BlockSpec(memory_space=pltpu.VMEM)
    hbm = pl.BlockSpec(memory_space=pl.ANY)

    def exchange(own):
        parts = [own]
        for k in range(1, faces):
            parts.append(
                lax.ppermute(own, "face", [((i + k) % faces, i) for i in range(faces)])
            )
        return parts

    packed = pl.pallas_call(
        functools.partial(pack_body, capacity),
        in_specs=[hbm] * 3,
        out_specs=hbm,
        out_shape=pltpu.HBM((devices, chunk, 128), BF16),
        scratch_shapes=[
            pltpu.VMEM((1, count), jnp.int32),
            pltpu.VMEM((1, count), jnp.int32),
            pltpu.VMEM((count, lifted), BF16),
            pltpu.VMEM((devices, chunk, 128), BF16),
            pltpu.SemaphoreType.DMA((3,)),
            pltpu.SemaphoreType.DMA((devices * capacity // 512,)),
        ],
        compiler_params=params(16),
        cost_estimate=cost(2 * devices * capacity * count * lifted, 2 << 20),
        name="pack",
    )(far(obs_dest.reshape(1, count)), far(obs_pixel.reshape(1, count)), far(obs_values))
    received = lax.all_to_all(packed, ("face", "tile"), 0, 0, tiled=True)

    b1 = bias_one.reshape(1, lifted)
    b2 = bias_two.reshape(1, channels)
    row_block = lambda n: pl.BlockSpec((1, width, n), lambda i: (i, 0, 0))
    edge_block = lambda n: pl.BlockSpec((1, width, n), lambda i: (border_row(i, rows), 0, 0))
    conv_flops = 2 * 9 * all_rows * width * channels * lifted
    plane = (4, width, channels)
    pre, grad_inner, k1t, k2t = pl.pallas_call(
        functools.partial(lift_body, rows),
        in_specs=[hbm] * 4 + [vmem],
        out_specs=[hbm] * 2 + [vmem] * 2,
        out_shape=[pltpu.HBM((2 * middle, width, lifted), F32)] * 2
        + [pltpu.HBM(kernel_two.shape, BF16), pltpu.HBM(kernel_one.shape, BF16)],
        scratch_shapes=[
            pltpu.VMEM(x.shape, BF16),
            pltpu.VMEM(c.shape, BF16),
            pltpu.VMEM(kernel_one.shape, BF16),
            pltpu.VMEM(kernel_two.shape, BF16),
            pltpu.VMEM((2, all_rows, width, 3 * channels), BF16),
            pltpu.VMEM((2, 2 * middle, width, lifted), F32),
            pltpu.SemaphoreType.DMA((4 + 4 * middle,)),
        ],
        compiler_params=params(40),
        cost_estimate=cost(conv_flops, 8 << 20),
        name="lift",
    )(far(x), far(c), far(kernel_one), far(kernel_two), b1)
    pre, grad_inner = far(pre), far(grad_inner)
    low = lambda n: pl.BlockSpec((n, strip, channels), lambda *_: (0, 0, 0))
    high = lambda n, at: pl.BlockSpec((n, strip, channels), lambda *_: (0, at, 0))
    tail = width // strip - 1
    edge_shape = (2, 2, 2 * GROUP, channels)
    edges = pl.pallas_call(
        functools.partial(edge_body, rows),
        grid=(1,),
        in_specs=[low(all_rows), high(all_rows, tail)] * 2 + [low(4), high(4, 1)] * 2,
        out_specs=fixed(edge_shape),
        out_shape=jax.ShapeDtypeStruct(edge_shape, F32),
        compiler_params=params(8),
        cost_estimate=cost(0, 1 << 18),
        name="edges",
    )(x, x, c, c, pair_ends, pair_ends, cross_ends, cross_ends)
    parts = exchange(edges)

    side_in = (2, 2 * GROUP, lifted)
    end = width // GROUP - 1
    edge_strip = lambda at: pl.BlockSpec((2 * middle, GROUP, lifted), lambda *_: (0, at, 0))
    rim_shape = (2, 4 * GROUP, lifted)
    taps_shape = (2, 2, 3, channels, lifted)
    rim_base, side_taps = pl.pallas_call(
        functools.partial(rim_in_body, rows),
        grid=(1,),
        in_specs=[smem, hbm, fixed(b1.shape), hbm]
        + [edge_strip(0), edge_strip(end)] * 2
        + [low(all_rows), high(all_rows, tail)] * 2
        + [low(4), high(4, 1)] * 2,
        out_specs=[fixed(rim_shape), fixed(taps_shape)],
        out_shape=[jax.ShapeDtypeStruct(rim_shape, F32), jax.ShapeDtypeStruct(taps_shape, BF16)],
        scratch_shapes=[
            pltpu.VMEM(kernel_one.shape, BF16),
            pltpu.VMEM(k2t.shape, BF16),
            pltpu.SemaphoreType.DMA((2,)),
        ],
        compiler_params=params(8),
        cost_estimate=cost(0, 2 << 20),
        name="rim_in",
    )(
        matching, far(kernel_one), b1, far(k2t), pre, pre, grad_inner, grad_inner, x, x, c, c, pair_ends,
        pair_ends, cross_ends, cross_ends,
    )
    x_side, c_side, rim_sums = pl.pallas_call(
        functools.partial(side_in_body, faces),
        in_specs=[smem] + [vmem] * (2 + faces),
        out_specs=[vmem] * 3,
        out_shape=[
            jax.ShapeDtypeStruct(side_in, F32),
            jax.ShapeDtypeStruct(side_in, F32),
            jax.ShapeDtypeStruct(rim_shape, F32),
        ],
        compiler_params=params(8),
        cost_estimate=cost(0, 1 << 20),
        name="sides_in",
    )(matching, side_taps, rim_base, *parts)

    side_two = (2, 2, 2 * GROUP, lifted)
    slots = devices * capacity
    onehot_flops = 2 * width * slots * lifted
    other_block = pl.BlockSpec(
        (1, width, channels), lambda j: ((1 - j // 2) * rows + rows - 1, 0, 0)
    )
    edges_two, values, keys = pl.pallas_call(
        functools.partial(rim_body, rows, width, capacity),
        in_specs=[vmem] * 2,
        out_specs=[vmem] * 3,
        out_shape=[
            jax.ShapeDtypeStruct(side_two, F32),
            hold((slots, lifted), BF16),
            hold((PIXEL_ROWS, slots), F32),
        ],
        compiler_params=params(8),
        cost_estimate=cost(0, 3 << 20),
        name="rim",
    )(received, rim_sums)
    values, keys = held(values), held(keys)
    parts_two = exchange(edges_two)

    border_shape = hold((4, width, lifted), BF16)
    inner_b, gp_b = pl.pallas_call(
        functools.partial(border_body, rows),
        in_specs=[vmem] * 5 + [hbm] * 6,
        out_specs=[vmem] * 2,
        out_shape=[border_shape] * 2,
        scratch_shapes=[
            pltpu.VMEM(x.shape, BF16),
            pltpu.VMEM(c.shape, BF16),
            pltpu.VMEM((2, 4, width, channels), BF16),
            pltpu.VMEM(kernel_one.shape, BF16),
            pltpu.VMEM(k2t.shape, BF16),
            pltpu.SemaphoreType.DMA((12,)),
        ],
        compiler_params=params(32),
        cost_estimate=cost(4 * onehot_flops + conv_flops // 6, 10 << 20),
        name="border",
    )(
        values, keys, x_side, c_side, b1, far(pair_rows), far(cross_rows), far(x), far(c),
        far(kernel_one), far(k2t),
    )
    inner_b, gp_b = held(inner_b), held(gp_b)

    side_out = (2, 2, 2 * GROUP, channels)
    to_pair, to_cross, sides = pl.pallas_call(
        functools.partial(send_body, rows, faces),
        in_specs=[smem] + [vmem] * (4 + faces),
        out_specs=[vmem] * 3,
        out_shape=[
            jax.ShapeDtypeStruct(plane, BF16),
            jax.ShapeDtypeStruct(plane, BF16),
            jax.ShapeDtypeStruct(side_out, F32),
        ],
        compiler_params=params(16),
        cost_estimate=cost(conv_flops // 6, 4 << 20),
        name="send",
    )(matching, inner_b, gp_b, kernel_two, k1t, *parts_two)
    from_pair = lax.ppermute(to_pair, "tile", pairs)
    from_cross = lax.ppermute(to_cross, "tile", crosses)

    middle_block = lambda k: pl.BlockSpec((1, width, lifted), lambda i: (i * middle + k, 0, 0))
    inner_m, gp_m = pl.pallas_call(
        functools.partial(middle_body, rows),
        grid=(2,),
        in_specs=[hbm, fixed(values.shape), fixed(keys.shape)]
        + [middle_block(k) for k in range(middle)] * 2
        + [fixed(side_in)] * 2,
        out_specs=[pl.BlockSpec((middle, width, lifted), lambda i: (i, 0, 0))] * 2,
        out_shape=[hold((2 * middle, width, lifted), BF16)] * 2,
        compiler_params=params(),
        cost_estimate=cost(2 * middle * onehot_flops, 10 << 20),
        name="middle",
    )(to_cross, values, keys, *[pre] * middle, *[grad_inner] * middle, x_side, c_side)
    inner_m, gp_m = held(inner_m), held(gp_m)

    analysis, ana_b, grad_state, grad_b = pl.pallas_call(
        functools.partial(inside_body, rows),
        in_specs=[vmem] * 8 + [hbm] * 2,
        out_specs=[hbm, vmem, hbm, vmem],
        out_shape=[
            pltpu.HBM((all_rows, width, channels), BF16),
            hold(plane, F32),
            pltpu.HBM((all_rows, width, channels), F32),
            hold(plane, F32),
        ],
        scratch_shapes=[
            pltpu.VMEM((2, all_rows, width, channels), BF16),
            pltpu.VMEM((2 * middle, width, channels), BF16),
            pltpu.VMEM((2 * middle, width, channels), F32),
            pltpu.SemaphoreType.DMA((2 + 4 * middle,)),
        ],
        compiler_params=params(),
        cost_estimate=cost(2 * conv_flops, 14 << 20),
        name="inside",
    )(inner_b, gp_b, inner_m, gp_m, sides, kernel_two, k1t, b2, far(x), far(c))
    ana_b, grad_b = held(ana_b), held(grad_b)

    analysis, grad_state = pl.pallas_call(
        functools.partial(final_body, rows),
        in_specs=[vmem] * 5 + [hbm] * 2,
        out_specs=[hbm] * 2,
        out_shape=[
            pltpu.HBM((all_rows, width, channels), BF16),
            pltpu.HBM((all_rows, width, channels), F32),
        ],
        scratch_shapes=[
            pltpu.VMEM(plane, BF16),
            pltpu.VMEM(plane, F32),
            pltpu.SemaphoreType.DMA((8,)),
        ],
        input_output_aliases={5: 0, 6: 1},
        compiler_params=params(16),
        cost_estimate=cost(0, 6 << 20),
        name="final",
    )(ana_b, grad_b, to_cross, from_pair, from_cross, far(analysis), far(grad_state))
    return analysis.reshape(state.shape), grad_state.reshape(cotangent.shape)


def solution(mesh):
    return jax.shard_map(
        per_device,
        mesh=mesh,
        in_specs=(
            P("face", "tile", None, None, None, None),
            P(("face", "tile"), None),
            P(("face", "tile"), None),
            P(("face", "tile")),
            P(),
            P(),
            P(),
            P(),
            P(),
            P("face", "tile", None, None, None, None),
        ),
        out_specs=(
            P("face", "tile", None, None, None, None),
            P("face", "tile", None, None, None, None),
        ),
        check_vma=False,
    )
```

```python
import functools
import math

import jax
import jax.numpy as jnp
from jax import lax
from jax.experimental import pallas as pl
from jax.experimental.pallas import tpu as pltpu
from jax.sharding import PartitionSpec as P

F32 = jnp.float32
BF16 = jnp.bfloat16
GROUP = 8
HIGH = 64
PIXEL_ROWS = 8
ROOT = math.sqrt(2.0 / math.pi)
CUBIC = 0.044715


def params(mib=24):
    return pltpu.CompilerParams(vmem_limit_bytes=mib << 20)


def cost(flops, nbytes):
    return pl.CostEstimate(flops=int(flops), bytes_accessed=int(nbytes), transcendentals=0)


def hold(shape, kind):
    return pltpu.VMEM(shape, kind)


def held(array):
    return pltpu.with_memory_space_constraint(array, pltpu.VMEM)


def far(array):
    return pltpu.with_memory_space_constraint(array, pltpu.HBM)


def fixed(shape):
    return pl.BlockSpec(shape, lambda *_: (0,) * len(shape))


def dot(a, b):
    return jnp.dot(a, b, preferred_element_type=F32)


def matched(matching_ref, side, faces):
    face = lax.axis_index("face")
    partner = matching_ref[face, side, 0]
    return lax.rem(partner - face + faces, faces), matching_ref[face, side, 1], matching_ref[face, side, 2]


def is_even():
    return lax.rem(lax.axis_index("tile"), 2) == 0


def is_last():
    return lax.axis_index("tile") == lax.axis_size("tile") - 1


def partner_rows(part_refs, array, hop, their_side, flipped):
    rows = None
    for k, ref in enumerate(part_refs):
        mine = jnp.where(their_side == 1, ref[array, 1], ref[array, 0])
        rows = mine if rows is None else jnp.where(hop == k, mine, rows)
    swapped = jnp.concatenate([rows[GROUP:], rows[:GROUP]], axis=0)
    return jnp.where(flipped == 1, swapped, rows)


def rolled_rows(rows, step):
    first, second = rows[:GROUP], rows[GROUP:]
    if step:
        first = pltpu.roll(first, (-step) % GROUP, 0)
        second = pltpu.roll(second, step % GROUP, 0)
    return jnp.concatenate([first, second], axis=0).astype(BF16)


def side_forward(rows, side, taps_ref):
    lhs = jnp.concatenate([rolled_rows(rows, dy) for dy in (-1, 0, 1)], axis=1)
    taps = jnp.concatenate([taps_ref[3 * row + 2 * side] for row in range(3)], axis=0)
    return dot(lhs, taps)


def side_adjoint(rows, their_side, flipped, taps_ref):
    lhs = jnp.concatenate([rolled_rows(rows, -dy) for dy in (-1, 0, 1)], axis=1)
    order = [jnp.where(flipped == 1, 2 - row, row) for row in range(3)]
    taps = jnp.concatenate([taps_ref[3 * row + 2 * their_side] for row in order], axis=0)
    return dot(lhs, taps)


def shift_columns(values, step):
    count = values.shape[0]
    at = lax.broadcasted_iota(jnp.int32, values.shape, 0)
    moved = pltpu.roll(values, (-step) % count, 0)
    edge = count - 1 if step == 1 else 0
    return jnp.where(at == edge, 0.0, moved)


def spread_columns(row, order):
    wide = row.astype(F32)
    return jnp.concatenate(
        [row if s == 0 else shift_columns(wide, s).astype(BF16) for s in order], axis=1
    )


def add_edges(values, left, right):
    count = values.shape[0]
    at = lax.broadcasted_iota(jnp.int32, (GROUP, values.shape[1]), 0)
    first = values[:GROUP] + jnp.where(at == 0, left, 0.0)
    tail = values[count - GROUP :] + jnp.where(at == GROUP - 1, right, 0.0)
    return jnp.concatenate([first, values[GROUP : count - GROUP], tail], axis=0)


def pack_body(
    capacity, dest_in, pixel_in, values_in, out_hbm, dest_ref, pixel_ref, values_ref, out_ref, in_sem,
    out_sem,
):
    count = values_ref.shape[0]
    devices = out_ref.shape[0]
    block = 128
    loads = [
        pltpu.make_async_copy(source, target, in_sem.at[k])
        for k, (source, target) in enumerate(
            ((dest_in, dest_ref), (pixel_in, pixel_ref), (values_in, values_ref))
        )
    ]
    for load in loads:
        load.start()
    loads[0].wait()
    loads[1].wait()
    dest_row = dest_ref[...].astype(F32)
    pixel_row = pixel_ref[...]
    eye = lax.broadcasted_iota(jnp.int32, (block, block), 0) == lax.broadcasted_iota(
        jnp.int32, (block, block), 1
    )

    def column(row, start):
        piece = row[:, start : start + block]
        return jnp.sum(jnp.where(eye, piece, 0.0), axis=1, keepdims=True)

    high_row = lax.shift_right_logical(pixel_row, 6).astype(F32) + 1.0
    low_row = (pixel_row & (HIGH - 1)).astype(F32)
    own = lax.broadcasted_iota(jnp.int32, (block, count), 0)
    other = lax.broadcasted_iota(jnp.int32, (block, count), 1)
    lane = lax.broadcasted_iota(jnp.int32, (block, 128), 1)
    lane_rank = (lane & (HIGH - 1)).astype(F32)
    rank_row = jnp.zeros((1, count), F32)
    coded = []
    for start in range(0, count, block):
        same = column(dest_row, start) == dest_row
        later = (own + start) < other
        rank_row = rank_row + jnp.sum(
            jnp.where(same & later, 1.0, 0.0), axis=0, keepdims=True
        )
    for start in range(0, count, block):
        code = jnp.where(lane < HIGH, column(high_row, start), column(low_row, start))
        coded.append(jnp.where(column(rank_row, start) == lane_rank, code, 0.0).astype(BF16))
    to_device = (
        lax.broadcasted_iota(jnp.int32, (devices, count), 0).astype(F32) == dest_row
    )
    pixels = dot(
        jnp.where(to_device, 1.0, 0.0).astype(BF16), jnp.concatenate(coded, axis=0)
    )
    out_ref[:, 2 * capacity :, :] = jnp.broadcast_to(
        pixels[:, None, :], (devices, PIXEL_ROWS, 128)
    ).astype(BF16)
    slot_row = dest_row * capacity + rank_row
    slots = 512
    per_block = slots // capacity
    loads[2].wait()
    values = values_ref[...]
    stores = []
    slot_at = lax.broadcasted_iota(jnp.int32, (slots, count), 0).astype(F32)
    for start in range(0, devices * capacity, slots):
        onehot = jnp.where(slot_at == slot_row - start, 1.0, 0.0).astype(BF16)
        rows = dot(onehot, values).astype(BF16)
        first = start // capacity
        for half in range(2):
            out_ref[first : first + per_block, half * capacity : (half + 1) * capacity, :] = (
                rows[:, half * 128 : (half + 1) * 128].reshape(per_block, capacity, 128)
            )
        store = pltpu.make_async_copy(
            out_ref.at[first : first + per_block],
            out_hbm.at[first : first + per_block],
            out_sem.at[len(stores)],
        )
        store.start()
        stores.append(store)
    for store in stores:
        store.wait()


def end_rows(rows, x_ends, c_ends, pair_ends, cross_ends):
    prev, after = [], []
    even = is_even()
    for side in range(2):
        pair, cross = pair_ends[side], cross_ends[side]
        prev.append(jnp.where(even, cross, pair))
        after.append(jnp.where(even, pair, cross))
    outside = {}
    for array, own in enumerate((x_ends, c_ends)):
        for side in range(2):
            for band in range(2):
                plane = 2 * array + band
                fold = own[side][(1 - band) * rows + rows - 1]
                outside[array, side, 2 * band] = prev[side][plane]
                outside[array, side, 2 * band + 1] = jnp.where(is_last(), fold, after[side][plane])
    return outside


def edge_body(rows, x_lo, x_hi, c_lo, c_hi, a_lo, a_hi, b_lo, b_hi, out_ref):
    out_ref[...] = jnp.zeros_like(out_ref)
    wide = lambda refs: [ref[...].astype(F32) for ref in refs]
    x_ends, c_ends = wide((x_lo, x_hi)), wide((c_lo, c_hi))
    outside = end_rows(rows, x_ends, c_ends, wide((a_lo, a_hi)), wide((b_lo, b_hi)))
    for array, own in enumerate((x_ends, c_ends)):
        for side in range(2):
            at = 0 if side == 0 else own[side].shape[1] - 1
            for band in range(2):
                base = band * GROUP
                out_ref[array, side, base, :] = outside[array, side, 2 * band][at]
                for r in range(rows):
                    out_ref[array, side, base + 1 + r, :] = own[side][band * rows + r, at]
                out_ref[array, side, base + 1 + rows, :] = outside[array, side, 2 * band + 1][at]


def row_groups(rows, way):
    first, last = ((0, 0), (1, rows - 1)), ((0, rows - 1), (1, 0))
    if way < 0:
        first, last = last, first
    inner = tuple((b, r) for b in range(2) for r in range(1, rows - 1))
    return ((inner, (-1, 0, 1)), (first, (0, 1)), (last, (-1, 0)))


def border_index(j, rows):
    return (j // 2) * rows + (j % 2) * (rows - 1)


def border_row(j, rows):
    return (j // 2) * rows + lax.rem(j, 2) * (rows - 1)


def lift_body(
    rows, x_in, c_in, k1_in, k2_in, b1_ref, pre_out, grad_out, k1t_ref, k2t_ref, x_ref, c_ref, k1_ref,
    k2_ref, cat, held_rows, sem,
):
    width, channels = x_ref.shape[1], x_ref.shape[2]
    lifted = k1_ref.shape[2]
    used = [0]

    def slot():
        used[0] += 1
        return sem.at[used[0] - 1]

    loads = [
        pltpu.make_async_copy(source, target, slot())
        for source, target in ((x_in, x_ref), (k1_in, k1_ref), (k2_in, k2_ref), (c_in, c_ref))
    ]
    for load in loads:
        load.start()
    stores = []
    for array, (source, weights, order, out) in enumerate(
        ((x_ref, k1_ref, (-1, 0, 1), pre_out), (c_ref, k2t_ref, (1, 0, -1), grad_out))
    ):
        way = 1 - 2 * array
        loads[2 * array].wait()
        loads[2 * array + 1].wait()
        if array == 1:
            for t in range(k2_ref.shape[0]):
                k2t_ref[t] = k2_ref[t].astype(F32).T.astype(BF16)
        for i in range(2 * rows):
            cat[array, i] = spread_columns(source[i], order)
        inner, first, last = row_groups(rows, way)
        half = len(inner[0]) // 2
        groups = ((inner[0][:half], inner[1]), (inner[0][half:], inner[1]), first, last)
        for members, steps in groups:
            lhs = jnp.concatenate(
                [
                    jnp.concatenate(
                        [cat[array, b * rows + r + way * (1 - 2 * b) * dy] for dy in steps], axis=1
                    )
                    for b, r in members
                ],
                axis=0,
            )
            taps = weights[3 * (steps[0] + 1) : 3 * (steps[-1] + 2)]
            total = dot(lhs, taps.reshape(3 * len(steps) * channels, lifted))
            if array == 0:
                total = total + b1_ref[...]
            for k, (b, r) in enumerate(members):
                i = b * rows + r
                held_rows[array, i] = total[k * width : (k + 1) * width]
                store = pltpu.make_async_copy(held_rows.at[array, i], out.at[i], slot())
                store.start()
                stores.append(store)
    for t in range(k1_ref.shape[0]):
        k1t_ref[t] = k1_ref[t].astype(F32).T.astype(BF16)
    for store in stores:
        store.wait()


def row_onehot(keys, row, width):
    column = lax.broadcasted_iota(jnp.int32, (width, keys.shape[1]), 0).astype(F32)
    return jnp.where(column == keys[0:1, :] - float(row * width), 1.0, 0.0).astype(BF16)


def rim_in_body(
    rows, matching_ref, k1_in, k2t_in, pre_lo, pre_hi, grad_lo, grad_hi, x_lo, x_hi, c_lo, c_hi,
    a_lo, a_hi, b_lo, b_hi, base_ref, taps_ref, k1_ref, k2t_ref, sem,
):
    loads = [
        pltpu.make_async_copy(k1_in, k1_ref, sem.at[0]),
        pltpu.make_async_copy(k2t_in, k2t_ref, sem.at[1]),
    ]
    for load in loads:
        load.start()
    for load in loads:
        load.wait()
    face = lax.axis_index("face")
    for side in range(2):
        their_side, flipped = matching_ref[face, side, 1], matching_ref[face, side, 2]
        for row in range(3):
            taps_ref[0, side, row] = k1_ref[3 * row + 2 * side]
            turned = jnp.where(flipped == 1, 2 - row, row)
            taps_ref[1, side, row] = k2t_ref[3 * turned + 2 * their_side]
    whole = lambda refs: [ref[...] for ref in refs]
    x_ends, c_ends = whole((x_lo, x_hi)), whole((c_lo, c_hi))
    outside = end_rows(rows, x_ends, c_ends, whole((a_lo, a_hi)), whole((b_lo, b_hi)))
    channels, lifted = k1_ref.shape[1], k1_ref.shape[2]
    base_ref[...] = jnp.zeros_like(base_ref)
    for array, (strips, weights, order) in enumerate(
        (((pre_lo, pre_hi), k1_ref, (-1, 0, 1)), ((grad_lo, grad_hi), k2t_ref, (1, 0, -1)))
    ):
        for side in range(2):
            spot = 0 if side == 0 else GROUP - 1
            for b in range(2):
                for r in range(rows):
                    at = 2 * GROUP * side + GROUP * b + r + 1
                    base_ref[array, at : at + 1, :] = strips[side][
                        b * rows + r, spot : spot + 1, :
                    ]
        for pair in ((0, 3), (1, 2)):
            spots = [(side, j) for side in range(2) for j in pair]
            lhs = [spread_columns(outside[array, side, j], order) for side, j in spots]
            row = 0 if (pair[0] == 0) == (array == 0) else 6
            found = dot(
                jnp.concatenate(lhs, axis=0), weights[row : row + 3].reshape(3 * channels, lifted)
            )
            strip = found.shape[0] // len(spots)
            for k, (side, j) in enumerate(spots):
                at = 2 * GROUP * side + GROUP * (j // 2) + 1 + (rows - 1) * (j % 2)
                spot = k * strip + (0 if side == 0 else strip - 1)
                base_ref[array, at : at + 1, :] += found[spot : spot + 1]


def rim_body(rows, faces, matching_ref, taps_ref, base_ref, found_ref, *rest):
    parts = rest[:faces]
    x_side, c_side, edge_ref = rest[faces:]
    taps = taps_ref[...].reshape(2, 2, 3 * taps_ref.shape[3], taps_ref.shape[4])
    for side in range(2):
        hop, their_side, flipped = matched(matching_ref, side, faces)
        for array, out in enumerate((x_side, c_side)):
            near = partner_rows(parts, array, hop, their_side, flipped)
            way = 1 - 2 * array
            lhs = jnp.concatenate([rolled_rows(near, way * dy) for dy in (-1, 0, 1)], axis=1)
            out[side] = dot(lhs, taps[array, side])
    e = lax.broadcasted_iota(jnp.int32, (4 * GROUP, 1), 0) & (GROUP - 1)
    inside = (e >= 1) & (e <= rows)
    shape = base_ref.shape[1:]
    v = base_ref[0] + x_side[...].reshape(shape) + found_ref[...]
    inner, gp = gelu_pair(v, base_ref[1] + c_side[...].reshape(shape))
    edge_ref[0] = jnp.where(inside, inner.astype(F32), 0.0).reshape(edge_ref.shape[1:])
    edge_ref[1] = jnp.where(inside, gp.astype(F32), 0.0).reshape(edge_ref.shape[1:])


def gelu_pair(v, grad):
    square = v * v
    t = jnp.tanh(v * (ROOT + (ROOT * CUBIC) * square))
    half = 0.5 + 0.5 * t
    slope = half + (0.5 * v) * (1.0 - t * t) * (ROOT + (3.0 * ROOT * CUBIC) * square)
    return (v * half).astype(BF16), (grad * slope).astype(BF16)


def unpack_received(capacity, recv_ref, values, keys):
    devices = recv_ref.shape[0]
    slots = devices * capacity
    per_lane = 128 // capacity
    for half in range(2):
        values[:, half * 128 : (half + 1) * 128] = recv_ref[
            :, half * capacity : (half + 1) * capacity, :
        ].reshape(slots, 128)
    owner = lax.broadcasted_iota(jnp.int32, (PIXEL_ROWS, 128), 1) // capacity
    for start in range(0, devices, per_lane):
        key = jnp.zeros((PIXEL_ROWS, 128), F32)
        for k in range(per_lane):
            code = recv_ref[start + k, 2 * capacity :, :].astype(F32)
            mine = (code - 1.0) * HIGH + pltpu.roll(code, HIGH, 1)
            if k:
                mine = pltpu.roll(mine, k * capacity, 1)
            key = jnp.where(owner == k, mine, key)
        keys[:, start * capacity : start * capacity + 128] = key


def row_taps(taps_ref, row):
    return jnp.concatenate([taps_ref[3 * row + dx] for dx in range(3)], axis=1)


def merge_shifts(wide, forward):
    channels = wide.shape[1] // 3
    left, mid, right = (wide[:, k * channels : (k + 1) * channels] for k in range(3))
    step = -1 if forward else 1
    return mid + shift_columns(left, step) + shift_columns(right, -step)


def found_body(
    rows, capacity, recv_in, pre_in, grad_in, k1_in, k2t_in, values, keys, pre_b, grad_b, found_b, rim_ref,
    taps, recv_ref, sem,
):
    width = pre_b.shape[1]
    loads = [pltpu.make_async_copy(recv_in, recv_ref, sem.at[0])]
    for j in range(4):
        row = border_index(j, rows)
        loads.append(pltpu.make_async_copy(pre_in.at[row], pre_b.at[j], sem.at[1 + j]))
    for j in range(4):
        row = border_index(j, rows)
        loads.append(pltpu.make_async_copy(grad_in.at[row], grad_b.at[j], sem.at[5 + j]))
    for array, source in enumerate((k1_in, k2t_in)):
        for k in range(2):
            loads.append(
                pltpu.make_async_copy(
                    source.at[6 * k : 6 * k + 3], taps.at[array, k], sem.at[9 + 2 * array + k]
                )
            )
    for load in loads:
        load.start()
    loads[0].wait()
    unpack_received(capacity, recv_ref, values, keys)
    at = lax.broadcasted_iota(jnp.int32, (4 * GROUP, 1), 0)
    e = at & (GROUP - 1)
    b = (at // GROUP) & 1
    side = at // (2 * GROUP)
    inside = (e >= 1) & (e <= rows)
    pixel = (b * rows + e - 1) * width + side * (width - 1)
    wanted = jnp.where(inside, pixel, -1).astype(F32)
    onehot = jnp.where(keys[0:1, :] == wanted, 1.0, 0.0).astype(BF16)
    rim_ref[...] = dot(onehot, values[...])
    for half in range(2):
        members = (2 * half, 2 * half + 1)
        found = dot(
            jnp.concatenate(
                [row_onehot(keys, border_index(j, rows), width) for j in members], axis=0
            ),
            values[...],
        )
        for k, j in enumerate(members):
            found_b[j] = found[k * width : (k + 1) * width]
    for load in loads[1:]:
        load.wait()


def border_body(
    rows, pre_b, grad_b, found_b, taps, x_side, c_side, a_in, b_in, x_in, c_in, inner_ref, gp_ref, outside,
    sem,
):
    width, lifted = inner_ref.shape[1], inner_ref.shape[2]
    channels = outside.shape[3]
    even, last = is_even(), is_last()
    waits = [[], []]
    used = [0]

    def load(array, target, *sources):
        slot = sem.at[used[0]]
        used[0] += 1
        for condition, source in sources:
            copy = pltpu.make_async_copy(source, target, slot)
            pl.when(condition)(copy.start)
        waits[array].append(copy)

    for array, source in enumerate((x_in, c_in)):
        for j in range(4):
            band = j // 2
            plane = 2 * array + band
            if j % 2 == 0:
                choices = ((even, b_in.at[plane]), (jnp.logical_not(even), a_in.at[plane]))
            else:
                fold = source.at[(1 - band) * rows + rows - 1]
                middle = jnp.logical_not(even) & jnp.logical_not(last)
                choices = ((last, fold), (even, a_in.at[plane]), (middle, b_in.at[plane]))
            load(array, outside.at[array, j], *choices)

    for copy in waits[0] + waits[1]:
        copy.wait()
    for pair in ((0, 3), (1, 2)):
        totals = []
        for array, order in enumerate(((-1, 0, 1), (1, 0, -1))):
            lhs = [spread_columns(outside[array, j], order) for j in pair]
            tap = taps[array, 0 if (pair[0] == 0) == (array == 0) else 1]
            totals.append(dot(jnp.concatenate(lhs, axis=0), tap.reshape(3 * channels, lifted)))
        for k, j in enumerate(pair):
            at = GROUP * (j // 2) + 1 + (rows - 1) * (j % 2)
            piece = slice(k * width, (k + 1) * width)
            inner, gp = gelu_pair(
                add_edges(
                    totals[0][piece] + (pre_b[j] + found_b[j]),
                    x_side[0, at : at + 1, :],
                    x_side[1, at : at + 1, :],
                ),
                add_edges(
                    totals[1][piece] + grad_b[j], c_side[0, at : at + 1, :], c_side[1, at : at + 1, :]
                ),
            )
            inner_ref[j] = inner
            gp_ref[j] = gp


def send_body(rows, faces, matching_ref, inner_ref, gp_ref, k2_ref, k1t_ref, *rest):
    parts = rest[:faces]
    pair_ref, cross_ref, side_ref = rest[faces:]
    even = is_even()
    width = inner_ref.shape[1]
    for side in range(2):
        hop, their_side, flipped = matched(matching_ref, side, faces)
        near = partner_rows(parts, 0, hop, their_side, flipped)
        side_ref[0, side] = side_forward(near, side, k2_ref)
        near = partner_rows(parts, 1, hop, their_side, flipped)
        side_ref[1, side] = side_adjoint(near, their_side, flipped, k1t_ref)
    up = jnp.where(even, 1, 0)
    for array, (source, taps) in enumerate(((inner_ref, k2_ref), (gp_ref, k1t_ref))):
        for group in range(2):
            members = ((pair_ref, group, up), (cross_ref, 1 - group, 1 - up))
            tap = jnp.where((group == up) == (array == 0), 2, 0)
            lhs = jnp.concatenate([source[2 * band + bottom] for _, band, bottom in members], axis=0)
            wide = dot(lhs, row_taps(taps, tap))
            for k, (target, band, bottom) in enumerate(members):
                part = merge_shifts(wide[k * width : (k + 1) * width], array == 0)
                corner = GROUP * band + (rows + 1) * bottom
                part = add_edges(
                    part,
                    side_ref[array, 0, pl.ds(corner, 1), :],
                    side_ref[array, 1, pl.ds(corner, 1), :],
                )
                target[2 * array + band] = part.astype(BF16)


def middle_body(
    rows, _, values, keys, pre_in, grad_in, x_side, c_side, inner_ref, gp_ref, base, sem
):
    middle = rows - 2
    width = base.shape[2]
    members = [(b, r) for b in range(2) for r in range(1, rows - 1)]
    loads = []
    for k in range(len(members)):
        for array, source in enumerate((pre_in, grad_in)):
            row = members[k][0] * rows + members[k][1]
            load = pltpu.make_async_copy(source.at[row], base.at[array, k], sem.at[2 * k + array])
            load.start()
            loads.append(load)
    found = dot(
        jnp.concatenate([row_onehot(keys, b * rows + r, width) for b, r in members], axis=0),
        values[...],
    )
    for k, (b, r) in enumerate(members):
        at = b * GROUP + r + 1
        loads[2 * k].wait()
        loads[2 * k + 1].wait()
        inner, gp = gelu_pair(
            add_edges(
                base[0, k] + found[k * width : (k + 1) * width],
                x_side[0, at : at + 1, :],
                x_side[1, at : at + 1, :],
            ),
            add_edges(base[1, k], c_side[0, at : at + 1, :], c_side[1, at : at + 1, :]),
        )
        inner_ref[k] = inner
        gp_ref[k] = gp


def inside_body(
    rows, inner_b, gp_b, inner_m, gp_m, side_ref, k2_ref, k1t_ref, b2_ref, x_in, c_in, ana_out, ana_b,
    grad_out, grad_b, own_rows, ana_rows, grad_rows, sem,
):
    width, channels = own_rows.shape[2], own_rows.shape[3]
    middle = rows - 2
    loads = [
        pltpu.make_async_copy(x_in, own_rows.at[0], sem.at[0]),
        pltpu.make_async_copy(c_in, own_rows.at[1], sem.at[1]),
    ]
    for load in loads:
        load.start()
    stores = []
    for array, (border, inner, taps) in enumerate(
        ((inner_b, inner_m, k2_ref), (gp_b, gp_m, k1t_ref))
    ):
        way = 1 - 2 * array

        def plane(b, r):
            if r == 0 or r == rows - 1:
                return border[2 * b + r // (rows - 1)]
            return inner[middle * b + r - 1]

        for members, steps in row_groups(rows, way):
            lhs = jnp.concatenate(
                [
                    jnp.concatenate(
                        [plane(b, r + way * (1 - 2 * b) * dy) for dy in steps], axis=1
                    )
                    for b, r in members
                ],
                axis=0,
            )
            wide = dot(lhs, jnp.concatenate([row_taps(taps, dy + 1) for dy in steps], axis=0))
            if len(steps) == 3:
                loads[array].wait()
            for k, (b, r) in enumerate(members):
                i = b * rows + r
                at = b * GROUP + r + 1
                total = merge_shifts(wide[k * width : (k + 1) * width], array == 0)
                total = add_edges(
                    total + own_rows[array, i].astype(F32),
                    side_ref[array, 0, at : at + 1, :],
                    side_ref[array, 1, at : at + 1, :],
                )
                if array == 0:
                    total = total + b2_ref[...]
                if len(steps) == 2:
                    (ana_b, grad_b)[array][2 * b + r // (rows - 1)] = total
                    continue
                held_rows, out = ((ana_rows, ana_out), (grad_rows, grad_out))[array]
                held_rows[k] = total.astype(held_rows.dtype)
                store = pltpu.make_async_copy(held_rows.at[k], out.at[i], sem.at[2 + len(stores)])
                store.start()
                stores.append(store)
    for store in stores:
        store.wait()


def final_body(
    rows, ana_b, grad_b, own_ref, pair_ref, cross_ref, _, __, ana_out, grad_out, ana_rows, grad_rows, sem
):
    even, last = is_even(), is_last()
    stores = []
    for array, (acc, held_rows, out) in enumerate(
        ((ana_b, ana_rows, ana_out), (grad_b, grad_rows, grad_out))
    ):
        for j in range(4):
            band = j // 2
            plane = 2 * array + band
            if j % 2:
                add = jnp.where(even, pair_ref[plane], cross_ref[plane])
                add = jnp.where(last, own_ref[2 * array + 1 - band], add)
            else:
                add = jnp.where(even, cross_ref[plane], pair_ref[plane])
            held_rows[j] = (acc[j] + add.astype(F32)).astype(held_rows.dtype)
            store = pltpu.make_async_copy(
                held_rows.at[j], out.at[border_index(j, rows)], sem.at[len(stores)]
            )
            store.start()
            stores.append(store)
    for store in stores:
        store.wait()


def per_device(
    state,
    obs_values,
    obs_dest,
    obs_pixel,
    matching,
    kernel_one,
    bias_one,
    kernel_two,
    bias_two,
    cotangent,
):
    rows, width, channels = state.shape[3], state.shape[4], state.shape[5]
    lifted = kernel_one.shape[2]
    tiles, faces = lax.axis_size("tile"), lax.axis_size("face")
    devices = tiles * faces
    count = obs_values.shape[0]
    capacity = 2 * count // devices
    all_rows = 2 * rows
    middle = rows - 2
    chunk = 2 * capacity + PIXEL_ROWS
    x = state.reshape(all_rows, width, channels)
    c = cotangent.reshape(all_rows, width, channels)
    even = is_even()
    pairs = [(i, i ^ 1) for i in range(tiles)]
    crosses = [(i, i + 1 if i % 2 else i - 1) for i in range(1, tiles - 1)]
    strip = 16

    def ends(at):
        fields = [field.reshape(2, rows, width, channels) for field in (x, c)]
        picked = [
            jnp.concatenate(
                [
                    lax.dynamic_slice(field, (0, at, start, 0), (2, 1, strip, channels))[:, 0]
                    for start in (0, width - strip)
                ],
                axis=1,
            )
            for field in fields
        ]
        return jnp.concatenate(picked, axis=0)

    pair_ends = lax.ppermute(ends(jnp.where(even, rows - 1, 0)), "tile", pairs)
    cross_ends = lax.ppermute(ends(jnp.where(even, 0, rows - 1)), "tile", crosses)
    low_row = lambda field, at: lax.dynamic_index_in_dim(
        field.reshape(2, rows, width, channels), at, 1, keepdims=False
    )
    border_rows = lambda at: jnp.concatenate([low_row(x, at), low_row(c, at)], axis=0)
    pair_out = border_rows(jnp.where(even, rows - 1, 0))
    cross_out = border_rows(jnp.where(even, 0, rows - 1))
    smem = pl.BlockSpec(memory_space=pltpu.SMEM)
    vmem = pl.BlockSpec(memory_space=pltpu.VMEM)
    hbm = pl.BlockSpec(memory_space=pl.ANY)

    def exchange(own):
        parts = [own]
        for k in range(1, faces):
            parts.append(
                lax.ppermute(own, "face", [((i + k) % faces, i) for i in range(faces)])
            )
        return parts

    packed = pl.pallas_call(
        functools.partial(pack_body, capacity),
        in_specs=[hbm] * 3,
        out_specs=hbm,
        out_shape=pltpu.HBM((devices, chunk, 128), BF16),
        scratch_shapes=[
            pltpu.VMEM((1, count), jnp.int32),
            pltpu.VMEM((1, count), jnp.int32),
            pltpu.VMEM((count, lifted), BF16),
            pltpu.VMEM((devices, chunk, 128), BF16),
            pltpu.SemaphoreType.DMA((3,)),
            pltpu.SemaphoreType.DMA((devices * capacity // 512,)),
        ],
        compiler_params=params(16),
        cost_estimate=cost(2 * devices * capacity * count * lifted, 2 << 20),
        name="pack",
    )(far(obs_dest.reshape(1, count)), far(obs_pixel.reshape(1, count)), far(obs_values))
    received = lax.all_to_all(packed, ("face", "tile"), 0, 0, tiled=True)

    b1 = bias_one.reshape(1, lifted)
    b2 = bias_two.reshape(1, channels)
    row_block = lambda n: pl.BlockSpec((1, width, n), lambda i: (i, 0, 0))
    edge_block = lambda n: pl.BlockSpec((1, width, n), lambda i: (border_row(i, rows), 0, 0))
    conv_flops = 2 * 9 * all_rows * width * channels * lifted
    plane = (4, width, channels)
    pre, grad_inner, k1t, k2t = pl.pallas_call(
        functools.partial(lift_body, rows),
        in_specs=[hbm] * 4 + [vmem],
        out_specs=[hbm] * 2 + [vmem] * 2,
        out_shape=[pltpu.HBM((all_rows, width, lifted), F32)] * 2
        + [pltpu.HBM(kernel_two.shape, BF16), pltpu.HBM(kernel_one.shape, BF16)],
        scratch_shapes=[
            pltpu.VMEM(x.shape, BF16),
            pltpu.VMEM(c.shape, BF16),
            pltpu.VMEM(kernel_one.shape, BF16),
            pltpu.VMEM(kernel_two.shape, BF16),
            pltpu.VMEM((2, all_rows, width, 3 * channels), BF16),
            pltpu.VMEM((2, all_rows, width, lifted), F32),
            pltpu.SemaphoreType.DMA((4 + 2 * all_rows,)),
        ],
        compiler_params=params(40),
        cost_estimate=cost(conv_flops, 8 << 20),
        name="lift",
    )(far(x), far(c), far(kernel_one), far(kernel_two), b1)
    pre, grad_inner = far(pre), far(grad_inner)
    pair_out, cross_out, pair_ends, cross_ends, k1t = lax.optimization_barrier(
        (pair_out, cross_out, pair_ends, cross_ends, k1t)
    )
    pair_rows = lax.ppermute(pair_out, "tile", pairs)
    cross_rows = lax.ppermute(cross_out, "tile", crosses)
    low = lambda n: pl.BlockSpec((n, strip, channels), lambda *_: (0, 0, 0))
    high = lambda n, at: pl.BlockSpec((n, strip, channels), lambda *_: (0, at, 0))
    tail = width // strip - 1
    edge_shape = (2, 2, 2 * GROUP, channels)
    edges = pl.pallas_call(
        functools.partial(edge_body, rows),
        grid=(1,),
        in_specs=[low(all_rows), high(all_rows, tail)] * 2 + [low(4), high(4, 1)] * 2,
        out_specs=fixed(edge_shape),
        out_shape=jax.ShapeDtypeStruct(edge_shape, F32),
        compiler_params=params(8),
        cost_estimate=cost(0, 1 << 18),
        name="edges",
    )(x, x, c, c, pair_ends, pair_ends, cross_ends, cross_ends)
    parts = exchange(edges)

    side_in = (2, 2 * GROUP, lifted)
    end = width // GROUP - 1
    edge_strip = lambda at: pl.BlockSpec((all_rows, GROUP, lifted), lambda *_: (0, at, 0))
    rim_shape = (2, 4 * GROUP, lifted)
    taps_shape = (2, 2, 3, channels, lifted)
    rim_base, side_taps = pl.pallas_call(
        functools.partial(rim_in_body, rows),
        grid=(1,),
        in_specs=[smem, hbm, hbm]
        + [edge_strip(0), edge_strip(end)] * 2
        + [low(all_rows), high(all_rows, tail)] * 2
        + [low(4), high(4, 1)] * 2,
        out_specs=[fixed(rim_shape), fixed(taps_shape)],
        out_shape=[jax.ShapeDtypeStruct(rim_shape, F32), jax.ShapeDtypeStruct(taps_shape, BF16)],
        scratch_shapes=[
            pltpu.VMEM(kernel_one.shape, BF16),
            pltpu.VMEM(k2t.shape, BF16),
            pltpu.SemaphoreType.DMA((2,)),
        ],
        compiler_params=params(8),
        cost_estimate=cost(0, 2 << 20),
        name="rim_in",
    )(
        matching, far(kernel_one), far(k2t), pre, pre, grad_inner, grad_inner, x, x, c, c, pair_ends,
        pair_ends, cross_ends, cross_ends,
    )
    side_two = (2, 2, 2 * GROUP, lifted)
    slots = devices * capacity
    onehot_flops = 2 * width * slots * lifted
    other_block = pl.BlockSpec(
        (1, width, channels), lambda j: ((1 - j // 2) * rows + rows - 1, 0, 0)
    )
    values, keys, pre_b, grad_b, found_b, rim_found, rim_taps = pl.pallas_call(
        functools.partial(found_body, rows, capacity),
        in_specs=[hbm] * 5,
        out_specs=[vmem] * 7,
        out_shape=[
            hold((slots, lifted), BF16),
            hold((PIXEL_ROWS, slots), F32),
            hold((4, width, lifted), F32),
            hold((4, width, lifted), F32),
            hold((4, width, lifted), F32),
            hold(rim_shape[1:], F32),
            hold((2, 2, 3, channels, lifted), BF16),
        ],
        scratch_shapes=[
            pltpu.VMEM(received.shape, BF16),
            pltpu.SemaphoreType.DMA((13,)),
        ],
        compiler_params=params(),
        cost_estimate=cost(4 * onehot_flops, 6 << 20),
        name="found",
    )(far(received), pre, grad_inner, far(kernel_one), far(k2t))
    values, keys, pre_b, grad_b = held(values), held(keys), held(pre_b), held(grad_b)
    found_b = held(found_b)
    x_side, c_side, edges_two = pl.pallas_call(
        functools.partial(rim_body, rows, faces),
        in_specs=[smem] + [vmem] * (3 + faces),
        out_specs=[vmem] * 3,
        out_shape=[
            hold(side_in, F32),
            hold(side_in, F32),
            jax.ShapeDtypeStruct(side_two, F32),
        ],
        compiler_params=params(8),
        cost_estimate=cost(0, 1 << 20),
        name="rim",
    )(matching, side_taps, rim_base, held(rim_found), *parts)
    x_side, c_side = held(x_side), held(c_side)
    parts_two = exchange(edges_two)

    border_shape = hold((4, width, lifted), BF16)
    inner_b, gp_b = pl.pallas_call(
        functools.partial(border_body, rows),
        in_specs=[vmem] * 6 + [hbm] * 4,
        out_specs=[vmem] * 2,
        out_shape=[border_shape] * 2,
        scratch_shapes=[
            pltpu.VMEM((2, 4, width, channels), BF16),
            pltpu.SemaphoreType.DMA((8,)),
        ],
        compiler_params=params(),
        cost_estimate=cost(conv_flops // 6, 4 << 20),
        name="border",
    )(
        pre_b, grad_b, found_b, held(rim_taps), x_side, c_side, far(pair_rows), far(cross_rows), far(x),
        far(c),
    )
    inner_b, gp_b = held(inner_b), held(gp_b)

    side_out = (2, 2, 2 * GROUP, channels)
    to_pair, to_cross, sides = pl.pallas_call(
        functools.partial(send_body, rows, faces),
        in_specs=[smem] + [vmem] * (4 + faces),
        out_specs=[vmem] * 3,
        out_shape=[
            jax.ShapeDtypeStruct(plane, BF16),
            jax.ShapeDtypeStruct(plane, BF16),
            jax.ShapeDtypeStruct(side_out, F32),
        ],
        compiler_params=params(16),
        cost_estimate=cost(conv_flops // 6, 4 << 20),
        name="send",
    )(matching, inner_b, gp_b, kernel_two, k1t, *parts_two)
    from_pair = lax.ppermute(to_pair, "tile", pairs)
    from_cross = lax.ppermute(to_cross, "tile", crosses)

    inner_m, gp_m = pl.pallas_call(
        functools.partial(middle_body, rows),
        in_specs=[hbm, vmem, vmem, hbm, hbm, vmem, vmem],
        out_specs=[vmem] * 2,
        out_shape=[hold((2 * middle, width, lifted), BF16)] * 2,
        scratch_shapes=[
            pltpu.VMEM((2, 2 * middle, width, lifted), F32),
            pltpu.SemaphoreType.DMA((4 * middle,)),
        ],
        compiler_params=params(32),
        cost_estimate=cost(2 * middle * onehot_flops, 10 << 20),
        name="middle",
    )(to_cross, values, keys, pre, grad_inner, x_side, c_side)
    inner_m, gp_m = held(inner_m), held(gp_m)

    analysis, ana_b, grad_state, grad_b = pl.pallas_call(
        functools.partial(inside_body, rows),
        in_specs=[vmem] * 8 + [hbm] * 2,
        out_specs=[hbm, vmem, hbm, vmem],
        out_shape=[
            pltpu.HBM((all_rows, width, channels), BF16),
            hold(plane, F32),
            pltpu.HBM((all_rows, width, channels), F32),
            hold(plane, F32),
        ],
        scratch_shapes=[
            pltpu.VMEM((2, all_rows, width, channels), BF16),
            pltpu.VMEM((2 * middle, width, channels), BF16),
            pltpu.VMEM((2 * middle, width, channels), F32),
            pltpu.SemaphoreType.DMA((2 + 4 * middle,)),
        ],
        compiler_params=params(),
        cost_estimate=cost(2 * conv_flops, 14 << 20),
        name="inside",
    )(inner_b, gp_b, inner_m, gp_m, sides, kernel_two, k1t, b2, far(x), far(c))
    ana_b, grad_b = held(ana_b), held(grad_b)

    analysis, grad_state = pl.pallas_call(
        functools.partial(final_body, rows),
        in_specs=[vmem] * 5 + [hbm] * 2,
        out_specs=[hbm] * 2,
        out_shape=[
            pltpu.HBM((all_rows, width, channels), BF16),
            pltpu.HBM((all_rows, width, channels), F32),
        ],
        scratch_shapes=[
            pltpu.VMEM(plane, BF16),
            pltpu.VMEM(plane, F32),
            pltpu.SemaphoreType.DMA((8,)),
        ],
        input_output_aliases={5: 0, 6: 1},
        compiler_params=params(16),
        cost_estimate=cost(0, 6 << 20),
        name="final",
    )(ana_b, grad_b, to_cross, from_pair, from_cross, far(analysis), far(grad_state))
    return analysis.reshape(state.shape), grad_state.reshape(cotangent.shape)


def solution(mesh):
    return jax.shard_map(
        per_device,
        mesh=mesh,
        in_specs=(
            P("face", "tile", None, None, None, None),
            P(("face", "tile"), None),
            P(("face", "tile"), None),
            P(("face", "tile")),
            P(),
            P(),
            P(),
            P(),
            P(),
            P("face", "tile", None, None, None, None),
        ),
        out_specs=(
            P("face", "tile", None, None, None, None),
            P("face", "tile", None, None, None, None),
        ),
        check_vma=False,
    )
```

```python
import functools
import math

import jax
import jax.numpy as jnp
from jax import lax
from jax.experimental import pallas as pl
from jax.experimental.pallas import tpu as pltpu
from jax.sharding import PartitionSpec as P

F32 = jnp.float32
BF16 = jnp.bfloat16
GROUP = 8
HIGH = 64
PIXEL_ROWS = 8
ROOT = math.sqrt(2.0 / math.pi)
CUBIC = 0.044715


def params(mib=24):
    return pltpu.CompilerParams(vmem_limit_bytes=mib << 20)


def cost(flops, nbytes):
    return pl.CostEstimate(flops=int(flops), bytes_accessed=int(nbytes), transcendentals=0)


def hold(shape, kind):
    return pltpu.VMEM(shape, kind)


def held(array):
    return pltpu.with_memory_space_constraint(array, pltpu.VMEM)


def far(array):
    return pltpu.with_memory_space_constraint(array, pltpu.HBM)


def fixed(shape):
    return pl.BlockSpec(shape, lambda *_: (0,) * len(shape))


def dot(a, b):
    return jnp.dot(a, b, preferred_element_type=F32)


def matched(matching_ref, side, faces):
    face = lax.axis_index("face")
    partner = matching_ref[face, side, 0]
    return lax.rem(partner - face + faces, faces), matching_ref[face, side, 1], matching_ref[face, side, 2]


def is_even():
    return lax.rem(lax.axis_index("tile"), 2) == 0


def is_last():
    return lax.axis_index("tile") == lax.axis_size("tile") - 1


def partner_rows(part_refs, array, hop, their_side, flipped):
    rows = None
    for k, ref in enumerate(part_refs):
        mine = jnp.where(their_side == 1, ref[array, 1], ref[array, 0])
        rows = mine if rows is None else jnp.where(hop == k, mine, rows)
    swapped = jnp.concatenate([rows[GROUP:], rows[:GROUP]], axis=0)
    return jnp.where(flipped == 1, swapped, rows)


def rolled_rows(rows, step):
    first, second = rows[:GROUP], rows[GROUP:]
    if step:
        first = pltpu.roll(first, (-step) % GROUP, 0)
        second = pltpu.roll(second, step % GROUP, 0)
    return jnp.concatenate([first, second], axis=0).astype(BF16)


def side_forward(rows, side, taps_ref):
    lhs = jnp.concatenate([rolled_rows(rows, dy) for dy in (-1, 0, 1)], axis=1)
    taps = jnp.concatenate([taps_ref[3 * row + 2 * side] for row in range(3)], axis=0)
    return dot(lhs, taps)


def side_adjoint(rows, their_side, flipped, taps_ref):
    lhs = jnp.concatenate([rolled_rows(rows, -dy) for dy in (-1, 0, 1)], axis=1)
    order = [jnp.where(flipped == 1, 2 - row, row) for row in range(3)]
    taps = jnp.concatenate([taps_ref[3 * row + 2 * their_side] for row in order], axis=0)
    return dot(lhs, taps)


def shift_columns(values, step):
    count = values.shape[0]
    at = lax.broadcasted_iota(jnp.int32, values.shape, 0)
    moved = pltpu.roll(values, (-step) % count, 0)
    edge = count - 1 if step == 1 else 0
    return jnp.where(at == edge, 0.0, moved)


def spread_columns(row, order):
    wide = row.astype(F32)
    return jnp.concatenate(
        [row if s == 0 else shift_columns(wide, s).astype(BF16) for s in order], axis=1
    )


def add_edges(values, left, right):
    count = values.shape[0]
    at = lax.broadcasted_iota(jnp.int32, (GROUP, values.shape[1]), 0)
    first = values[:GROUP] + jnp.where(at == 0, left, 0.0)
    tail = values[count - GROUP :] + jnp.where(at == GROUP - 1, right, 0.0)
    return jnp.concatenate([first, values[GROUP : count - GROUP], tail], axis=0)


def pack_body(
    capacity, dest_in, pixel_in, values_in, out_hbm, dest_ref, pixel_ref, values_ref, out_ref, in_sem,
    out_sem,
):
    count = values_ref.shape[0]
    devices = out_ref.shape[0]
    block = 128
    loads = [
        pltpu.make_async_copy(source, target, in_sem.at[k])
        for k, (source, target) in enumerate(
            ((dest_in, dest_ref), (pixel_in, pixel_ref), (values_in, values_ref))
        )
    ]
    for load in loads:
        load.start()
    loads[0].wait()
    loads[1].wait()
    dest_row = dest_ref[...].astype(F32)
    pixel_row = pixel_ref[...]
    eye = lax.broadcasted_iota(jnp.int32, (block, block), 0) == lax.broadcasted_iota(
        jnp.int32, (block, block), 1
    )

    def column(row, start):
        piece = row[:, start : start + block]
        return jnp.sum(jnp.where(eye, piece, 0.0), axis=1, keepdims=True)

    high_row = lax.shift_right_logical(pixel_row, 6).astype(F32) + 1.0
    low_row = (pixel_row & (HIGH - 1)).astype(F32)
    own = lax.broadcasted_iota(jnp.int32, (block, count), 0)
    other = lax.broadcasted_iota(jnp.int32, (block, count), 1)
    lane = lax.broadcasted_iota(jnp.int32, (block, 128), 1)
    lane_rank = (lane & (HIGH - 1)).astype(F32)
    rank_row = jnp.zeros((1, count), F32)
    coded = []
    for start in range(0, count, block):
        same = column(dest_row, start) == dest_row
        later = (own + start) < other
        rank_row = rank_row + jnp.sum(
            jnp.where(same & later, 1.0, 0.0), axis=0, keepdims=True
        )
    for start in range(0, count, block):
        code = jnp.where(lane < HIGH, column(high_row, start), column(low_row, start))
        coded.append(jnp.where(column(rank_row, start) == lane_rank, code, 0.0).astype(BF16))
    to_device = (
        lax.broadcasted_iota(jnp.int32, (devices, count), 0).astype(F32) == dest_row
    )
    pixels = dot(
        jnp.where(to_device, 1.0, 0.0).astype(BF16), jnp.concatenate(coded, axis=0)
    )
    out_ref[:, 2 * capacity :, :] = jnp.broadcast_to(
        pixels[:, None, :], (devices, PIXEL_ROWS, 128)
    ).astype(BF16)
    slot_row = dest_row * capacity + rank_row
    slots = 512
    per_block = slots // capacity
    loads[2].wait()
    values = values_ref[...]
    stores = []
    slot_at = lax.broadcasted_iota(jnp.int32, (slots, count), 0).astype(F32)
    for start in range(0, devices * capacity, slots):
        onehot = jnp.where(slot_at == slot_row - start, 1.0, 0.0).astype(BF16)
        rows = dot(onehot, values).astype(BF16)
        first = start // capacity
        for half in range(2):
            out_ref[first : first + per_block, half * capacity : (half + 1) * capacity, :] = (
                rows[:, half * 128 : (half + 1) * 128].reshape(per_block, capacity, 128)
            )
        store = pltpu.make_async_copy(
            out_ref.at[first : first + per_block],
            out_hbm.at[first : first + per_block],
            out_sem.at[len(stores)],
        )
        store.start()
        stores.append(store)
    for store in stores:
        store.wait()


def end_rows(rows, x_ends, c_ends, pair_ends, cross_ends):
    prev, after = [], []
    even = is_even()
    for side in range(2):
        pair, cross = pair_ends[side], cross_ends[side]
        prev.append(jnp.where(even, cross, pair))
        after.append(jnp.where(even, pair, cross))
    outside = {}
    for array, own in enumerate((x_ends, c_ends)):
        for side in range(2):
            for band in range(2):
                plane = 2 * array + band
                fold = own[side][(1 - band) * rows + rows - 1]
                outside[array, side, 2 * band] = prev[side][plane]
                outside[array, side, 2 * band + 1] = jnp.where(is_last(), fold, after[side][plane])
    return outside


def edge_body(rows, x_lo, x_hi, c_lo, c_hi, a_lo, a_hi, b_lo, b_hi, out_ref):
    out_ref[...] = jnp.zeros_like(out_ref)
    wide = lambda refs: [ref[...].astype(F32) for ref in refs]
    x_ends, c_ends = wide((x_lo, x_hi)), wide((c_lo, c_hi))
    outside = end_rows(rows, x_ends, c_ends, wide((a_lo, a_hi)), wide((b_lo, b_hi)))
    for array, own in enumerate((x_ends, c_ends)):
        for side in range(2):
            at = 0 if side == 0 else own[side].shape[1] - 1
            for band in range(2):
                base = band * GROUP
                out_ref[array, side, base, :] = outside[array, side, 2 * band][at]
                for r in range(rows):
                    out_ref[array, side, base + 1 + r, :] = own[side][band * rows + r, at]
                out_ref[array, side, base + 1 + rows, :] = outside[array, side, 2 * band + 1][at]


def row_groups(rows, way):
    first, last = ((0, 0), (1, rows - 1)), ((0, rows - 1), (1, 0))
    if way < 0:
        first, last = last, first
    inner = tuple((b, r) for b in range(2) for r in range(1, rows - 1))
    return ((inner, (-1, 0, 1)), (first, (0, 1)), (last, (-1, 0)))


def border_index(j, rows):
    return (j // 2) * rows + (j % 2) * (rows - 1)


def border_row(j, rows):
    return (j // 2) * rows + lax.rem(j, 2) * (rows - 1)


def lift_body(
    rows, x_in, c_in, k1_in, k2_in, b1_ref, pre_out, grad_out, k1t_ref, k2t_ref, x_ref, c_ref, k1_ref,
    k2_ref, cat, held_rows, sem,
):
    width, channels = x_ref.shape[1], x_ref.shape[2]
    lifted = k1_ref.shape[2]
    used = [0]

    def slot():
        used[0] += 1
        return sem.at[used[0] - 1]

    loads = [
        pltpu.make_async_copy(source, target, slot())
        for source, target in ((x_in, x_ref), (k1_in, k1_ref), (k2_in, k2_ref), (c_in, c_ref))
    ]
    for load in loads:
        load.start()
    stores = []
    for array, (source, weights, order, out) in enumerate(
        ((x_ref, k1_ref, (-1, 0, 1), pre_out), (c_ref, k2t_ref, (1, 0, -1), grad_out))
    ):
        way = 1 - 2 * array
        loads[2 * array].wait()
        loads[2 * array + 1].wait()
        if array == 1:
            for t in range(k2_ref.shape[0]):
                k2t_ref[t] = k2_ref[t].astype(F32).T.astype(BF16)
        for i in range(2 * rows):
            cat[array, i] = spread_columns(source[i], order)
        inner, first, last = row_groups(rows, way)
        half = len(inner[0]) // 2
        groups = ((inner[0][:half], inner[1]), (inner[0][half:], inner[1]), first, last)
        for members, steps in groups:
            lhs = jnp.concatenate(
                [
                    jnp.concatenate(
                        [cat[array, b * rows + r + way * (1 - 2 * b) * dy] for dy in steps], axis=1
                    )
                    for b, r in members
                ],
                axis=0,
            )
            taps = weights[3 * (steps[0] + 1) : 3 * (steps[-1] + 2)]
            total = dot(lhs, taps.reshape(3 * len(steps) * channels, lifted))
            if array == 0:
                total = total + b1_ref[...]
            for k, (b, r) in enumerate(members):
                i = b * rows + r
                held_rows[array, i] = total[k * width : (k + 1) * width]
                store = pltpu.make_async_copy(held_rows.at[array, i], out.at[i], slot())
                store.start()
                stores.append(store)
    for t in range(k1_ref.shape[0]):
        k1t_ref[t] = k1_ref[t].astype(F32).T.astype(BF16)
    for store in stores:
        store.wait()


def row_onehot(keys, row, width):
    column = lax.broadcasted_iota(jnp.int32, (width, keys.shape[1]), 0).astype(F32)
    return jnp.where(column == keys[0:1, :] - float(row * width), 1.0, 0.0).astype(BF16)


def rim_in_body(
    rows, matching_ref, k1_in, k2t_in, pre_lo, pre_hi, grad_lo, grad_hi, x_lo, x_hi, c_lo, c_hi,
    a_lo, a_hi, b_lo, b_hi, base_ref, taps_ref, k1_ref, k2t_ref, sem,
):
    loads = [
        pltpu.make_async_copy(k1_in, k1_ref, sem.at[0]),
        pltpu.make_async_copy(k2t_in, k2t_ref, sem.at[1]),
    ]
    for load in loads:
        load.start()
    for load in loads:
        load.wait()
    face = lax.axis_index("face")
    for side in range(2):
        their_side, flipped = matching_ref[face, side, 1], matching_ref[face, side, 2]
        for row in range(3):
            taps_ref[0, side, row] = k1_ref[3 * row + 2 * side]
            turned = jnp.where(flipped == 1, 2 - row, row)
            taps_ref[1, side, row] = k2t_ref[3 * turned + 2 * their_side]
    whole = lambda refs: [ref[...] for ref in refs]
    x_ends, c_ends = whole((x_lo, x_hi)), whole((c_lo, c_hi))
    outside = end_rows(rows, x_ends, c_ends, whole((a_lo, a_hi)), whole((b_lo, b_hi)))
    channels, lifted = k1_ref.shape[1], k1_ref.shape[2]
    base_ref[...] = jnp.zeros_like(base_ref)
    for array, (strips, weights, order) in enumerate(
        (((pre_lo, pre_hi), k1_ref, (-1, 0, 1)), ((grad_lo, grad_hi), k2t_ref, (1, 0, -1)))
    ):
        for side in range(2):
            spot = 0 if side == 0 else GROUP - 1
            for b in range(2):
                for r in range(rows):
                    at = 2 * GROUP * side + GROUP * b + r + 1
                    base_ref[array, at : at + 1, :] = strips[side][
                        b * rows + r, spot : spot + 1, :
                    ]
        for pair in ((0, 3), (1, 2)):
            spots = [(side, j) for side in range(2) for j in pair]
            lhs = [spread_columns(outside[array, side, j], order) for side, j in spots]
            row = 0 if (pair[0] == 0) == (array == 0) else 6
            found = dot(
                jnp.concatenate(lhs, axis=0), weights[row : row + 3].reshape(3 * channels, lifted)
            )
            strip = found.shape[0] // len(spots)
            for k, (side, j) in enumerate(spots):
                at = 2 * GROUP * side + GROUP * (j // 2) + 1 + (rows - 1) * (j % 2)
                spot = k * strip + (0 if side == 0 else strip - 1)
                base_ref[array, at : at + 1, :] += found[spot : spot + 1]


def rim_body(rows, faces, matching_ref, taps_ref, base_ref, found_ref, *rest):
    parts = rest[:faces]
    x_side, c_side, edge_ref = rest[faces:]
    taps = taps_ref[...].reshape(2, 2, 3 * taps_ref.shape[3], taps_ref.shape[4])
    for side in range(2):
        hop, their_side, flipped = matched(matching_ref, side, faces)
        for array, out in enumerate((x_side, c_side)):
            near = partner_rows(parts, array, hop, their_side, flipped)
            way = 1 - 2 * array
            lhs = jnp.concatenate([rolled_rows(near, way * dy) for dy in (-1, 0, 1)], axis=1)
            out[side] = dot(lhs, taps[array, side])
    e = lax.broadcasted_iota(jnp.int32, (4 * GROUP, 1), 0) & (GROUP - 1)
    inside = (e >= 1) & (e <= rows)
    shape = base_ref.shape[1:]
    v = base_ref[0] + x_side[...].reshape(shape) + found_ref[...]
    inner, gp = gelu_pair(v, base_ref[1] + c_side[...].reshape(shape))
    edge_ref[0] = jnp.where(inside, inner.astype(F32), 0.0).reshape(edge_ref.shape[1:])
    edge_ref[1] = jnp.where(inside, gp.astype(F32), 0.0).reshape(edge_ref.shape[1:])


def gelu_pair(v, grad):
    square = v * v
    t = jnp.tanh(v * (ROOT + (ROOT * CUBIC) * square))
    half = 0.5 + 0.5 * t
    slope = half + (0.5 * v) * (1.0 - t * t) * (ROOT + (3.0 * ROOT * CUBIC) * square)
    return (v * half).astype(BF16), (grad * slope).astype(BF16)


def unpack_received(capacity, recv_ref, values, keys):
    devices = recv_ref.shape[0]
    slots = devices * capacity
    per_lane = 128 // capacity
    for half in range(2):
        values[:, half * 128 : (half + 1) * 128] = recv_ref[
            :, half * capacity : (half + 1) * capacity, :
        ].reshape(slots, 128)
    owner = lax.broadcasted_iota(jnp.int32, (PIXEL_ROWS, 128), 1) // capacity
    for start in range(0, devices, per_lane):
        key = jnp.zeros((PIXEL_ROWS, 128), F32)
        for k in range(per_lane):
            code = recv_ref[start + k, 2 * capacity :, :].astype(F32)
            mine = (code - 1.0) * HIGH + pltpu.roll(code, HIGH, 1)
            if k:
                mine = pltpu.roll(mine, k * capacity, 1)
            key = jnp.where(owner == k, mine, key)
        keys[:, start * capacity : start * capacity + 128] = key


def row_taps(taps_ref, row):
    return jnp.concatenate([taps_ref[3 * row + dx] for dx in range(3)], axis=1)


def merge_shifts(wide, forward):
    channels = wide.shape[1] // 3
    left, mid, right = (wide[:, k * channels : (k + 1) * channels] for k in range(3))
    step = -1 if forward else 1
    return mid + shift_columns(left, step) + shift_columns(right, -step)


def found_body(
    rows, capacity, recv_in, pre_in, grad_in, k1_in, k2t_in, values, keys, pre_b, grad_b, found_b, rim_ref,
    taps, recv_ref, sem,
):
    width = pre_b.shape[1]
    loads = [pltpu.make_async_copy(recv_in, recv_ref, sem.at[0])]
    for j in range(4):
        row = border_index(j, rows)
        loads.append(pltpu.make_async_copy(pre_in.at[row], pre_b.at[j], sem.at[1 + j]))
    for j in range(4):
        row = border_index(j, rows)
        loads.append(pltpu.make_async_copy(grad_in.at[row], grad_b.at[j], sem.at[5 + j]))
    for array, source in enumerate((k1_in, k2t_in)):
        for k in range(2):
            loads.append(
                pltpu.make_async_copy(
                    source.at[6 * k : 6 * k + 3], taps.at[array, k], sem.at[9 + 2 * array + k]
                )
            )
    for load in loads:
        load.start()
    loads[0].wait()
    unpack_received(capacity, recv_ref, values, keys)
    at = lax.broadcasted_iota(jnp.int32, (4 * GROUP, 1), 0)
    e = at & (GROUP - 1)
    b = (at // GROUP) & 1
    side = at // (2 * GROUP)
    inside = (e >= 1) & (e <= rows)
    pixel = (b * rows + e - 1) * width + side * (width - 1)
    wanted = jnp.where(inside, pixel, -1).astype(F32)
    onehot = jnp.where(keys[0:1, :] == wanted, 1.0, 0.0).astype(BF16)
    rim_ref[...] = dot(onehot, values[...])
    for half in range(2):
        members = (2 * half, 2 * half + 1)
        found = dot(
            jnp.concatenate(
                [row_onehot(keys, border_index(j, rows), width) for j in members], axis=0
            ),
            values[...],
        )
        for k, j in enumerate(members):
            found_b[j] = found[k * width : (k + 1) * width]
    for load in loads[1:]:
        load.wait()


def border_body(
    rows, pre_b, grad_b, found_b, taps, x_side, c_side, a_in, b_in, x_in, c_in, inner_ref, gp_ref, outside,
    sem,
):
    width, lifted = inner_ref.shape[1], inner_ref.shape[2]
    channels = outside.shape[3]
    even, last = is_even(), is_last()
    waits = [[], []]
    used = [0]

    def load(array, target, *sources):
        slot = sem.at[used[0]]
        used[0] += 1
        for condition, source in sources:
            copy = pltpu.make_async_copy(source, target, slot)
            pl.when(condition)(copy.start)
        waits[array].append(copy)

    for array, source in enumerate((x_in, c_in)):
        for j in range(4):
            band = j // 2
            plane = 2 * array + band
            if j % 2 == 0:
                choices = ((even, b_in.at[plane]), (jnp.logical_not(even), a_in.at[plane]))
            else:
                fold = source.at[(1 - band) * rows + rows - 1]
                middle = jnp.logical_not(even) & jnp.logical_not(last)
                choices = ((last, fold), (even, a_in.at[plane]), (middle, b_in.at[plane]))
            load(array, outside.at[array, j], *choices)

    for copy in waits[0] + waits[1]:
        copy.wait()
    for pair in ((0, 3), (1, 2)):
        totals = []
        for array, order in enumerate(((-1, 0, 1), (1, 0, -1))):
            lhs = [spread_columns(outside[array, j], order) for j in pair]
            tap = taps[array, 0 if (pair[0] == 0) == (array == 0) else 1]
            totals.append(dot(jnp.concatenate(lhs, axis=0), tap.reshape(3 * channels, lifted)))
        for k, j in enumerate(pair):
            at = GROUP * (j // 2) + 1 + (rows - 1) * (j % 2)
            piece = slice(k * width, (k + 1) * width)
            inner, gp = gelu_pair(
                add_edges(
                    totals[0][piece] + (pre_b[j] + found_b[j]),
                    x_side[0, at : at + 1, :],
                    x_side[1, at : at + 1, :],
                ),
                add_edges(
                    totals[1][piece] + grad_b[j], c_side[0, at : at + 1, :], c_side[1, at : at + 1, :]
                ),
            )
            inner_ref[j] = inner
            gp_ref[j] = gp


def send_rows(rows, inner_ref, gp_ref, k2_ref, k1t_ref, side_ref, out_ref, bottom):
    width = inner_ref.shape[1]
    for array, (source, taps) in enumerate(((inner_ref, k2_ref), (gp_ref, k1t_ref))):
        for band in range(2):
            tap = jnp.where((bottom == band) == (array == 0), 2, 0)
            wide = dot(source[2 * band + bottom], row_taps(taps, tap))
            corner = GROUP * band + (rows + 1) * bottom
            part = add_edges(
                merge_shifts(wide, array == 0),
                side_ref[array, 0, pl.ds(corner, 1), :],
                side_ref[array, 1, pl.ds(corner, 1), :],
            )
            out_ref[2 * array + band] = part.astype(BF16)


def cross_body(rows, faces, matching_ref, inner_ref, gp_ref, k2_ref, k1t_ref, *rest):
    parts = rest[:faces]
    cross_ref, side_ref = rest[faces:]
    for side in range(2):
        hop, their_side, flipped = matched(matching_ref, side, faces)
        near = partner_rows(parts, 0, hop, their_side, flipped)
        side_ref[0, side] = side_forward(near, side, k2_ref)
        near = partner_rows(parts, 1, hop, their_side, flipped)
        side_ref[1, side] = side_adjoint(near, their_side, flipped, k1t_ref)
    bottom = jnp.where(is_even(), 0, 1)
    send_rows(rows, inner_ref, gp_ref, k2_ref, k1t_ref, side_ref, cross_ref, bottom)


def pair_body(rows, _, inner_ref, gp_ref, k2_ref, k1t_ref, side_ref, pair_ref):
    bottom = jnp.where(is_even(), 1, 0)
    send_rows(rows, inner_ref, gp_ref, k2_ref, k1t_ref, side_ref, pair_ref, bottom)


def middle_body(
    rows, _, values, keys, pre_in, grad_in, x_side, c_side, inner_ref, gp_ref, base, sem
):
    middle = rows - 2
    width = base.shape[2]
    members = [(b, r) for b in range(2) for r in range(1, rows - 1)]
    loads = []
    for k in range(len(members)):
        for array, source in enumerate((pre_in, grad_in)):
            row = members[k][0] * rows + members[k][1]
            load = pltpu.make_async_copy(source.at[row], base.at[array, k], sem.at[2 * k + array])
            load.start()
            loads.append(load)
    found = dot(
        jnp.concatenate([row_onehot(keys, b * rows + r, width) for b, r in members], axis=0),
        values[...],
    )
    for k, (b, r) in enumerate(members):
        at = b * GROUP + r + 1
        loads[2 * k].wait()
        loads[2 * k + 1].wait()
        inner, gp = gelu_pair(
            add_edges(
                base[0, k] + found[k * width : (k + 1) * width],
                x_side[0, at : at + 1, :],
                x_side[1, at : at + 1, :],
            ),
            add_edges(base[1, k], c_side[0, at : at + 1, :], c_side[1, at : at + 1, :]),
        )
        inner_ref[k] = inner
        gp_ref[k] = gp


def inside_body(
    rows, inner_b, gp_b, inner_m, gp_m, side_ref, k2_ref, k1t_ref, b2_ref, x_ref, c_ref, ana_out, ana_b,
    grad_out, grad_b, ana_rows, grad_rows, sem,
):
    width, channels = x_ref.shape[1], x_ref.shape[2]
    middle = rows - 2
    stores = []
    for array, (border, inner, taps) in enumerate(
        ((inner_b, inner_m, k2_ref), (gp_b, gp_m, k1t_ref))
    ):
        way = 1 - 2 * array

        def plane(b, r):
            if r == 0 or r == rows - 1:
                return border[2 * b + r // (rows - 1)]
            return inner[middle * b + r - 1]

        for members, steps in row_groups(rows, way):
            lhs = jnp.concatenate(
                [
                    jnp.concatenate(
                        [plane(b, r + way * (1 - 2 * b) * dy) for dy in steps], axis=1
                    )
                    for b, r in members
                ],
                axis=0,
            )
            wide = dot(lhs, jnp.concatenate([row_taps(taps, dy + 1) for dy in steps], axis=0))
            for k, (b, r) in enumerate(members):
                i = b * rows + r
                at = b * GROUP + r + 1
                total = merge_shifts(wide[k * width : (k + 1) * width], array == 0)
                total = add_edges(
                    total + (x_ref, c_ref)[array][i].astype(F32),
                    side_ref[array, 0, at : at + 1, :],
                    side_ref[array, 1, at : at + 1, :],
                )
                if array == 0:
                    total = total + b2_ref[...]
                if len(steps) == 2:
                    (ana_b, grad_b)[array][2 * b + r // (rows - 1)] = total
                    continue
                held_rows, out = ((ana_rows, ana_out), (grad_rows, grad_out))[array]
                held_rows[k] = total.astype(held_rows.dtype)
                store = pltpu.make_async_copy(held_rows.at[k], out.at[i], sem.at[len(stores)])
                store.start()
                stores.append(store)
    for store in stores:
        store.wait()


def final_body(
    rows, ana_b, grad_b, own_ref, pair_ref, cross_ref, _, __, ana_out, grad_out, ana_rows, grad_rows, sem
):
    even, last = is_even(), is_last()
    stores = []
    for array, (acc, held_rows, out) in enumerate(
        ((ana_b, ana_rows, ana_out), (grad_b, grad_rows, grad_out))
    ):
        for j in range(4):
            band = j // 2
            plane = 2 * array + band
            if j % 2:
                add = jnp.where(even, pair_ref[plane], cross_ref[plane])
                add = jnp.where(last, own_ref[2 * array + 1 - band], add)
            else:
                add = jnp.where(even, cross_ref[plane], pair_ref[plane])
            held_rows[j] = (acc[j] + add.astype(F32)).astype(held_rows.dtype)
            store = pltpu.make_async_copy(
                held_rows.at[j], out.at[border_index(j, rows)], sem.at[len(stores)]
            )
            store.start()
            stores.append(store)
    for store in stores:
        store.wait()


def per_device(
    state,
    obs_values,
    obs_dest,
    obs_pixel,
    matching,
    kernel_one,
    bias_one,
    kernel_two,
    bias_two,
    cotangent,
):
    rows, width, channels = state.shape[3], state.shape[4], state.shape[5]
    lifted = kernel_one.shape[2]
    tiles, faces = lax.axis_size("tile"), lax.axis_size("face")
    devices = tiles * faces
    count = obs_values.shape[0]
    capacity = 2 * count // devices
    all_rows = 2 * rows
    middle = rows - 2
    chunk = 2 * capacity + PIXEL_ROWS
    x = state.reshape(all_rows, width, channels)
    c = cotangent.reshape(all_rows, width, channels)
    even = is_even()
    pairs = [(i, i ^ 1) for i in range(tiles)]
    crosses = [(i, i + 1 if i % 2 else i - 1) for i in range(1, tiles - 1)]
    strip = 16

    def ends(at):
        fields = [field.reshape(2, rows, width, channels) for field in (x, c)]
        picked = [
            jnp.concatenate(
                [
                    lax.dynamic_slice(field, (0, at, start, 0), (2, 1, strip, channels))[:, 0]
                    for start in (0, width - strip)
                ],
                axis=1,
            )
            for field in fields
        ]
        return jnp.concatenate(picked, axis=0)

    pair_ends = lax.ppermute(ends(jnp.where(even, rows - 1, 0)), "tile", pairs)
    cross_ends = lax.ppermute(ends(jnp.where(even, 0, rows - 1)), "tile", crosses)
    low_row = lambda field, at: lax.dynamic_index_in_dim(
        field.reshape(2, rows, width, channels), at, 1, keepdims=False
    )
    border_rows = lambda at: jnp.concatenate([low_row(x, at), low_row(c, at)], axis=0)
    pair_out = border_rows(jnp.where(even, rows - 1, 0))
    cross_out = border_rows(jnp.where(even, 0, rows - 1))
    smem = pl.BlockSpec(memory_space=pltpu.SMEM)
    vmem = pl.BlockSpec(memory_space=pltpu.VMEM)
    hbm = pl.BlockSpec(memory_space=pl.ANY)

    def exchange(own):
        parts = [own]
        for k in range(1, faces):
            parts.append(
                lax.ppermute(own, "face", [((i + k) % faces, i) for i in range(faces)])
            )
        return parts

    packed = pl.pallas_call(
        functools.partial(pack_body, capacity),
        in_specs=[hbm] * 3,
        out_specs=hbm,
        out_shape=pltpu.HBM((devices, chunk, 128), BF16),
        scratch_shapes=[
            pltpu.VMEM((1, count), jnp.int32),
            pltpu.VMEM((1, count), jnp.int32),
            pltpu.VMEM((count, lifted), BF16),
            pltpu.VMEM((devices, chunk, 128), BF16),
            pltpu.SemaphoreType.DMA((3,)),
            pltpu.SemaphoreType.DMA((devices * capacity // 512,)),
        ],
        compiler_params=params(16),
        cost_estimate=cost(2 * devices * capacity * count * lifted, 2 << 20),
        name="pack",
    )(far(obs_dest.reshape(1, count)), far(obs_pixel.reshape(1, count)), far(obs_values))
    received = lax.all_to_all(packed, ("face", "tile"), 0, 0, tiled=True)

    b1 = bias_one.reshape(1, lifted)
    b2 = bias_two.reshape(1, channels)
    row_block = lambda n: pl.BlockSpec((1, width, n), lambda i: (i, 0, 0))
    edge_block = lambda n: pl.BlockSpec((1, width, n), lambda i: (border_row(i, rows), 0, 0))
    conv_flops = 2 * 9 * all_rows * width * channels * lifted
    plane = (4, width, channels)
    pre, grad_inner, k1t, k2t = pl.pallas_call(
        functools.partial(lift_body, rows),
        in_specs=[hbm] * 4 + [vmem],
        out_specs=[hbm] * 2 + [vmem] * 2,
        out_shape=[pltpu.HBM((all_rows, width, lifted), F32)] * 2
        + [pltpu.HBM(kernel_two.shape, BF16), pltpu.HBM(kernel_one.shape, BF16)],
        scratch_shapes=[
            pltpu.VMEM(x.shape, BF16),
            pltpu.VMEM(c.shape, BF16),
            pltpu.VMEM(kernel_one.shape, BF16),
            pltpu.VMEM(kernel_two.shape, BF16),
            pltpu.VMEM((2, all_rows, width, 3 * channels), BF16),
            pltpu.VMEM((2, all_rows, width, lifted), F32),
            pltpu.SemaphoreType.DMA((4 + 2 * all_rows,)),
        ],
        compiler_params=params(40),
        cost_estimate=cost(conv_flops, 8 << 20),
        name="lift",
    )(far(x), far(c), far(kernel_one), far(kernel_two), b1)
    pre, grad_inner = far(pre), far(grad_inner)
    pair_out, cross_out, pair_ends, cross_ends, k1t = lax.optimization_barrier(
        (pair_out, cross_out, pair_ends, cross_ends, k1t)
    )
    pair_rows = lax.ppermute(pair_out, "tile", pairs)
    cross_rows = lax.ppermute(cross_out, "tile", crosses)
    low = lambda n: pl.BlockSpec((n, strip, channels), lambda *_: (0, 0, 0))
    high = lambda n, at: pl.BlockSpec((n, strip, channels), lambda *_: (0, at, 0))
    tail = width // strip - 1
    edge_shape = (2, 2, 2 * GROUP, channels)
    edges = pl.pallas_call(
        functools.partial(edge_body, rows),
        grid=(1,),
        in_specs=[low(all_rows), high(all_rows, tail)] * 2 + [low(4), high(4, 1)] * 2,
        out_specs=fixed(edge_shape),
        out_shape=jax.ShapeDtypeStruct(edge_shape, F32),
        compiler_params=params(8),
        cost_estimate=cost(0, 1 << 18),
        name="edges",
    )(x, x, c, c, pair_ends, pair_ends, cross_ends, cross_ends)
    parts = exchange(edges)

    side_in = (2, 2 * GROUP, lifted)
    end = width // GROUP - 1
    edge_strip = lambda at: pl.BlockSpec((all_rows, GROUP, lifted), lambda *_: (0, at, 0))
    rim_shape = (2, 4 * GROUP, lifted)
    taps_shape = (2, 2, 3, channels, lifted)
    rim_base, side_taps = pl.pallas_call(
        functools.partial(rim_in_body, rows),
        grid=(1,),
        in_specs=[smem, hbm, hbm]
        + [edge_strip(0), edge_strip(end)] * 2
        + [low(all_rows), high(all_rows, tail)] * 2
        + [low(4), high(4, 1)] * 2,
        out_specs=[fixed(rim_shape), fixed(taps_shape)],
        out_shape=[jax.ShapeDtypeStruct(rim_shape, F32), jax.ShapeDtypeStruct(taps_shape, BF16)],
        scratch_shapes=[
            pltpu.VMEM(kernel_one.shape, BF16),
            pltpu.VMEM(k2t.shape, BF16),
            pltpu.SemaphoreType.DMA((2,)),
        ],
        compiler_params=params(8),
        cost_estimate=cost(0, 2 << 20),
        name="rim_in",
    )(
        matching, far(kernel_one), far(k2t), pre, pre, grad_inner, grad_inner, x, x, c, c, pair_ends,
        pair_ends, cross_ends, cross_ends,
    )
    side_two = (2, 2, 2 * GROUP, lifted)
    slots = devices * capacity
    onehot_flops = 2 * width * slots * lifted
    other_block = pl.BlockSpec(
        (1, width, channels), lambda j: ((1 - j // 2) * rows + rows - 1, 0, 0)
    )
    values, keys, pre_b, grad_b, found_b, rim_found, rim_taps = pl.pallas_call(
        functools.partial(found_body, rows, capacity),
        in_specs=[hbm] * 5,
        out_specs=[vmem] * 7,
        out_shape=[
            hold((slots, lifted), BF16),
            hold((PIXEL_ROWS, slots), F32),
            hold((4, width, lifted), F32),
            hold((4, width, lifted), F32),
            hold((4, width, lifted), F32),
            hold(rim_shape[1:], F32),
            hold((2, 2, 3, channels, lifted), BF16),
        ],
        scratch_shapes=[
            pltpu.VMEM(received.shape, BF16),
            pltpu.SemaphoreType.DMA((13,)),
        ],
        compiler_params=params(),
        cost_estimate=cost(4 * onehot_flops, 6 << 20),
        name="found",
    )(far(received), pre, grad_inner, far(kernel_one), far(k2t))
    values, keys, pre_b, grad_b = held(values), held(keys), held(pre_b), held(grad_b)
    found_b = held(found_b)
    x_side, c_side, edges_two = pl.pallas_call(
        functools.partial(rim_body, rows, faces),
        in_specs=[smem] + [vmem] * (3 + faces),
        out_specs=[vmem] * 3,
        out_shape=[
            hold(side_in, F32),
            hold(side_in, F32),
            jax.ShapeDtypeStruct(side_two, F32),
        ],
        compiler_params=params(8),
        cost_estimate=cost(0, 1 << 20),
        name="rim",
    )(matching, side_taps, rim_base, held(rim_found), *parts)
    x_side, c_side = held(x_side), held(c_side)
    parts_two = exchange(edges_two)

    border_shape = hold((4, width, lifted), BF16)
    inner_b, gp_b = pl.pallas_call(
        functools.partial(border_body, rows),
        in_specs=[vmem] * 6 + [hbm] * 4,
        out_specs=[vmem] * 2,
        out_shape=[border_shape] * 2,
        scratch_shapes=[
            pltpu.VMEM((2, 4, width, channels), BF16),
            pltpu.SemaphoreType.DMA((8,)),
        ],
        compiler_params=params(),
        cost_estimate=cost(conv_flops // 6, 4 << 20),
        name="border",
    )(
        pre_b, grad_b, found_b, held(rim_taps), x_side, c_side, far(pair_rows), far(cross_rows), far(x),
        far(c),
    )
    inner_b, gp_b = held(inner_b), held(gp_b)

    side_out = (2, 2, 2 * GROUP, channels)
    to_cross, sides = pl.pallas_call(
        functools.partial(cross_body, rows, faces),
        in_specs=[smem] + [vmem] * (4 + faces),
        out_specs=[vmem] * 2,
        out_shape=[jax.ShapeDtypeStruct(plane, BF16), jax.ShapeDtypeStruct(side_out, F32)],
        compiler_params=params(16),
        cost_estimate=cost(conv_flops // 12, 3 << 20),
        name="send_cross",
    )(matching, inner_b, gp_b, kernel_two, k1t, *parts_two)
    from_cross = lax.ppermute(to_cross, "tile", crosses)
    to_pair = pl.pallas_call(
        functools.partial(pair_body, rows),
        in_specs=[hbm] + [vmem] * 5,
        out_specs=vmem,
        out_shape=jax.ShapeDtypeStruct(plane, BF16),
        compiler_params=params(16),
        cost_estimate=cost(conv_flops // 12, 3 << 20),
        name="send_pair",
    )(to_cross, inner_b, gp_b, kernel_two, k1t, sides)
    from_pair = lax.ppermute(to_pair, "tile", pairs)

    inner_m, gp_m = pl.pallas_call(
        functools.partial(middle_body, rows),
        in_specs=[hbm, vmem, vmem, hbm, hbm, vmem, vmem],
        out_specs=[vmem] * 2,
        out_shape=[hold((2 * middle, width, lifted), BF16)] * 2,
        scratch_shapes=[
            pltpu.VMEM((2, 2 * middle, width, lifted), F32),
            pltpu.SemaphoreType.DMA((4 * middle,)),
        ],
        compiler_params=params(32),
        cost_estimate=cost(2 * middle * onehot_flops, 10 << 20),
        name="middle",
    )(to_pair, values, keys, pre, grad_inner, x_side, c_side)
    inner_m, gp_m = held(inner_m), held(gp_m)

    analysis, ana_b, grad_state, grad_b = pl.pallas_call(
        functools.partial(inside_body, rows),
        in_specs=[vmem] * 10,
        out_specs=[hbm, vmem, hbm, vmem],
        out_shape=[
            pltpu.HBM((all_rows, width, channels), BF16),
            hold(plane, F32),
            pltpu.HBM((all_rows, width, channels), F32),
            hold(plane, F32),
        ],
        scratch_shapes=[
            pltpu.VMEM((2 * middle, width, channels), BF16),
            pltpu.VMEM((2 * middle, width, channels), F32),
            pltpu.SemaphoreType.DMA((4 * middle,)),
        ],
        compiler_params=params(),
        cost_estimate=cost(2 * conv_flops, 14 << 20),
        name="inside",
    )(inner_b, gp_b, inner_m, gp_m, sides, kernel_two, k1t, b2, x, c)
    ana_b, grad_b = held(ana_b), held(grad_b)

    analysis, grad_state = pl.pallas_call(
        functools.partial(final_body, rows),
        in_specs=[vmem] * 5 + [hbm] * 2,
        out_specs=[hbm] * 2,
        out_shape=[
            pltpu.HBM((all_rows, width, channels), BF16),
            pltpu.HBM((all_rows, width, channels), F32),
        ],
        scratch_shapes=[
            pltpu.VMEM(plane, BF16),
            pltpu.VMEM(plane, F32),
            pltpu.SemaphoreType.DMA((8,)),
        ],
        input_output_aliases={5: 0, 6: 1},
        compiler_params=params(16),
        cost_estimate=cost(0, 6 << 20),
        name="final",
    )(ana_b, grad_b, to_cross, from_pair, from_cross, far(analysis), far(grad_state))
    return analysis.reshape(state.shape), grad_state.reshape(cotangent.shape)


def solution(mesh):
    return jax.shard_map(
        per_device,
        mesh=mesh,
        in_specs=(
            P("face", "tile", None, None, None, None),
            P(("face", "tile"), None),
            P(("face", "tile"), None),
            P(("face", "tile")),
            P(),
            P(),
            P(),
            P(),
            P(),
            P("face", "tile", None, None, None, None),
        ),
        out_specs=(
            P("face", "tile", None, None, None, None),
            P("face", "tile", None, None, None, None),
        ),
        check_vma=False,
    )
```

```python
import functools
import math

import jax
import jax.numpy as jnp
from jax import lax
from jax.experimental import pallas as pl
from jax.experimental.pallas import tpu as pltpu
from jax.sharding import PartitionSpec as P

F32 = jnp.float32
BF16 = jnp.bfloat16
GROUP = 8
HIGH = 64
PIXEL_ROWS = 8
ROOT = math.sqrt(2.0 / math.pi)
CUBIC = 0.044715


def params(mib=24):
    return pltpu.CompilerParams(vmem_limit_bytes=mib << 20)


def cost(flops, nbytes):
    return pl.CostEstimate(flops=int(flops), bytes_accessed=int(nbytes), transcendentals=0)


def hold(shape, kind):
    return pltpu.VMEM(shape, kind)


def held(array):
    return pltpu.with_memory_space_constraint(array, pltpu.VMEM)


def far(array):
    return pltpu.with_memory_space_constraint(array, pltpu.HBM)


def fixed(shape):
    return pl.BlockSpec(shape, lambda *_: (0,) * len(shape))


def dot(a, b):
    return jnp.dot(a, b, preferred_element_type=F32)


def matched(matching_ref, side, faces):
    face = lax.axis_index("face")
    partner = matching_ref[face, side, 0]
    return lax.rem(partner - face + faces, faces), matching_ref[face, side, 1], matching_ref[face, side, 2]


def is_even():
    return lax.rem(lax.axis_index("tile"), 2) == 0


def is_last():
    return lax.axis_index("tile") == lax.axis_size("tile") - 1


def partner_rows(part_refs, array, hop, their_side, flipped):
    rows = None
    for k, ref in enumerate(part_refs):
        mine = jnp.where(their_side == 1, ref[array, 1], ref[array, 0])
        rows = mine if rows is None else jnp.where(hop == k, mine, rows)
    swapped = jnp.concatenate([rows[GROUP:], rows[:GROUP]], axis=0)
    return jnp.where(flipped == 1, swapped, rows)


def rolled_rows(rows, step):
    first, second = rows[:GROUP], rows[GROUP:]
    if step:
        first = pltpu.roll(first, (-step) % GROUP, 0)
        second = pltpu.roll(second, step % GROUP, 0)
    return jnp.concatenate([first, second], axis=0).astype(BF16)


def side_forward(rows, side, taps_ref):
    lhs = jnp.concatenate([rolled_rows(rows, dy) for dy in (-1, 0, 1)], axis=1)
    taps = jnp.concatenate([taps_ref[3 * row + 2 * side] for row in range(3)], axis=0)
    return dot(lhs, taps)


def side_adjoint(rows, their_side, flipped, taps_ref):
    lhs = jnp.concatenate([rolled_rows(rows, -dy) for dy in (-1, 0, 1)], axis=1)
    order = [jnp.where(flipped == 1, 2 - row, row) for row in range(3)]
    taps = jnp.concatenate([taps_ref[3 * row + 2 * their_side] for row in order], axis=0)
    return dot(lhs, taps)


def shift_columns(values, step):
    count = values.shape[0]
    at = lax.broadcasted_iota(jnp.int32, values.shape, 0)
    moved = pltpu.roll(values, (-step) % count, 0)
    edge = count - 1 if step == 1 else 0
    return jnp.where(at == edge, 0.0, moved)


def spread_columns(row, order):
    wide = row.astype(F32)
    return jnp.concatenate(
        [row if s == 0 else shift_columns(wide, s).astype(BF16) for s in order], axis=1
    )


def add_edges(values, left, right):
    count = values.shape[0]
    at = lax.broadcasted_iota(jnp.int32, (GROUP, values.shape[1]), 0)
    first = values[:GROUP] + jnp.where(at == 0, left, 0.0)
    tail = values[count - GROUP :] + jnp.where(at == GROUP - 1, right, 0.0)
    return jnp.concatenate([first, values[GROUP : count - GROUP], tail], axis=0)


def pack_body(
    capacity, dest_in, pixel_in, values_in, out_hbm, dest_ref, pixel_ref, values_ref, out_ref, in_sem,
    out_sem,
):
    count = values_ref.shape[0]
    devices = out_ref.shape[0]
    block = 128
    loads = [
        pltpu.make_async_copy(source, target, in_sem.at[k])
        for k, (source, target) in enumerate(
            ((dest_in, dest_ref), (pixel_in, pixel_ref), (values_in, values_ref))
        )
    ]
    for load in loads:
        load.start()
    loads[0].wait()
    loads[1].wait()
    tiles, faces = lax.axis_size("tile"), lax.axis_size("face")
    dest = dest_ref[...]
    dest_face = dest // tiles
    dest_row = ((dest - dest_face * tiles) * faces + dest_face).astype(F32)
    pixel_row = pixel_ref[...]
    eye = lax.broadcasted_iota(jnp.int32, (block, block), 0) == lax.broadcasted_iota(
        jnp.int32, (block, block), 1
    )

    def column(row, start):
        piece = row[:, start : start + block]
        return jnp.sum(jnp.where(eye, piece, 0.0), axis=1, keepdims=True)

    high_row = lax.shift_right_logical(pixel_row, 6).astype(F32) + 1.0
    low_row = (pixel_row & (HIGH - 1)).astype(F32)
    own = lax.broadcasted_iota(jnp.int32, (block, count), 0)
    other = lax.broadcasted_iota(jnp.int32, (block, count), 1)
    lane = lax.broadcasted_iota(jnp.int32, (block, 128), 1)
    lane_rank = (lane & (HIGH - 1)).astype(F32)
    rank_row = jnp.zeros((1, count), F32)
    coded = []
    for start in range(0, count, block):
        same = column(dest_row, start) == dest_row
        later = (own + start) < other
        rank_row = rank_row + jnp.sum(
            jnp.where(same & later, 1.0, 0.0), axis=0, keepdims=True
        )
    for start in range(0, count, block):
        code = jnp.where(lane < HIGH, column(high_row, start), column(low_row, start))
        coded.append(jnp.where(column(rank_row, start) == lane_rank, code, 0.0).astype(BF16))
    to_device = (
        lax.broadcasted_iota(jnp.int32, (devices, count), 0).astype(F32) == dest_row
    )
    pixels = dot(
        jnp.where(to_device, 1.0, 0.0).astype(BF16), jnp.concatenate(coded, axis=0)
    )
    out_ref[:, 2 * capacity :, :] = jnp.broadcast_to(
        pixels[:, None, :], (devices, PIXEL_ROWS, 128)
    ).astype(BF16)
    slot_row = dest_row * capacity + rank_row
    slots = 512
    per_block = slots // capacity
    loads[2].wait()
    values = values_ref[...]
    stores = []
    slot_at = lax.broadcasted_iota(jnp.int32, (slots, count), 0).astype(F32)
    for start in range(0, devices * capacity, slots):
        onehot = jnp.where(slot_at == slot_row - start, 1.0, 0.0).astype(BF16)
        rows = dot(onehot, values).astype(BF16)
        first = start // capacity
        for half in range(2):
            out_ref[first : first + per_block, half * capacity : (half + 1) * capacity, :] = (
                rows[:, half * 128 : (half + 1) * 128].reshape(per_block, capacity, 128)
            )
        store = pltpu.make_async_copy(
            out_ref.at[first : first + per_block],
            out_hbm.at[first : first + per_block],
            out_sem.at[len(stores)],
        )
        store.start()
        stores.append(store)
    for store in stores:
        store.wait()


def end_rows(rows, x_ends, c_ends, pair_ends, cross_ends):
    prev, after = [], []
    even = is_even()
    for side in range(2):
        pair, cross = pair_ends[side], cross_ends[side]
        prev.append(jnp.where(even, cross, pair))
        after.append(jnp.where(even, pair, cross))
    outside = {}
    for array, own in enumerate((x_ends, c_ends)):
        for side in range(2):
            for band in range(2):
                plane = 2 * array + band
                fold = own[side][(1 - band) * rows + rows - 1]
                outside[array, side, 2 * band] = prev[side][plane]
                outside[array, side, 2 * band + 1] = jnp.where(is_last(), fold, after[side][plane])
    return outside


def edge_body(rows, x_lo, x_hi, c_lo, c_hi, a_lo, a_hi, b_lo, b_hi, out_ref):
    out_ref[...] = jnp.zeros_like(out_ref)
    wide = lambda refs: [ref[...].astype(F32) for ref in refs]
    x_ends, c_ends = wide((x_lo, x_hi)), wide((c_lo, c_hi))
    outside = end_rows(rows, x_ends, c_ends, wide((a_lo, a_hi)), wide((b_lo, b_hi)))
    for array, own in enumerate((x_ends, c_ends)):
        for side in range(2):
            at = 0 if side == 0 else own[side].shape[1] - 1
            for band in range(2):
                base = band * GROUP
                out_ref[array, side, base, :] = outside[array, side, 2 * band][at]
                for r in range(rows):
                    out_ref[array, side, base + 1 + r, :] = own[side][band * rows + r, at]
                out_ref[array, side, base + 1 + rows, :] = outside[array, side, 2 * band + 1][at]


def row_groups(rows, way):
    first, last = ((0, 0), (1, rows - 1)), ((0, rows - 1), (1, 0))
    if way < 0:
        first, last = last, first
    inner = tuple((b, r) for b in range(2) for r in range(1, rows - 1))
    return ((inner, (-1, 0, 1)), (first, (0, 1)), (last, (-1, 0)))


def border_index(j, rows):
    return (j // 2) * rows + (j % 2) * (rows - 1)


def border_row(j, rows):
    return (j // 2) * rows + lax.rem(j, 2) * (rows - 1)


def lift_body(
    rows, x_in, c_in, k1_in, k2_in, b1_ref, pre_out, grad_out, k1t_ref, k2t_ref, x_ref, c_ref, k1_ref,
    k2_ref, cat, held_rows, sem,
):
    width, channels = x_ref.shape[1], x_ref.shape[2]
    lifted = k1_ref.shape[2]
    used = [0]

    def slot():
        used[0] += 1
        return sem.at[used[0] - 1]

    loads = [
        pltpu.make_async_copy(source, target, slot())
        for source, target in ((x_in, x_ref), (k1_in, k1_ref), (k2_in, k2_ref), (c_in, c_ref))
    ]
    for load in loads:
        load.start()
    stores = []
    for array, (source, weights, order, out) in enumerate(
        ((x_ref, k1_ref, (-1, 0, 1), pre_out), (c_ref, k2t_ref, (1, 0, -1), grad_out))
    ):
        way = 1 - 2 * array
        loads[2 * array].wait()
        loads[2 * array + 1].wait()
        if array == 1:
            for t in range(k2_ref.shape[0]):
                k2t_ref[t] = k2_ref[t].astype(F32).T.astype(BF16)
        for i in range(2 * rows):
            cat[array, i] = spread_columns(source[i], order)
        inner, first, last = row_groups(rows, way)
        half = len(inner[0]) // 2
        groups = ((inner[0][:half], inner[1]), (inner[0][half:], inner[1]), first, last)
        for members, steps in groups:
            lhs = jnp.concatenate(
                [
                    jnp.concatenate(
                        [cat[array, b * rows + r + way * (1 - 2 * b) * dy] for dy in steps], axis=1
                    )
                    for b, r in members
                ],
                axis=0,
            )
            taps = weights[3 * (steps[0] + 1) : 3 * (steps[-1] + 2)]
            total = dot(lhs, taps.reshape(3 * len(steps) * channels, lifted))
            if array == 0:
                total = total + b1_ref[...]
            for k, (b, r) in enumerate(members):
                i = b * rows + r
                held_rows[array, i] = total[k * width : (k + 1) * width]
                store = pltpu.make_async_copy(held_rows.at[array, i], out.at[i], slot())
                store.start()
                stores.append(store)
    for t in range(k1_ref.shape[0]):
        k1t_ref[t] = k1_ref[t].astype(F32).T.astype(BF16)
    for store in stores:
        store.wait()


def row_onehot(keys, row, width):
    column = lax.broadcasted_iota(jnp.int32, (width, keys.shape[1]), 0).astype(F32)
    return jnp.where(column == keys[0:1, :] - float(row * width), 1.0, 0.0).astype(BF16)


def rim_in_body(
    rows, matching_ref, k1_in, k2t_in, pre_lo, pre_hi, grad_lo, grad_hi, x_lo, x_hi, c_lo, c_hi,
    a_lo, a_hi, b_lo, b_hi, base_ref, taps_ref, k1_ref, k2t_ref, sem,
):
    loads = [
        pltpu.make_async_copy(k1_in, k1_ref, sem.at[0]),
        pltpu.make_async_copy(k2t_in, k2t_ref, sem.at[1]),
    ]
    for load in loads:
        load.start()
    for load in loads:
        load.wait()
    face = lax.axis_index("face")
    for side in range(2):
        their_side, flipped = matching_ref[face, side, 1], matching_ref[face, side, 2]
        for row in range(3):
            taps_ref[0, side, row] = k1_ref[3 * row + 2 * side]
            turned = jnp.where(flipped == 1, 2 - row, row)
            taps_ref[1, side, row] = k2t_ref[3 * turned + 2 * their_side]
    whole = lambda refs: [ref[...] for ref in refs]
    x_ends, c_ends = whole((x_lo, x_hi)), whole((c_lo, c_hi))
    outside = end_rows(rows, x_ends, c_ends, whole((a_lo, a_hi)), whole((b_lo, b_hi)))
    channels, lifted = k1_ref.shape[1], k1_ref.shape[2]
    base_ref[...] = jnp.zeros_like(base_ref)
    for array, (strips, weights, order) in enumerate(
        (((pre_lo, pre_hi), k1_ref, (-1, 0, 1)), ((grad_lo, grad_hi), k2t_ref, (1, 0, -1)))
    ):
        for side in range(2):
            spot = 0 if side == 0 else GROUP - 1
            for b in range(2):
                for r in range(rows):
                    at = 2 * GROUP * side + GROUP * b + r + 1
                    base_ref[array, at : at + 1, :] = strips[side][
                        b * rows + r, spot : spot + 1, :
                    ]
        for pair in ((0, 3), (1, 2)):
            spots = [(side, j) for side in range(2) for j in pair]
            lhs = [spread_columns(outside[array, side, j], order) for side, j in spots]
            row = 0 if (pair[0] == 0) == (array == 0) else 6
            found = dot(
                jnp.concatenate(lhs, axis=0), weights[row : row + 3].reshape(3 * channels, lifted)
            )
            strip = found.shape[0] // len(spots)
            for k, (side, j) in enumerate(spots):
                at = 2 * GROUP * side + GROUP * (j // 2) + 1 + (rows - 1) * (j % 2)
                spot = k * strip + (0 if side == 0 else strip - 1)
                base_ref[array, at : at + 1, :] += found[spot : spot + 1]


def rim_body(rows, faces, matching_ref, taps_ref, base_ref, found_ref, *rest):
    parts = rest[:faces]
    x_side, c_side, edge_ref = rest[faces:]
    taps = taps_ref[...].reshape(2, 2, 3 * taps_ref.shape[3], taps_ref.shape[4])
    for side in range(2):
        hop, their_side, flipped = matched(matching_ref, side, faces)
        for array, out in enumerate((x_side, c_side)):
            near = partner_rows(parts, array, hop, their_side, flipped)
            way = 1 - 2 * array
            lhs = jnp.concatenate([rolled_rows(near, way * dy) for dy in (-1, 0, 1)], axis=1)
            out[side] = dot(lhs, taps[array, side])
    e = lax.broadcasted_iota(jnp.int32, (4 * GROUP, 1), 0) & (GROUP - 1)
    inside = (e >= 1) & (e <= rows)
    shape = base_ref.shape[1:]
    v = base_ref[0] + x_side[...].reshape(shape) + found_ref[...]
    inner, gp = gelu_pair(v, base_ref[1] + c_side[...].reshape(shape))
    edge_ref[0] = jnp.where(inside, inner.astype(F32), 0.0).reshape(edge_ref.shape[1:])
    edge_ref[1] = jnp.where(inside, gp.astype(F32), 0.0).reshape(edge_ref.shape[1:])


def gelu_pair(v, grad):
    square = v * v
    t = jnp.tanh(v * (ROOT + (ROOT * CUBIC) * square))
    half = 0.5 + 0.5 * t
    slope = half + (0.5 * v) * (1.0 - t * t) * (ROOT + (3.0 * ROOT * CUBIC) * square)
    return (v * half).astype(BF16), (grad * slope).astype(BF16)


def unpack_received(capacity, recv_ref, values, keys):
    devices = recv_ref.shape[0]
    slots = devices * capacity
    per_lane = 128 // capacity
    for half in range(2):
        values[:, half * 128 : (half + 1) * 128] = recv_ref[
            :, half * capacity : (half + 1) * capacity, :
        ].reshape(slots, 128)
    owner = lax.broadcasted_iota(jnp.int32, (PIXEL_ROWS, 128), 1) // capacity
    for start in range(0, devices, per_lane):
        key = jnp.zeros((PIXEL_ROWS, 128), F32)
        for k in range(per_lane):
            code = recv_ref[start + k, 2 * capacity :, :].astype(F32)
            mine = (code - 1.0) * HIGH + pltpu.roll(code, HIGH, 1)
            if k:
                mine = pltpu.roll(mine, k * capacity, 1)
            key = jnp.where(owner == k, mine, key)
        keys[:, start * capacity : start * capacity + 128] = key


def row_taps(taps_ref, row):
    return jnp.concatenate([taps_ref[3 * row + dx] for dx in range(3)], axis=1)


def merge_shifts(wide, forward):
    channels = wide.shape[1] // 3
    left, mid, right = (wide[:, k * channels : (k + 1) * channels] for k in range(3))
    step = -1 if forward else 1
    return mid + shift_columns(left, step) + shift_columns(right, -step)


def found_body(
    rows, capacity, recv_in, pre_in, grad_in, k1_in, k2t_in, values, keys, pre_b, grad_b, found_b, rim_ref,
    taps, recv_ref, sem,
):
    width = pre_b.shape[1]
    loads = [pltpu.make_async_copy(recv_in, recv_ref, sem.at[0])]
    for j in range(4):
        row = border_index(j, rows)
        loads.append(pltpu.make_async_copy(pre_in.at[row], pre_b.at[j], sem.at[1 + j]))
    for j in range(4):
        row = border_index(j, rows)
        loads.append(pltpu.make_async_copy(grad_in.at[row], grad_b.at[j], sem.at[5 + j]))
    for array, source in enumerate((k1_in, k2t_in)):
        for k in range(2):
            loads.append(
                pltpu.make_async_copy(
                    source.at[6 * k : 6 * k + 3], taps.at[array, k], sem.at[9 + 2 * array + k]
                )
            )
    for load in loads:
        load.start()
    loads[0].wait()
    unpack_received(capacity, recv_ref, values, keys)
    at = lax.broadcasted_iota(jnp.int32, (4 * GROUP, 1), 0)
    e = at & (GROUP - 1)
    b = (at // GROUP) & 1
    side = at // (2 * GROUP)
    inside = (e >= 1) & (e <= rows)
    pixel = (b * rows + e - 1) * width + side * (width - 1)
    wanted = jnp.where(inside, pixel, -1).astype(F32)
    onehot = jnp.where(keys[0:1, :] == wanted, 1.0, 0.0).astype(BF16)
    rim_ref[...] = dot(onehot, values[...])
    for half in range(2):
        members = (2 * half, 2 * half + 1)
        found = dot(
            jnp.concatenate(
                [row_onehot(keys, border_index(j, rows), width) for j in members], axis=0
            ),
            values[...],
        )
        for k, j in enumerate(members):
            found_b[j] = found[k * width : (k + 1) * width]
    for load in loads[1:]:
        load.wait()


def border_body(
    rows, pre_b, grad_b, found_b, taps, x_side, c_side, a_in, b_in, x_in, c_in, inner_ref, gp_ref, outside,
    sem,
):
    width, lifted = inner_ref.shape[1], inner_ref.shape[2]
    channels = outside.shape[3]
    even, last = is_even(), is_last()
    waits = [[], []]
    used = [0]

    def load(array, target, *sources):
        slot = sem.at[used[0]]
        used[0] += 1
        for condition, source in sources:
            copy = pltpu.make_async_copy(source, target, slot)
            pl.when(condition)(copy.start)
        waits[array].append(copy)

    for array, source in enumerate((x_in, c_in)):
        for j in range(4):
            band = j // 2
            plane = 2 * array + band
            if j % 2 == 0:
                choices = ((even, b_in.at[plane]), (jnp.logical_not(even), a_in.at[plane]))
            else:
                fold = source.at[(1 - band) * rows + rows - 1]
                middle = jnp.logical_not(even) & jnp.logical_not(last)
                choices = ((last, fold), (even, a_in.at[plane]), (middle, b_in.at[plane]))
            load(array, outside.at[array, j], *choices)

    for copy in waits[0] + waits[1]:
        copy.wait()
    for pair in ((0, 3), (1, 2)):
        totals = []
        for array, order in enumerate(((-1, 0, 1), (1, 0, -1))):
            lhs = [spread_columns(outside[array, j], order) for j in pair]
            tap = taps[array, 0 if (pair[0] == 0) == (array == 0) else 1]
            totals.append(dot(jnp.concatenate(lhs, axis=0), tap.reshape(3 * channels, lifted)))
        for k, j in enumerate(pair):
            at = GROUP * (j // 2) + 1 + (rows - 1) * (j % 2)
            piece = slice(k * width, (k + 1) * width)
            inner, gp = gelu_pair(
                add_edges(
                    totals[0][piece] + (pre_b[j] + found_b[j]),
                    x_side[0, at : at + 1, :],
                    x_side[1, at : at + 1, :],
                ),
                add_edges(
                    totals[1][piece] + grad_b[j], c_side[0, at : at + 1, :], c_side[1, at : at + 1, :]
                ),
            )
            inner_ref[j] = inner
            gp_ref[j] = gp


def send_rows(rows, inner_ref, gp_ref, k2_ref, k1t_ref, side_ref, out_ref, bottom):
    width = inner_ref.shape[1]
    for array, (source, taps) in enumerate(((inner_ref, k2_ref), (gp_ref, k1t_ref))):
        for band in range(2):
            tap = jnp.where((bottom == band) == (array == 0), 2, 0)
            wide = dot(source[2 * band + bottom], row_taps(taps, tap))
            corner = GROUP * band + (rows + 1) * bottom
            part = add_edges(
                merge_shifts(wide, array == 0),
                side_ref[array, 0, pl.ds(corner, 1), :],
                side_ref[array, 1, pl.ds(corner, 1), :],
            )
            out_ref[2 * array + band] = part.astype(BF16)


def cross_body(rows, faces, matching_ref, inner_ref, gp_ref, k2_ref, k1t_ref, *rest):
    parts = rest[:faces]
    cross_ref, side_ref = rest[faces:]
    for side in range(2):
        hop, their_side, flipped = matched(matching_ref, side, faces)
        near = partner_rows(parts, 0, hop, their_side, flipped)
        side_ref[0, side] = side_forward(near, side, k2_ref)
        near = partner_rows(parts, 1, hop, their_side, flipped)
        side_ref[1, side] = side_adjoint(near, their_side, flipped, k1t_ref)
    bottom = jnp.where(is_even(), 0, 1)
    send_rows(rows, inner_ref, gp_ref, k2_ref, k1t_ref, side_ref, cross_ref, bottom)


def pair_body(rows, _, inner_ref, gp_ref, k2_ref, k1t_ref, side_ref, pair_ref):
    bottom = jnp.where(is_even(), 1, 0)
    send_rows(rows, inner_ref, gp_ref, k2_ref, k1t_ref, side_ref, pair_ref, bottom)


def middle_body(
    rows, _, values, keys, pre_in, grad_in, x_side, c_side, inner_ref, gp_ref, base, sem
):
    middle = rows - 2
    width = base.shape[2]
    members = [(b, r) for b in range(2) for r in range(1, rows - 1)]
    loads = []
    for k in range(len(members)):
        for array, source in enumerate((pre_in, grad_in)):
            row = members[k][0] * rows + members[k][1]
            load = pltpu.make_async_copy(source.at[row], base.at[array, k], sem.at[2 * k + array])
            load.start()
            loads.append(load)
    found = dot(
        jnp.concatenate([row_onehot(keys, b * rows + r, width) for b, r in members], axis=0),
        values[...],
    )
    for k, (b, r) in enumerate(members):
        at = b * GROUP + r + 1
        loads[2 * k].wait()
        loads[2 * k + 1].wait()
        inner, gp = gelu_pair(
            add_edges(
                base[0, k] + found[k * width : (k + 1) * width],
                x_side[0, at : at + 1, :],
                x_side[1, at : at + 1, :],
            ),
            add_edges(base[1, k], c_side[0, at : at + 1, :], c_side[1, at : at + 1, :]),
        )
        inner_ref[k] = inner
        gp_ref[k] = gp


def inside_body(
    rows, inner_b, gp_b, inner_m, gp_m, side_ref, k2_ref, k1t_ref, b2_ref, x_ref, c_ref, ana_out, ana_b,
    grad_out, grad_b, ana_rows, grad_rows, sem,
):
    width, channels = x_ref.shape[1], x_ref.shape[2]
    middle = rows - 2
    stores = []
    for array, (border, inner, taps) in enumerate(
        ((inner_b, inner_m, k2_ref), (gp_b, gp_m, k1t_ref))
    ):
        way = 1 - 2 * array

        def plane(b, r):
            if r == 0 or r == rows - 1:
                return border[2 * b + r // (rows - 1)]
            return inner[middle * b + r - 1]

        for members, steps in row_groups(rows, way):
            lhs = jnp.concatenate(
                [
                    jnp.concatenate(
                        [plane(b, r + way * (1 - 2 * b) * dy) for dy in steps], axis=1
                    )
                    for b, r in members
                ],
                axis=0,
            )
            wide = dot(lhs, jnp.concatenate([row_taps(taps, dy + 1) for dy in steps], axis=0))
            for k, (b, r) in enumerate(members):
                i = b * rows + r
                at = b * GROUP + r + 1
                total = merge_shifts(wide[k * width : (k + 1) * width], array == 0)
                total = add_edges(
                    total + (x_ref, c_ref)[array][i].astype(F32),
                    side_ref[array, 0, at : at + 1, :],
                    side_ref[array, 1, at : at + 1, :],
                )
                if array == 0:
                    total = total + b2_ref[...]
                if len(steps) == 2:
                    (ana_b, grad_b)[array][2 * b + r // (rows - 1)] = total
                    continue
                held_rows, out = ((ana_rows, ana_out), (grad_rows, grad_out))[array]
                held_rows[k] = total.astype(held_rows.dtype)
                store = pltpu.make_async_copy(held_rows.at[k], out.at[i], sem.at[len(stores)])
                store.start()
                stores.append(store)
    for store in stores:
        store.wait()


def final_body(
    rows, ana_b, grad_b, own_ref, pair_ref, cross_ref, _, __, ana_out, grad_out, ana_rows, grad_rows, sem
):
    even, last = is_even(), is_last()
    stores = []
    for array, (acc, held_rows, out) in enumerate(
        ((ana_b, ana_rows, ana_out), (grad_b, grad_rows, grad_out))
    ):
        for j in range(4):
            band = j // 2
            plane = 2 * array + band
            if j % 2:
                add = jnp.where(even, pair_ref[plane], cross_ref[plane])
                add = jnp.where(last, own_ref[2 * array + 1 - band], add)
            else:
                add = jnp.where(even, cross_ref[plane], pair_ref[plane])
            held_rows[j] = (acc[j] + add.astype(F32)).astype(held_rows.dtype)
            store = pltpu.make_async_copy(
                held_rows.at[j], out.at[border_index(j, rows)], sem.at[len(stores)]
            )
            store.start()
            stores.append(store)
    for store in stores:
        store.wait()


def per_device(
    state,
    obs_values,
    obs_dest,
    obs_pixel,
    matching,
    kernel_one,
    bias_one,
    kernel_two,
    bias_two,
    cotangent,
):
    rows, width, channels = state.shape[3], state.shape[4], state.shape[5]
    lifted = kernel_one.shape[2]
    tiles, faces = lax.axis_size("tile"), lax.axis_size("face")
    devices = tiles * faces
    count = obs_values.shape[0]
    capacity = 2 * count // devices
    all_rows = 2 * rows
    middle = rows - 2
    chunk = 2 * capacity + PIXEL_ROWS
    x = state.reshape(all_rows, width, channels)
    c = cotangent.reshape(all_rows, width, channels)
    even = is_even()
    pairs = [(i, i ^ 1) for i in range(tiles)]
    crosses = [(i, i + 1 if i % 2 else i - 1) for i in range(1, tiles - 1)]
    strip = 16

    def ends(at):
        fields = [field.reshape(2, rows, width, channels) for field in (x, c)]
        picked = [
            jnp.concatenate(
                [
                    lax.dynamic_slice(field, (0, at, start, 0), (2, 1, strip, channels))[:, 0]
                    for start in (0, width - strip)
                ],
                axis=1,
            )
            for field in fields
        ]
        return jnp.concatenate(picked, axis=0)

    pair_ends = lax.ppermute(ends(jnp.where(even, rows - 1, 0)), "tile", pairs)
    cross_ends = lax.ppermute(ends(jnp.where(even, 0, rows - 1)), "tile", crosses)
    low_row = lambda field, at: lax.dynamic_index_in_dim(
        field.reshape(2, rows, width, channels), at, 1, keepdims=False
    )
    border_rows = lambda at: jnp.concatenate([low_row(x, at), low_row(c, at)], axis=0)
    pair_out = border_rows(jnp.where(even, rows - 1, 0))
    cross_out = border_rows(jnp.where(even, 0, rows - 1))
    smem = pl.BlockSpec(memory_space=pltpu.SMEM)
    vmem = pl.BlockSpec(memory_space=pltpu.VMEM)
    hbm = pl.BlockSpec(memory_space=pl.ANY)

    def exchange(own):
        parts = [own]
        for k in range(1, faces):
            parts.append(
                lax.ppermute(own, "face", [((i + k) % faces, i) for i in range(faces)])
            )
        return parts

    packed = pl.pallas_call(
        functools.partial(pack_body, capacity),
        in_specs=[hbm] * 3,
        out_specs=hbm,
        out_shape=pltpu.HBM((devices, chunk, 128), BF16),
        scratch_shapes=[
            pltpu.VMEM((1, count), jnp.int32),
            pltpu.VMEM((1, count), jnp.int32),
            pltpu.VMEM((count, lifted), BF16),
            pltpu.VMEM((devices, chunk, 128), BF16),
            pltpu.SemaphoreType.DMA((3,)),
            pltpu.SemaphoreType.DMA((devices * capacity // 512,)),
        ],
        compiler_params=params(16),
        cost_estimate=cost(2 * devices * capacity * count * lifted, 2 << 20),
        name="pack",
    )(far(obs_dest.reshape(1, count)), far(obs_pixel.reshape(1, count)), far(obs_values))
    received = lax.all_to_all(packed, ("tile", "face"), 0, 0, tiled=True)

    b1 = bias_one.reshape(1, lifted)
    b2 = bias_two.reshape(1, channels)
    row_block = lambda n: pl.BlockSpec((1, width, n), lambda i: (i, 0, 0))
    edge_block = lambda n: pl.BlockSpec((1, width, n), lambda i: (border_row(i, rows), 0, 0))
    conv_flops = 2 * 9 * all_rows * width * channels * lifted
    plane = (4, width, channels)
    pre, grad_inner, k1t, k2t = pl.pallas_call(
        functools.partial(lift_body, rows),
        in_specs=[hbm] * 4 + [vmem],
        out_specs=[hbm] * 2 + [vmem] * 2,
        out_shape=[pltpu.HBM((all_rows, width, lifted), F32)] * 2
        + [pltpu.HBM(kernel_two.shape, BF16), pltpu.HBM(kernel_one.shape, BF16)],
        scratch_shapes=[
            pltpu.VMEM(x.shape, BF16),
            pltpu.VMEM(c.shape, BF16),
            pltpu.VMEM(kernel_one.shape, BF16),
            pltpu.VMEM(kernel_two.shape, BF16),
            pltpu.VMEM((2, all_rows, width, 3 * channels), BF16),
            pltpu.VMEM((2, all_rows, width, lifted), F32),
            pltpu.SemaphoreType.DMA((4 + 2 * all_rows,)),
        ],
        compiler_params=params(40),
        cost_estimate=cost(conv_flops, 8 << 20),
        name="lift",
    )(far(x), far(c), far(kernel_one), far(kernel_two), b1)
    pre, grad_inner = far(pre), far(grad_inner)
    pair_out, cross_out, pair_ends, cross_ends, k1t = lax.optimization_barrier(
        (pair_out, cross_out, pair_ends, cross_ends, k1t)
    )
    pair_rows = lax.ppermute(pair_out, "tile", pairs)
    cross_rows = lax.ppermute(cross_out, "tile", crosses)
    low = lambda n: pl.BlockSpec((n, strip, channels), lambda *_: (0, 0, 0))
    high = lambda n, at: pl.BlockSpec((n, strip, channels), lambda *_: (0, at, 0))
    tail = width // strip - 1
    edge_shape = (2, 2, 2 * GROUP, channels)
    edges = pl.pallas_call(
        functools.partial(edge_body, rows),
        grid=(1,),
        in_specs=[low(all_rows), high(all_rows, tail)] * 2 + [low(4), high(4, 1)] * 2,
        out_specs=fixed(edge_shape),
        out_shape=jax.ShapeDtypeStruct(edge_shape, F32),
        compiler_params=params(8),
        cost_estimate=cost(0, 1 << 18),
        name="edges",
    )(x, x, c, c, pair_ends, pair_ends, cross_ends, cross_ends)
    parts = exchange(edges)

    side_in = (2, 2 * GROUP, lifted)
    end = width // GROUP - 1
    edge_strip = lambda at: pl.BlockSpec((all_rows, GROUP, lifted), lambda *_: (0, at, 0))
    rim_shape = (2, 4 * GROUP, lifted)
    taps_shape = (2, 2, 3, channels, lifted)
    rim_base, side_taps = pl.pallas_call(
        functools.partial(rim_in_body, rows),
        grid=(1,),
        in_specs=[smem, hbm, hbm]
        + [edge_strip(0), edge_strip(end)] * 2
        + [low(all_rows), high(all_rows, tail)] * 2
        + [low(4), high(4, 1)] * 2,
        out_specs=[fixed(rim_shape), fixed(taps_shape)],
        out_shape=[jax.ShapeDtypeStruct(rim_shape, F32), jax.ShapeDtypeStruct(taps_shape, BF16)],
        scratch_shapes=[
            pltpu.VMEM(kernel_one.shape, BF16),
            pltpu.VMEM(k2t.shape, BF16),
            pltpu.SemaphoreType.DMA((2,)),
        ],
        compiler_params=params(8),
        cost_estimate=cost(0, 2 << 20),
        name="rim_in",
    )(
        matching, far(kernel_one), far(k2t), pre, pre, grad_inner, grad_inner, x, x, c, c, pair_ends,
        pair_ends, cross_ends, cross_ends,
    )
    side_two = (2, 2, 2 * GROUP, lifted)
    slots = devices * capacity
    onehot_flops = 2 * width * slots * lifted
    other_block = pl.BlockSpec(
        (1, width, channels), lambda j: ((1 - j // 2) * rows + rows - 1, 0, 0)
    )
    values, keys, pre_b, grad_b, found_b, rim_found, rim_taps = pl.pallas_call(
        functools.partial(found_body, rows, capacity),
        in_specs=[hbm] * 5,
        out_specs=[vmem] * 7,
        out_shape=[
            hold((slots, lifted), BF16),
            hold((PIXEL_ROWS, slots), F32),
            hold((4, width, lifted), F32),
            hold((4, width, lifted), F32),
            hold((4, width, lifted), F32),
            hold(rim_shape[1:], F32),
            hold((2, 2, 3, channels, lifted), BF16),
        ],
        scratch_shapes=[
            pltpu.VMEM(received.shape, BF16),
            pltpu.SemaphoreType.DMA((13,)),
        ],
        compiler_params=params(),
        cost_estimate=cost(4 * onehot_flops, 6 << 20),
        name="found",
    )(far(received), pre, grad_inner, far(kernel_one), far(k2t))
    values, keys, pre_b, grad_b = held(values), held(keys), held(pre_b), held(grad_b)
    found_b = held(found_b)
    x_side, c_side, edges_two = pl.pallas_call(
        functools.partial(rim_body, rows, faces),
        in_specs=[smem] + [vmem] * (3 + faces),
        out_specs=[vmem] * 3,
        out_shape=[
            hold(side_in, F32),
            hold(side_in, F32),
            jax.ShapeDtypeStruct(side_two, F32),
        ],
        compiler_params=params(8),
        cost_estimate=cost(0, 1 << 20),
        name="rim",
    )(matching, side_taps, rim_base, held(rim_found), *parts)
    x_side, c_side = held(x_side), held(c_side)
    parts_two = exchange(edges_two)

    border_shape = hold((4, width, lifted), BF16)
    inner_b, gp_b = pl.pallas_call(
        functools.partial(border_body, rows),
        in_specs=[vmem] * 6 + [hbm] * 4,
        out_specs=[vmem] * 2,
        out_shape=[border_shape] * 2,
        scratch_shapes=[
            pltpu.VMEM((2, 4, width, channels), BF16),
            pltpu.SemaphoreType.DMA((8,)),
        ],
        compiler_params=params(),
        cost_estimate=cost(conv_flops // 6, 4 << 20),
        name="border",
    )(
        pre_b, grad_b, found_b, held(rim_taps), x_side, c_side, far(pair_rows), far(cross_rows), far(x),
        far(c),
    )
    inner_b, gp_b = held(inner_b), held(gp_b)

    side_out = (2, 2, 2 * GROUP, channels)
    to_cross, sides = pl.pallas_call(
        functools.partial(cross_body, rows, faces),
        in_specs=[smem] + [vmem] * (4 + faces),
        out_specs=[vmem] * 2,
        out_shape=[jax.ShapeDtypeStruct(plane, BF16), jax.ShapeDtypeStruct(side_out, F32)],
        compiler_params=params(16),
        cost_estimate=cost(conv_flops // 12, 3 << 20),
        name="send_cross",
    )(matching, inner_b, gp_b, kernel_two, k1t, *parts_two)
    from_cross = lax.ppermute(to_cross, "tile", crosses)
    to_pair = pl.pallas_call(
        functools.partial(pair_body, rows),
        in_specs=[hbm] + [vmem] * 5,
        out_specs=vmem,
        out_shape=jax.ShapeDtypeStruct(plane, BF16),
        compiler_params=params(16),
        cost_estimate=cost(conv_flops // 12, 3 << 20),
        name="send_pair",
    )(to_cross, inner_b, gp_b, kernel_two, k1t, sides)
    from_pair = lax.ppermute(to_pair, "tile", pairs)

    inner_m, gp_m = pl.pallas_call(
        functools.partial(middle_body, rows),
        in_specs=[hbm, vmem, vmem, hbm, hbm, vmem, vmem],
        out_specs=[vmem] * 2,
        out_shape=[hold((2 * middle, width, lifted), BF16)] * 2,
        scratch_shapes=[
            pltpu.VMEM((2, 2 * middle, width, lifted), F32),
            pltpu.SemaphoreType.DMA((4 * middle,)),
        ],
        compiler_params=params(32),
        cost_estimate=cost(2 * middle * onehot_flops, 10 << 20),
        name="middle",
    )(to_pair, values, keys, pre, grad_inner, x_side, c_side)
    inner_m, gp_m = held(inner_m), held(gp_m)

    analysis, ana_b, grad_state, grad_b = pl.pallas_call(
        functools.partial(inside_body, rows),
        in_specs=[vmem] * 10,
        out_specs=[hbm, vmem, hbm, vmem],
        out_shape=[
            pltpu.HBM((all_rows, width, channels), BF16),
            hold(plane, F32),
            pltpu.HBM((all_rows, width, channels), F32),
            hold(plane, F32),
        ],
        scratch_shapes=[
            pltpu.VMEM((2 * middle, width, channels), BF16),
            pltpu.VMEM((2 * middle, width, channels), F32),
            pltpu.SemaphoreType.DMA((4 * middle,)),
        ],
        compiler_params=params(),
        cost_estimate=cost(2 * conv_flops, 14 << 20),
        name="inside",
    )(inner_b, gp_b, inner_m, gp_m, sides, kernel_two, k1t, b2, x, c)
    ana_b, grad_b = held(ana_b), held(grad_b)

    analysis, grad_state = pl.pallas_call(
        functools.partial(final_body, rows),
        in_specs=[vmem] * 5 + [hbm] * 2,
        out_specs=[hbm] * 2,
        out_shape=[
            pltpu.HBM((all_rows, width, channels), BF16),
            pltpu.HBM((all_rows, width, channels), F32),
        ],
        scratch_shapes=[
            pltpu.VMEM(plane, BF16),
            pltpu.VMEM(plane, F32),
            pltpu.SemaphoreType.DMA((8,)),
        ],
        input_output_aliases={5: 0, 6: 1},
        compiler_params=params(16),
        cost_estimate=cost(0, 6 << 20),
        name="final",
    )(ana_b, grad_b, to_cross, from_pair, from_cross, far(analysis), far(grad_state))
    return analysis.reshape(state.shape), grad_state.reshape(cotangent.shape)


def solution(mesh):
    return jax.shard_map(
        per_device,
        mesh=mesh,
        in_specs=(
            P("face", "tile", None, None, None, None),
            P(("face", "tile"), None),
            P(("face", "tile"), None),
            P(("face", "tile")),
            P(),
            P(),
            P(),
            P(),
            P(),
            P("face", "tile", None, None, None, None),
        ),
        out_specs=(
            P("face", "tile", None, None, None, None),
            P("face", "tile", None, None, None, None),
        ),
        check_vma=False,
    )
```

```python
import functools
import math

import jax
import jax.numpy as jnp
from jax import lax
from jax.experimental import pallas as pl
from jax.experimental.pallas import tpu as pltpu
from jax.sharding import PartitionSpec as P

F32 = jnp.float32
BF16 = jnp.bfloat16
GROUP = 8
HIGH = 64
PIXEL_ROWS = 8
ROOT = math.sqrt(2.0 / math.pi)
CUBIC = 0.044715


def params(mib=24):
    return pltpu.CompilerParams(vmem_limit_bytes=mib << 20)


def cost(flops, nbytes):
    return pl.CostEstimate(flops=int(flops), bytes_accessed=int(nbytes), transcendentals=0)


def hold(shape, kind):
    return pltpu.VMEM(shape, kind)


def held(array):
    return pltpu.with_memory_space_constraint(array, pltpu.VMEM)


def far(array):
    return pltpu.with_memory_space_constraint(array, pltpu.HBM)


def fixed(shape):
    return pl.BlockSpec(shape, lambda *_: (0,) * len(shape))


def dot(a, b):
    return jnp.dot(a, b, preferred_element_type=F32)


def matched(matching_ref, side, faces):
    face = lax.axis_index("face")
    partner = matching_ref[face, side, 0]
    return lax.rem(partner - face + faces, faces), matching_ref[face, side, 1], matching_ref[face, side, 2]


def is_even():
    return lax.rem(lax.axis_index("tile"), 2) == 0


def is_last():
    return lax.axis_index("tile") == lax.axis_size("tile") - 1


def partner_rows(part_refs, array, hop, their_side, flipped):
    rows = None
    for k, ref in enumerate(part_refs):
        mine = jnp.where(their_side == 1, ref[array, 1], ref[array, 0])
        rows = mine if rows is None else jnp.where(hop == k, mine, rows)
    swapped = jnp.concatenate([rows[GROUP:], rows[:GROUP]], axis=0)
    return jnp.where(flipped == 1, swapped, rows)


def rolled_rows(rows, step):
    first, second = rows[:GROUP], rows[GROUP:]
    if step:
        first = pltpu.roll(first, (-step) % GROUP, 0)
        second = pltpu.roll(second, step % GROUP, 0)
    return jnp.concatenate([first, second], axis=0).astype(BF16)


def side_forward(rows, side, taps_ref):
    lhs = jnp.concatenate([rolled_rows(rows, dy) for dy in (-1, 0, 1)], axis=1)
    taps = jnp.concatenate([taps_ref[3 * row + 2 * side] for row in range(3)], axis=0)
    return dot(lhs, taps)


def side_adjoint(rows, their_side, flipped, taps_ref):
    lhs = jnp.concatenate([rolled_rows(rows, -dy) for dy in (-1, 0, 1)], axis=1)
    order = [jnp.where(flipped == 1, 2 - row, row) for row in range(3)]
    taps = jnp.concatenate([taps_ref[3 * row + 2 * their_side] for row in order], axis=0)
    return dot(lhs, taps)


def shift_columns(values, step):
    count = values.shape[0]
    at = lax.broadcasted_iota(jnp.int32, values.shape, 0)
    moved = pltpu.roll(values, (-step) % count, 0)
    edge = count - 1 if step == 1 else 0
    return jnp.where(at == edge, 0.0, moved)


def spread_columns(row, order):
    wide = row.astype(F32)
    return jnp.concatenate(
        [row if s == 0 else shift_columns(wide, s).astype(BF16) for s in order], axis=1
    )


def add_edges(values, left, right):
    count = values.shape[0]
    at = lax.broadcasted_iota(jnp.int32, (GROUP, values.shape[1]), 0)
    first = values[:GROUP] + jnp.where(at == 0, left, 0.0)
    tail = values[count - GROUP :] + jnp.where(at == GROUP - 1, right, 0.0)
    return jnp.concatenate([first, values[GROUP : count - GROUP], tail], axis=0)


def pack_body(
    capacity, dest_in, pixel_in, values_in, out_hbm, dest_ref, pixel_ref, values_ref, out_ref, in_sem,
    out_sem,
):
    count = values_ref.shape[0]
    devices = out_ref.shape[0]
    block = 128
    loads = [
        pltpu.make_async_copy(source, target, in_sem.at[k])
        for k, (source, target) in enumerate(
            ((dest_in, dest_ref), (pixel_in, pixel_ref), (values_in, values_ref))
        )
    ]
    for load in loads:
        load.start()
    loads[0].wait()
    loads[1].wait()
    tiles, faces = lax.axis_size("tile"), lax.axis_size("face")
    dest = dest_ref[...]
    dest_face = dest // tiles
    dest_row = ((dest - dest_face * tiles) * faces + dest_face).astype(F32)
    pixel_row = pixel_ref[...]
    eye = lax.broadcasted_iota(jnp.int32, (block, block), 0) == lax.broadcasted_iota(
        jnp.int32, (block, block), 1
    )

    def column(row, start):
        piece = row[:, start : start + block]
        return jnp.sum(jnp.where(eye, piece, 0.0), axis=1, keepdims=True)

    high_row = lax.shift_right_logical(pixel_row, 6).astype(F32) + 1.0
    low_row = (pixel_row & (HIGH - 1)).astype(F32)
    own = lax.broadcasted_iota(jnp.int32, (block, count), 0)
    other = lax.broadcasted_iota(jnp.int32, (block, count), 1)
    lane = lax.broadcasted_iota(jnp.int32, (block, 128), 1)
    lane_rank = (lane & (HIGH - 1)).astype(F32)
    rank_row = jnp.zeros((1, count), F32)
    coded = []
    for start in range(0, count, block):
        same = column(dest_row, start) == dest_row
        later = (own + start) < other
        rank_row = rank_row + jnp.sum(
            jnp.where(same & later, 1.0, 0.0), axis=0, keepdims=True
        )
    for start in range(0, count, block):
        code = jnp.where(lane < HIGH, column(high_row, start), column(low_row, start))
        coded.append(jnp.where(column(rank_row, start) == lane_rank, code, 0.0).astype(BF16))
    to_device = (
        lax.broadcasted_iota(jnp.int32, (devices, count), 0).astype(F32) == dest_row
    )
    pixels = dot(
        jnp.where(to_device, 1.0, 0.0).astype(BF16), jnp.concatenate(coded, axis=0)
    )
    out_ref[:, 2 * capacity :, :] = jnp.broadcast_to(
        pixels[:, None, :], (devices, PIXEL_ROWS, 128)
    ).astype(BF16)
    slot_row = dest_row * capacity + rank_row
    slots = 512
    per_block = slots // capacity
    loads[2].wait()
    values = values_ref[...]
    stores = []
    slot_at = lax.broadcasted_iota(jnp.int32, (slots, count), 0).astype(F32)
    for start in range(0, devices * capacity, slots):
        onehot = jnp.where(slot_at == slot_row - start, 1.0, 0.0).astype(BF16)
        rows = dot(onehot, values).astype(BF16)
        first = start // capacity
        for half in range(2):
            out_ref[first : first + per_block, half * capacity : (half + 1) * capacity, :] = (
                rows[:, half * 128 : (half + 1) * 128].reshape(per_block, capacity, 128)
            )
        store = pltpu.make_async_copy(
            out_ref.at[first : first + per_block],
            out_hbm.at[first : first + per_block],
            out_sem.at[len(stores)],
        )
        store.start()
        stores.append(store)
    for store in stores:
        store.wait()


def end_rows(rows, x_ends, c_ends, pair_ends, cross_ends):
    prev, after = [], []
    even = is_even()
    for side in range(2):
        pair, cross = pair_ends[side], cross_ends[side]
        prev.append(jnp.where(even, cross, pair))
        after.append(jnp.where(even, pair, cross))
    outside = {}
    for array, own in enumerate((x_ends, c_ends)):
        for side in range(2):
            for band in range(2):
                plane = 2 * array + band
                fold = own[side][(1 - band) * rows + rows - 1]
                outside[array, side, 2 * band] = prev[side][plane]
                outside[array, side, 2 * band + 1] = jnp.where(is_last(), fold, after[side][plane])
    return outside


def edge_body(rows, x_lo, x_hi, c_lo, c_hi, a_lo, a_hi, b_lo, b_hi, out_ref):
    out_ref[...] = jnp.zeros_like(out_ref)
    wide = lambda refs: [ref[...].astype(F32) for ref in refs]
    x_ends, c_ends = wide((x_lo, x_hi)), wide((c_lo, c_hi))
    outside = end_rows(rows, x_ends, c_ends, wide((a_lo, a_hi)), wide((b_lo, b_hi)))
    for array, own in enumerate((x_ends, c_ends)):
        for side in range(2):
            at = 0 if side == 0 else own[side].shape[1] - 1
            for band in range(2):
                base = band * GROUP
                out_ref[array, side, base, :] = outside[array, side, 2 * band][at]
                for r in range(rows):
                    out_ref[array, side, base + 1 + r, :] = own[side][band * rows + r, at]
                out_ref[array, side, base + 1 + rows, :] = outside[array, side, 2 * band + 1][at]


def row_groups(rows, way):
    first, last = ((0, 0), (1, rows - 1)), ((0, rows - 1), (1, 0))
    if way < 0:
        first, last = last, first
    inner = tuple((b, r) for b in range(2) for r in range(1, rows - 1))
    return ((inner, (-1, 0, 1)), (first, (0, 1)), (last, (-1, 0)))


def border_index(j, rows):
    return (j // 2) * rows + (j % 2) * (rows - 1)


def border_row(j, rows):
    return (j // 2) * rows + lax.rem(j, 2) * (rows - 1)


def lift_body(
    rows, x_in, c_in, k1_in, k2_in, b1_ref, pre_out, grad_out, k1t_ref, k2t_ref, x_ref, c_ref, k1_ref,
    k2_ref, cat, held_rows, sem,
):
    width, channels = x_ref.shape[1], x_ref.shape[2]
    lifted = k1_ref.shape[2]
    used = [0]

    def slot():
        used[0] += 1
        return sem.at[used[0] - 1]

    loads = [
        pltpu.make_async_copy(source, target, slot())
        for source, target in ((x_in, x_ref), (k1_in, k1_ref), (k2_in, k2_ref), (c_in, c_ref))
    ]
    for load in loads:
        load.start()
    stores = []
    for array, (source, weights, order, out) in enumerate(
        ((x_ref, k1_ref, (-1, 0, 1), pre_out), (c_ref, k2t_ref, (1, 0, -1), grad_out))
    ):
        way = 1 - 2 * array
        loads[2 * array].wait()
        loads[2 * array + 1].wait()
        if array == 1:
            for t in range(k2_ref.shape[0]):
                k2t_ref[t] = k2_ref[t].astype(F32).T.astype(BF16)
        for i in range(2 * rows):
            cat[array, i] = spread_columns(source[i], order)
        inner, first, last = row_groups(rows, way)
        half = len(inner[0]) // 2
        groups = ((inner[0][:half], inner[1]), (inner[0][half:], inner[1]), first, last)
        for members, steps in groups:
            lhs = jnp.concatenate(
                [
                    jnp.concatenate(
                        [cat[array, b * rows + r + way * (1 - 2 * b) * dy] for dy in steps], axis=1
                    )
                    for b, r in members
                ],
                axis=0,
            )
            taps = weights[3 * (steps[0] + 1) : 3 * (steps[-1] + 2)]
            total = dot(lhs, taps.reshape(3 * len(steps) * channels, lifted))
            if array == 0:
                total = total + b1_ref[...]
            for k, (b, r) in enumerate(members):
                i = b * rows + r
                held_rows[array, i] = total[k * width : (k + 1) * width]
                store = pltpu.make_async_copy(held_rows.at[array, i], out.at[i], slot())
                store.start()
                stores.append(store)
    for t in range(k1_ref.shape[0]):
        k1t_ref[t] = k1_ref[t].astype(F32).T.astype(BF16)
    for store in stores:
        store.wait()


def row_onehot(keys, row, width):
    column = lax.broadcasted_iota(jnp.int32, (width, keys.shape[1]), 0).astype(F32)
    return jnp.where(column == keys[0:1, :] - float(row * width), 1.0, 0.0).astype(BF16)


def rim_in_body(
    rows, matching_ref, k1_in, k2t_in, pre_lo, pre_hi, grad_lo, grad_hi, x_lo, x_hi, c_lo, c_hi,
    a_lo, a_hi, b_lo, b_hi, base_ref, taps_ref, k1_ref, k2t_ref, sem,
):
    loads = [
        pltpu.make_async_copy(k1_in, k1_ref, sem.at[0]),
        pltpu.make_async_copy(k2t_in, k2t_ref, sem.at[1]),
    ]
    for load in loads:
        load.start()
    for load in loads:
        load.wait()
    face = lax.axis_index("face")
    for side in range(2):
        their_side, flipped = matching_ref[face, side, 1], matching_ref[face, side, 2]
        for row in range(3):
            taps_ref[0, side, row] = k1_ref[3 * row + 2 * side]
            turned = jnp.where(flipped == 1, 2 - row, row)
            taps_ref[1, side, row] = k2t_ref[3 * turned + 2 * their_side]
    whole = lambda refs: [ref[...] for ref in refs]
    x_ends, c_ends = whole((x_lo, x_hi)), whole((c_lo, c_hi))
    outside = end_rows(rows, x_ends, c_ends, whole((a_lo, a_hi)), whole((b_lo, b_hi)))
    channels, lifted = k1_ref.shape[1], k1_ref.shape[2]
    base_ref[...] = jnp.zeros_like(base_ref)
    for array, (strips, weights, order) in enumerate(
        (((pre_lo, pre_hi), k1_ref, (-1, 0, 1)), ((grad_lo, grad_hi), k2t_ref, (1, 0, -1)))
    ):
        for side in range(2):
            spot = 0 if side == 0 else GROUP - 1
            for b in range(2):
                for r in range(rows):
                    at = 2 * GROUP * side + GROUP * b + r + 1
                    base_ref[array, at : at + 1, :] = strips[side][
                        b * rows + r, spot : spot + 1, :
                    ]
        for pair in ((0, 3), (1, 2)):
            spots = [(side, j) for side in range(2) for j in pair]
            lhs = [spread_columns(outside[array, side, j], order) for side, j in spots]
            row = 0 if (pair[0] == 0) == (array == 0) else 6
            found = dot(
                jnp.concatenate(lhs, axis=0), weights[row : row + 3].reshape(3 * channels, lifted)
            )
            strip = found.shape[0] // len(spots)
            for k, (side, j) in enumerate(spots):
                at = 2 * GROUP * side + GROUP * (j // 2) + 1 + (rows - 1) * (j % 2)
                spot = k * strip + (0 if side == 0 else strip - 1)
                base_ref[array, at : at + 1, :] += found[spot : spot + 1]


def rim_body(rows, faces, matching_ref, taps_ref, base_ref, found_ref, *rest):
    parts = rest[:faces]
    x_side, c_side, edge_ref = rest[faces:]
    taps = taps_ref[...].reshape(2, 2, 3 * taps_ref.shape[3], taps_ref.shape[4])
    for side in range(2):
        hop, their_side, flipped = matched(matching_ref, side, faces)
        for array, out in enumerate((x_side, c_side)):
            near = partner_rows(parts, array, hop, their_side, flipped)
            way = 1 - 2 * array
            lhs = jnp.concatenate([rolled_rows(near, way * dy) for dy in (-1, 0, 1)], axis=1)
            out[side] = dot(lhs, taps[array, side])
    e = lax.broadcasted_iota(jnp.int32, (4 * GROUP, 1), 0) & (GROUP - 1)
    inside = (e >= 1) & (e <= rows)
    shape = base_ref.shape[1:]
    v = base_ref[0] + x_side[...].reshape(shape) + found_ref[...]
    inner, gp = gelu_pair(v, base_ref[1] + c_side[...].reshape(shape))
    edge_ref[0] = jnp.where(inside, inner.astype(F32), 0.0).reshape(edge_ref.shape[1:])
    edge_ref[1] = jnp.where(inside, gp.astype(F32), 0.0).reshape(edge_ref.shape[1:])


def gelu_pair(v, grad):
    square = v * v
    t = jnp.tanh(v * (ROOT + (ROOT * CUBIC) * square))
    half = 0.5 + 0.5 * t
    slope = half + (0.5 * v) * (1.0 - t * t) * (ROOT + (3.0 * ROOT * CUBIC) * square)
    return (v * half).astype(BF16), (grad * slope).astype(BF16)


def unpack_received(capacity, recv_ref, values, keys):
    devices = recv_ref.shape[0]
    slots = devices * capacity
    per_lane = 128 // capacity
    for half in range(2):
        values[:, half * 128 : (half + 1) * 128] = recv_ref[
            :, half * capacity : (half + 1) * capacity, :
        ].reshape(slots, 128)
    owner = lax.broadcasted_iota(jnp.int32, (PIXEL_ROWS, 128), 1) // capacity
    for start in range(0, devices, per_lane):
        key = jnp.zeros((PIXEL_ROWS, 128), F32)
        for k in range(per_lane):
            code = recv_ref[start + k, 2 * capacity :, :].astype(F32)
            mine = (code - 1.0) * HIGH + pltpu.roll(code, HIGH, 1)
            if k:
                mine = pltpu.roll(mine, k * capacity, 1)
            key = jnp.where(owner == k, mine, key)
        keys[:, start * capacity : start * capacity + 128] = key


def row_taps(taps_ref, row):
    return jnp.concatenate([taps_ref[3 * row + dx] for dx in range(3)], axis=1)


def merge_shifts(wide, forward):
    channels = wide.shape[1] // 3
    left, mid, right = (wide[:, k * channels : (k + 1) * channels] for k in range(3))
    step = -1 if forward else 1
    return mid + shift_columns(left, step) + shift_columns(right, -step)


def found_body(
    rows, capacity, recv_in, pre_in, grad_in, k1_in, k2t_in, values, keys, pre_b, grad_b, found_b, rim_ref,
    taps, recv_ref, sem,
):
    width = pre_b.shape[1]
    loads = [pltpu.make_async_copy(recv_in, recv_ref, sem.at[0])]
    for j in range(4):
        row = border_index(j, rows)
        loads.append(pltpu.make_async_copy(pre_in.at[row], pre_b.at[j], sem.at[1 + j]))
    for j in range(4):
        row = border_index(j, rows)
        loads.append(pltpu.make_async_copy(grad_in.at[row], grad_b.at[j], sem.at[5 + j]))
    for array, source in enumerate((k1_in, k2t_in)):
        for k in range(2):
            loads.append(
                pltpu.make_async_copy(
                    source.at[6 * k : 6 * k + 3], taps.at[array, k], sem.at[9 + 2 * array + k]
                )
            )
    for load in loads:
        load.start()
    loads[0].wait()
    unpack_received(capacity, recv_ref, values, keys)
    at = lax.broadcasted_iota(jnp.int32, (4 * GROUP, 1), 0)
    e = at & (GROUP - 1)
    b = (at // GROUP) & 1
    side = at // (2 * GROUP)
    inside = (e >= 1) & (e <= rows)
    pixel = (b * rows + e - 1) * width + side * (width - 1)
    wanted = jnp.where(inside, pixel, -1).astype(F32)
    onehot = jnp.where(keys[0:1, :] == wanted, 1.0, 0.0).astype(BF16)
    rim_ref[...] = dot(onehot, values[...])
    for half in range(2):
        members = (2 * half, 2 * half + 1)
        found = dot(
            jnp.concatenate(
                [row_onehot(keys, border_index(j, rows), width) for j in members], axis=0
            ),
            values[...],
        )
        for k, j in enumerate(members):
            found_b[j] = found[k * width : (k + 1) * width]
    for load in loads[1:]:
        load.wait()


def border_body(
    rows, pre_b, grad_b, found_b, taps, x_side, c_side, a_in, b_in, x_in, c_in, inner_ref, gp_ref, outside,
    sem,
):
    width, lifted = inner_ref.shape[1], inner_ref.shape[2]
    channels = outside.shape[3]
    even, last = is_even(), is_last()
    waits = [[], []]
    used = [0]

    def load(array, target, *sources):
        slot = sem.at[used[0]]
        used[0] += 1
        for condition, source in sources:
            copy = pltpu.make_async_copy(source, target, slot)
            pl.when(condition)(copy.start)
        waits[array].append(copy)

    for array, source in enumerate((x_in, c_in)):
        for j in range(4):
            band = j // 2
            plane = 2 * array + band
            if j % 2 == 0:
                choices = ((even, b_in.at[plane]), (jnp.logical_not(even), a_in.at[plane]))
            else:
                fold = source.at[(1 - band) * rows + rows - 1]
                middle = jnp.logical_not(even) & jnp.logical_not(last)
                choices = ((last, fold), (even, a_in.at[plane]), (middle, b_in.at[plane]))
            load(array, outside.at[array, j], *choices)

    for copy in waits[0] + waits[1]:
        copy.wait()
    for pair in ((0, 3), (1, 2)):
        totals = []
        for array, order in enumerate(((-1, 0, 1), (1, 0, -1))):
            lhs = [spread_columns(outside[array, j], order) for j in pair]
            tap = taps[array, 0 if (pair[0] == 0) == (array == 0) else 1]
            totals.append(dot(jnp.concatenate(lhs, axis=0), tap.reshape(3 * channels, lifted)))
        for k, j in enumerate(pair):
            at = GROUP * (j // 2) + 1 + (rows - 1) * (j % 2)
            piece = slice(k * width, (k + 1) * width)
            inner, gp = gelu_pair(
                add_edges(
                    totals[0][piece] + (pre_b[j] + found_b[j]),
                    x_side[0, at : at + 1, :],
                    x_side[1, at : at + 1, :],
                ),
                add_edges(
                    totals[1][piece] + grad_b[j], c_side[0, at : at + 1, :], c_side[1, at : at + 1, :]
                ),
            )
            inner_ref[j] = inner
            gp_ref[j] = gp


def send_rows(rows, inner_ref, gp_ref, k2_ref, k1t_ref, side_ref, out_ref, bottom):
    width = inner_ref.shape[1]
    for array, (source, taps) in enumerate(((inner_ref, k2_ref), (gp_ref, k1t_ref))):
        for band in range(2):
            tap = jnp.where((bottom == band) == (array == 0), 2, 0)
            wide = dot(source[2 * band + bottom], row_taps(taps, tap))
            corner = GROUP * band + (rows + 1) * bottom
            part = add_edges(
                merge_shifts(wide, array == 0),
                side_ref[array, 0, pl.ds(corner, 1), :],
                side_ref[array, 1, pl.ds(corner, 1), :],
            )
            out_ref[2 * array + band] = part.astype(BF16)


def cross_body(rows, faces, matching_ref, inner_ref, gp_ref, k2_ref, k1t_ref, *rest):
    parts = rest[:faces]
    cross_ref, side_ref = rest[faces:]
    for side in range(2):
        hop, their_side, flipped = matched(matching_ref, side, faces)
        near = partner_rows(parts, 0, hop, their_side, flipped)
        side_ref[0, side] = side_forward(near, side, k2_ref)
        near = partner_rows(parts, 1, hop, their_side, flipped)
        side_ref[1, side] = side_adjoint(near, their_side, flipped, k1t_ref)
    bottom = jnp.where(is_even(), 0, 1)
    send_rows(rows, inner_ref, gp_ref, k2_ref, k1t_ref, side_ref, cross_ref, bottom)


def pair_body(rows, _, inner_ref, gp_ref, k2_ref, k1t_ref, side_ref, pair_ref):
    bottom = jnp.where(is_even(), 1, 0)
    send_rows(rows, inner_ref, gp_ref, k2_ref, k1t_ref, side_ref, pair_ref, bottom)


def middle_body(
    rows, _, values, keys, pre_in, grad_in, x_side, c_side, inner_ref, gp_ref, base, sem
):
    middle = rows - 2
    width = base.shape[2]
    members = [(b, r) for b in range(2) for r in range(1, rows - 1)]
    loads = []
    for k in range(len(members)):
        for array, source in enumerate((pre_in, grad_in)):
            row = members[k][0] * rows + members[k][1]
            load = pltpu.make_async_copy(source.at[row], base.at[array, k], sem.at[2 * k + array])
            load.start()
            loads.append(load)
    found = dot(
        jnp.concatenate([row_onehot(keys, b * rows + r, width) for b, r in members], axis=0),
        values[...],
    )
    for k, (b, r) in enumerate(members):
        at = b * GROUP + r + 1
        loads[2 * k].wait()
        loads[2 * k + 1].wait()
        inner, gp = gelu_pair(
            add_edges(
                base[0, k] + found[k * width : (k + 1) * width],
                x_side[0, at : at + 1, :],
                x_side[1, at : at + 1, :],
            ),
            add_edges(base[1, k], c_side[0, at : at + 1, :], c_side[1, at : at + 1, :]),
        )
        inner_ref[k] = inner
        gp_ref[k] = gp


def inside_body(
    rows, inner_b, gp_b, inner_m, gp_m, side_ref, k2_ref, k1t_ref, b2_ref, x_ref, c_ref, ana_out, ana_b,
    grad_out, grad_b, ana_rows, grad_rows, sem,
):
    width, channels = x_ref.shape[1], x_ref.shape[2]
    middle = rows - 2
    stores = []
    for array, (border, inner, taps) in enumerate(
        ((inner_b, inner_m, k2_ref), (gp_b, gp_m, k1t_ref))
    ):
        way = 1 - 2 * array

        def plane(b, r):
            if r == 0 or r == rows - 1:
                return border[2 * b + r // (rows - 1)]
            return inner[middle * b + r - 1]

        for members, steps in row_groups(rows, way):
            lhs = jnp.concatenate(
                [
                    jnp.concatenate(
                        [plane(b, r + way * (1 - 2 * b) * dy) for dy in steps], axis=1
                    )
                    for b, r in members
                ],
                axis=0,
            )
            wide = dot(lhs, jnp.concatenate([row_taps(taps, dy + 1) for dy in steps], axis=0))
            for k, (b, r) in enumerate(members):
                i = b * rows + r
                at = b * GROUP + r + 1
                total = merge_shifts(wide[k * width : (k + 1) * width], array == 0)
                total = add_edges(
                    total + (x_ref, c_ref)[array][i].astype(F32),
                    side_ref[array, 0, at : at + 1, :],
                    side_ref[array, 1, at : at + 1, :],
                )
                if array == 0:
                    total = total + b2_ref[...]
                if len(steps) == 2:
                    (ana_b, grad_b)[array][2 * b + r // (rows - 1)] = total
                    continue
                held_rows, out = ((ana_rows, ana_out), (grad_rows, grad_out))[array]
                held_rows[k] = total.astype(held_rows.dtype)
                store = pltpu.make_async_copy(held_rows.at[k], out.at[i], sem.at[len(stores)])
                store.start()
                stores.append(store)
    for store in stores:
        store.wait()


def final_body(
    rows, ana_b, grad_b, own_ref, pair_ref, cross_ref, _, __, ana_out, grad_out, ana_rows, grad_rows, sem
):
    even, last = is_even(), is_last()
    stores = []
    for array, (acc, held_rows, out) in enumerate(
        ((ana_b, ana_rows, ana_out), (grad_b, grad_rows, grad_out))
    ):
        for j in range(4):
            band = j // 2
            plane = 2 * array + band
            if j % 2:
                add = jnp.where(even, pair_ref[plane], cross_ref[plane])
                add = jnp.where(last, own_ref[2 * array + 1 - band], add)
            else:
                add = jnp.where(even, cross_ref[plane], pair_ref[plane])
            held_rows[j] = (acc[j] + add.astype(F32)).astype(held_rows.dtype)
            store = pltpu.make_async_copy(
                held_rows.at[j], out.at[border_index(j, rows)], sem.at[len(stores)]
            )
            store.start()
            stores.append(store)
    for store in stores:
        store.wait()


def per_device(
    state,
    obs_values,
    obs_dest,
    obs_pixel,
    matching,
    kernel_one,
    bias_one,
    kernel_two,
    bias_two,
    cotangent,
):
    rows, width, channels = state.shape[3], state.shape[4], state.shape[5]
    lifted = kernel_one.shape[2]
    tiles, faces = lax.axis_size("tile"), lax.axis_size("face")
    devices = tiles * faces
    count = obs_values.shape[0]
    capacity = 2 * count // devices
    all_rows = 2 * rows
    middle = rows - 2
    chunk = 2 * capacity + PIXEL_ROWS
    x = state.reshape(all_rows, width, channels)
    c = cotangent.reshape(all_rows, width, channels)
    even = is_even()
    pairs = [(i, i ^ 1) for i in range(tiles)]
    crosses = [(i, i + 1 if i % 2 else i - 1) for i in range(1, tiles - 1)]
    strip = 16

    def ends(at):
        fields = [field.reshape(2, rows, width, channels) for field in (x, c)]
        picked = [
            jnp.concatenate(
                [
                    lax.dynamic_slice(field, (0, at, start, 0), (2, 1, strip, channels))[:, 0]
                    for start in (0, width - strip)
                ],
                axis=1,
            )
            for field in fields
        ]
        return jnp.concatenate(picked, axis=0)

    pair_ends = lax.ppermute(ends(jnp.where(even, rows - 1, 0)), "tile", pairs)
    cross_ends = lax.ppermute(ends(jnp.where(even, 0, rows - 1)), "tile", crosses)
    low_row = lambda field, at: lax.dynamic_index_in_dim(
        field.reshape(2, rows, width, channels), at, 1, keepdims=False
    )
    border_rows = lambda at: jnp.concatenate([low_row(x, at), low_row(c, at)], axis=0)
    pair_out = border_rows(jnp.where(even, rows - 1, 0))
    cross_out = border_rows(jnp.where(even, 0, rows - 1))
    smem = pl.BlockSpec(memory_space=pltpu.SMEM)
    vmem = pl.BlockSpec(memory_space=pltpu.VMEM)
    hbm = pl.BlockSpec(memory_space=pl.ANY)

    def exchange(own):
        parts = [own]
        for k in range(1, faces):
            parts.append(
                lax.ppermute(own, "face", [((i + k) % faces, i) for i in range(faces)])
            )
        return parts

    packed = pl.pallas_call(
        functools.partial(pack_body, capacity),
        in_specs=[hbm] * 3,
        out_specs=hbm,
        out_shape=pltpu.HBM((devices, chunk, 128), BF16),
        scratch_shapes=[
            pltpu.VMEM((1, count), jnp.int32),
            pltpu.VMEM((1, count), jnp.int32),
            pltpu.VMEM((count, lifted), BF16),
            pltpu.VMEM((devices, chunk, 128), BF16),
            pltpu.SemaphoreType.DMA((3,)),
            pltpu.SemaphoreType.DMA((devices * capacity // 512,)),
        ],
        compiler_params=params(16),
        cost_estimate=cost(2 * devices * capacity * count * lifted, 2 << 20),
        name="pack",
    )(far(obs_dest.reshape(1, count)), far(obs_pixel.reshape(1, count)), far(obs_values))
    received = lax.all_to_all(packed, ("tile", "face"), 0, 0, tiled=True)

    b1 = bias_one.reshape(1, lifted)
    b2 = bias_two.reshape(1, channels)
    row_block = lambda n: pl.BlockSpec((1, width, n), lambda i: (i, 0, 0))
    edge_block = lambda n: pl.BlockSpec((1, width, n), lambda i: (border_row(i, rows), 0, 0))
    conv_flops = 2 * 9 * all_rows * width * channels * lifted
    plane = (4, width, channels)
    pre, grad_inner, k1t, k2t = pl.pallas_call(
        functools.partial(lift_body, rows),
        in_specs=[hbm] * 4 + [vmem],
        out_specs=[hbm] * 2 + [vmem] * 2,
        out_shape=[pltpu.HBM((all_rows, width, lifted), F32)] * 2
        + [pltpu.HBM(kernel_two.shape, BF16), pltpu.HBM(kernel_one.shape, BF16)],
        scratch_shapes=[
            pltpu.VMEM(x.shape, BF16),
            pltpu.VMEM(c.shape, BF16),
            pltpu.VMEM(kernel_one.shape, BF16),
            pltpu.VMEM(kernel_two.shape, BF16),
            pltpu.VMEM((2, all_rows, width, 3 * channels), BF16),
            pltpu.VMEM((2, all_rows, width, lifted), F32),
            pltpu.SemaphoreType.DMA((4 + 2 * all_rows,)),
        ],
        compiler_params=params(40),
        cost_estimate=cost(conv_flops, 8 << 20),
        name="lift",
    )(far(x), far(c), far(kernel_one), far(kernel_two), b1)
    pre, grad_inner = far(pre), far(grad_inner)
    pair_ends, cross_ends, k1t = lax.optimization_barrier((pair_ends, cross_ends, k1t))
    low = lambda n: pl.BlockSpec((n, strip, channels), lambda *_: (0, 0, 0))
    high = lambda n, at: pl.BlockSpec((n, strip, channels), lambda *_: (0, at, 0))
    tail = width // strip - 1
    edge_shape = (2, 2, 2 * GROUP, channels)
    edges = pl.pallas_call(
        functools.partial(edge_body, rows),
        grid=(1,),
        in_specs=[low(all_rows), high(all_rows, tail)] * 2 + [low(4), high(4, 1)] * 2,
        out_specs=fixed(edge_shape),
        out_shape=jax.ShapeDtypeStruct(edge_shape, F32),
        compiler_params=params(8),
        cost_estimate=cost(0, 1 << 18),
        name="edges",
    )(x, x, c, c, pair_ends, pair_ends, cross_ends, cross_ends)
    parts = exchange(edges)

    side_in = (2, 2 * GROUP, lifted)
    end = width // GROUP - 1
    edge_strip = lambda at: pl.BlockSpec((all_rows, GROUP, lifted), lambda *_: (0, at, 0))
    rim_shape = (2, 4 * GROUP, lifted)
    taps_shape = (2, 2, 3, channels, lifted)
    rim_base, side_taps = pl.pallas_call(
        functools.partial(rim_in_body, rows),
        grid=(1,),
        in_specs=[smem, hbm, hbm]
        + [edge_strip(0), edge_strip(end)] * 2
        + [low(all_rows), high(all_rows, tail)] * 2
        + [low(4), high(4, 1)] * 2,
        out_specs=[fixed(rim_shape), fixed(taps_shape)],
        out_shape=[jax.ShapeDtypeStruct(rim_shape, F32), jax.ShapeDtypeStruct(taps_shape, BF16)],
        scratch_shapes=[
            pltpu.VMEM(kernel_one.shape, BF16),
            pltpu.VMEM(k2t.shape, BF16),
            pltpu.SemaphoreType.DMA((2,)),
        ],
        compiler_params=params(8),
        cost_estimate=cost(0, 2 << 20),
        name="rim_in",
    )(
        matching, far(kernel_one), far(k2t), pre, pre, grad_inner, grad_inner, x, x, c, c, pair_ends,
        pair_ends, cross_ends, cross_ends,
    )
    pair_out, cross_out, side_taps = lax.optimization_barrier((pair_out, cross_out, side_taps))
    pair_rows = lax.ppermute(pair_out, "tile", pairs)
    cross_rows = lax.ppermute(cross_out, "tile", crosses)
    side_two = (2, 2, 2 * GROUP, lifted)
    slots = devices * capacity
    onehot_flops = 2 * width * slots * lifted
    other_block = pl.BlockSpec(
        (1, width, channels), lambda j: ((1 - j // 2) * rows + rows - 1, 0, 0)
    )
    values, keys, pre_b, grad_b, found_b, rim_found, rim_taps = pl.pallas_call(
        functools.partial(found_body, rows, capacity),
        in_specs=[hbm] * 5,
        out_specs=[vmem] * 7,
        out_shape=[
            hold((slots, lifted), BF16),
            hold((PIXEL_ROWS, slots), F32),
            hold((4, width, lifted), F32),
            hold((4, width, lifted), F32),
            hold((4, width, lifted), F32),
            hold(rim_shape[1:], F32),
            hold((2, 2, 3, channels, lifted), BF16),
        ],
        scratch_shapes=[
            pltpu.VMEM(received.shape, BF16),
            pltpu.SemaphoreType.DMA((13,)),
        ],
        compiler_params=params(),
        cost_estimate=cost(4 * onehot_flops, 6 << 20),
        name="found",
    )(far(received), pre, grad_inner, far(kernel_one), far(k2t))
    values, keys, pre_b, grad_b = held(values), held(keys), held(pre_b), held(grad_b)
    found_b = held(found_b)
    x_side, c_side, edges_two = pl.pallas_call(
        functools.partial(rim_body, rows, faces),
        in_specs=[smem] + [vmem] * (3 + faces),
        out_specs=[vmem] * 3,
        out_shape=[
            hold(side_in, F32),
            hold(side_in, F32),
            jax.ShapeDtypeStruct(side_two, F32),
        ],
        compiler_params=params(8),
        cost_estimate=cost(0, 1 << 20),
        name="rim",
    )(matching, side_taps, rim_base, held(rim_found), *parts)
    x_side, c_side = held(x_side), held(c_side)
    parts_two = exchange(edges_two)

    border_shape = hold((4, width, lifted), BF16)
    inner_b, gp_b = pl.pallas_call(
        functools.partial(border_body, rows),
        in_specs=[vmem] * 6 + [hbm] * 4,
        out_specs=[vmem] * 2,
        out_shape=[border_shape] * 2,
        scratch_shapes=[
            pltpu.VMEM((2, 4, width, channels), BF16),
            pltpu.SemaphoreType.DMA((8,)),
        ],
        compiler_params=params(),
        cost_estimate=cost(conv_flops // 6, 4 << 20),
        name="border",
    )(
        pre_b, grad_b, found_b, held(rim_taps), x_side, c_side, far(pair_rows), far(cross_rows), far(x),
        far(c),
    )
    inner_b, gp_b = held(inner_b), held(gp_b)

    side_out = (2, 2, 2 * GROUP, channels)
    to_cross, sides = pl.pallas_call(
        functools.partial(cross_body, rows, faces),
        in_specs=[smem] + [vmem] * (4 + faces),
        out_specs=[vmem] * 2,
        out_shape=[jax.ShapeDtypeStruct(plane, BF16), jax.ShapeDtypeStruct(side_out, F32)],
        compiler_params=params(16),
        cost_estimate=cost(conv_flops // 12, 3 << 20),
        name="send_cross",
    )(matching, inner_b, gp_b, kernel_two, k1t, *parts_two)
    from_cross = lax.ppermute(to_cross, "tile", crosses)
    to_pair = pl.pallas_call(
        functools.partial(pair_body, rows),
        in_specs=[hbm] + [vmem] * 5,
        out_specs=vmem,
        out_shape=jax.ShapeDtypeStruct(plane, BF16),
        compiler_params=params(16),
        cost_estimate=cost(conv_flops // 12, 3 << 20),
        name="send_pair",
    )(to_cross, inner_b, gp_b, kernel_two, k1t, sides)
    from_pair = lax.ppermute(to_pair, "tile", pairs)

    inner_m, gp_m = pl.pallas_call(
        functools.partial(middle_body, rows),
        in_specs=[hbm, vmem, vmem, hbm, hbm, vmem, vmem],
        out_specs=[vmem] * 2,
        out_shape=[hold((2 * middle, width, lifted), BF16)] * 2,
        scratch_shapes=[
            pltpu.VMEM((2, 2 * middle, width, lifted), F32),
            pltpu.SemaphoreType.DMA((4 * middle,)),
        ],
        compiler_params=params(32),
        cost_estimate=cost(2 * middle * onehot_flops, 10 << 20),
        name="middle",
    )(to_pair, values, keys, pre, grad_inner, x_side, c_side)
    inner_m, gp_m = held(inner_m), held(gp_m)

    analysis, ana_b, grad_state, grad_b = pl.pallas_call(
        functools.partial(inside_body, rows),
        in_specs=[vmem] * 10,
        out_specs=[hbm, vmem, hbm, vmem],
        out_shape=[
            pltpu.HBM((all_rows, width, channels), BF16),
            hold(plane, F32),
            pltpu.HBM((all_rows, width, channels), F32),
            hold(plane, F32),
        ],
        scratch_shapes=[
            pltpu.VMEM((2 * middle, width, channels), BF16),
            pltpu.VMEM((2 * middle, width, channels), F32),
            pltpu.SemaphoreType.DMA((4 * middle,)),
        ],
        compiler_params=params(),
        cost_estimate=cost(2 * conv_flops, 14 << 20),
        name="inside",
    )(inner_b, gp_b, inner_m, gp_m, sides, kernel_two, k1t, b2, x, c)
    ana_b, grad_b = held(ana_b), held(grad_b)

    analysis, grad_state = pl.pallas_call(
        functools.partial(final_body, rows),
        in_specs=[vmem] * 5 + [hbm] * 2,
        out_specs=[hbm] * 2,
        out_shape=[
            pltpu.HBM((all_rows, width, channels), BF16),
            pltpu.HBM((all_rows, width, channels), F32),
        ],
        scratch_shapes=[
            pltpu.VMEM(plane, BF16),
            pltpu.VMEM(plane, F32),
            pltpu.SemaphoreType.DMA((8,)),
        ],
        input_output_aliases={5: 0, 6: 1},
        compiler_params=params(16),
        cost_estimate=cost(0, 6 << 20),
        name="final",
    )(ana_b, grad_b, to_cross, from_pair, from_cross, far(analysis), far(grad_state))
    return analysis.reshape(state.shape), grad_state.reshape(cotangent.shape)


def solution(mesh):
    return jax.shard_map(
        per_device,
        mesh=mesh,
        in_specs=(
            P("face", "tile", None, None, None, None),
            P(("face", "tile"), None),
            P(("face", "tile"), None),
            P(("face", "tile")),
            P(),
            P(),
            P(),
            P(),
            P(),
            P("face", "tile", None, None, None, None),
        ),
        out_specs=(
            P("face", "tile", None, None, None, None),
            P("face", "tile", None, None, None, None),
        ),
        check_vma=False,
    )
```
